32 devices in a mesh: dp: 4 (over y, x), row: 2 (over core), col: 4 (over z).
Axes of the slice: x: 2, y: 2, z: 4, core: 2. Of those that a mesh axis runs over, the one named last changes fastest.
Arguments:
- tokens: bfloat16 [16384, 2048], P(('dp', 'col'), 'row'), may hold values from -76 to 76
- gain_attn: float32 [2048], P('row'), may hold values from 0.25 to 1.75
- gain_ffn: float32 [2048], P('row'), may hold values from 0.25 to 1.75
- w_query: bfloat16 [2048, 2048], P('row', 'col'), may hold values from -0.125 to 0.125
- w_key: bfloat16 [2048, 2048], P('row', 'col'), may hold values from -0.125 to 0.125
- w_value: bfloat16 [2048, 2048], P('row', 'col'), may hold values from -0.125 to 0.125
- w_out: bfloat16 [2048, 2048], P('col', 'row'), may hold values from -0.5 to 0.5
- w_gate: bfloat16 [2048, 8192], P('row', 'col'), may hold values from -0.125 to 0.125
- w_up: bfloat16 [2048, 8192], P('row', 'col'), may hold values from -0.125 to 0.125
- w_down: bfloat16 [8192, 2048], P('col', 'row'), may hold values from -0.0625 to 0.0625
- cotangent: bfloat16 [16384, 2048], P(('dp', 'col'), 'row'), may hold values from -76 to 76
Outputs:
- mixed: bfloat16 [16384, 2048], P(('dp', 'col'), 'row')
- input_grad: float32 [16384, 2048], P(('dp', 'col'), 'row')
- gain_attn_grad: float32 [2048], P('row')
- gain_ffn_grad: float32 [2048], P('row')
- w_query_grad: float32 [2048, 2048], P('row', 'col')
- w_key_grad: float32 [2048, 2048], P('row', 'col')
- w_value_grad: float32 [2048, 2048], P('row', 'col')
- w_out_grad: float32 [2048, 2048], P('col', 'row')
- w_gate_grad: float32 [2048, 8192], P('row', 'col')
- w_up_grad: float32 [2048, 8192], P('row', 'col')
- w_down_grad: float32 [8192, 2048], P('col', 'row')
The draws below stay inside these ranges and needn't reach their ends.
All inputs are finite; a program needn't handle non-finite values.
Results may differ from the reference program's by a relative error of at most 0.012.
Values may be sent and summed in bfloat16 or wider, within the bound.
No kernel may reach another device: no remote copies, remote signals or barrier semaphores. Data moves between devices by JAX's collectives and lax.ppermute only.
A program may use at most 384 MiB of HBM per device.

```python
import jax
import jax.numpy as jnp
from jax import lax

D = 2048
FF = 8192
HEADS = 32
HEAD_DIM = 64
SEQ_LEN = 1024
GROUP = 4096
TOKENS = 16384
N_DP = 4


def scaled_field(key, rows_total, width):
    row_key, col_key = jax.random.split(key, 2)
    ramp = 1.0 + 2.0 * jnp.arange(rows_total, dtype=jnp.float32)[:, None] / rows_total
    row_scale = jnp.exp(jax.random.uniform(row_key, (rows_total, 1), jnp.float32, -0.693, 0.693))
    col_rise = 0.6 + 1.2 * jnp.arange(width, dtype=jnp.float32)[None, :] / width
    col_scale = jnp.exp(jax.random.uniform(col_key, (1, width), jnp.float32, -0.693, 0.693)) * col_rise
    return ramp * row_scale * col_scale


def draw_tokens(key, part):
    key = jax.random.fold_in(key, 11)
    scales = scaled_field(key, TOKENS, D)
    base_key = jax.random.fold_in(key, 5)
    base = jnp.clip(jax.random.normal(base_key, (TOKENS, D), jnp.float32), -3.5, 3.5)
    return (base * scales).astype(jnp.bfloat16)


def draw_cotangent(key, part):
    key = jax.random.fold_in(key, 23)
    scales = scaled_field(key, TOKENS, D)
    base_key = jax.random.fold_in(key, 7)
    base = jnp.clip(jax.random.normal(base_key, (TOKENS, D), jnp.float32), -3.5, 3.5)
    return (base * scales).astype(jnp.bfloat16)


def level_of(key, shape, cuts, smallest, largest):
    def one(position, parts):
        steps = jax.random.uniform(jax.random.fold_in(jax.random.fold_in(key, 6), position), (parts,), jnp.float32, smallest / len(cuts), largest / len(cuts))
        return jnp.repeat(jnp.exp(steps), shape[position] // parts).reshape((-1,) + (1,) * (len(shape) - position - 1))

    factor_of = one(*cuts[0])
    for cut in cuts[1:]:
        factor_of = factor_of * one(*cut)
    return factor_of


def centred(stream_key, shape, spread, reach, pieces=(), held_as=jnp.bfloat16):
    loudness = level_of(stream_key, shape, pieces, -0.22, 0.18) if pieces else 1.0
    drawn = jax.random.normal(stream_key, shape, jnp.float32) * spread * loudness
    return jnp.minimum(jnp.maximum(drawn, -reach), reach).astype(held_as)


def setup_inputs(seed: int = 0) -> dict:
    arg_keys = jax.random.split(jax.random.key(seed), 12)
    return {
        "tokens": draw_tokens(jax.random.fold_in(arg_keys[11], 71), 0),
        "gain_attn": jnp.clip(1.0 + 0.15 * jax.random.normal(arg_keys[1], (D,), jnp.float32), 0.25, 1.75),
        "gain_ffn": jnp.clip(1.0 + 0.15 * jax.random.normal(arg_keys[2], (D,), jnp.float32), 0.25, 1.75),
        "w_query": centred(arg_keys[3], (D, D), D ** -0.5, 0.125, ((0, 2), (1, 4))),
        "w_key": centred(arg_keys[4], (D, D), D ** -0.5, 0.125, ((0, 2), (1, 4))),
        "w_value": centred(arg_keys[5], (D, D), D ** -0.5, 0.125, ((0, 2), (1, 4))),
        "w_out": centred(arg_keys[6], (D, D), (D // 16) ** -0.5, 0.5, ((0, 4), (1, 2))),
        "w_gate": centred(arg_keys[7], (D, FF), D ** -0.5, 0.125, ((0, 2), (1, 4))),
        "w_up": centred(arg_keys[8], (D, FF), D ** -0.5, 0.125, ((0, 2), (1, 4))),
        "w_down": centred(arg_keys[9], (FF, D), FF ** -0.5, 0.0625, ((0, 4), (1, 2))),
        "cotangent": draw_cotangent(jax.random.fold_in(arg_keys[11], 71), 0),
    }


@jax.custom_vjp
def low(v):
    return lax.optimization_barrier(v.astype(jnp.bfloat16)).astype(jnp.float32)

@jax.custom_vjp
def low_back(v):
    return v

def low_keep(v):
    return (low(v), None)

def low_pass(kept, grad):
    return (grad,)

def back_keep(v):
    return (v, None)

def back_low(kept, grad):
    return (low(grad),)
low.defvjp(low_keep, low_pass)
low_back.defvjp(back_keep, back_low)
eps_norm = 1e-05
rope_base = 130000.0

def matmul(left_side, weight):
    return jnp.dot(left_side, weight, precision=lax.Precision.HIGHEST, preferred_element_type=jnp.float32)

def rms_scale(stream, gain):
    return stream * lax.rsqrt(lax.optimization_barrier(jnp.mean(stream * stream, axis=-1, keepdims=True)) + eps_norm) * gain

def rotary(values):
    half_dim = HEAD_DIM // 2
    frequency = jnp.exp(-jnp.log(rope_base) * jnp.arange(half_dim, dtype=jnp.float32) * (2.0 / HEAD_DIM))
    angles = jnp.arange(SEQ_LEN, dtype=jnp.float32)[:, None] * frequency[None, :]
    cosine = jnp.cos(angles)[:, None, :]
    sine_table = jnp.sin(angles)[:, None, :]
    first_half = values[..., :half_dim]
    second = values[..., half_dim:]
    return jnp.concatenate((first_half * cosine - second * sine_table, second * cosine + first_half * sine_table), axis=-1)

def attend(sequence):
    queries, key_rows, values = sequence
    scores = jnp.einsum('qhd,khd->hqk', queries, key_rows, precision=lax.Precision.HIGHEST) * HEAD_DIM ** (-0.5)
    scores = low_back(scores)
    places = jnp.arange(SEQ_LEN)
    causal = places[:, None] >= places[None, :]
    scores = jnp.where(causal[None], scores, -1e+30)
    weights = low(jax.nn.softmax(scores, axis=-1))
    return jnp.einsum('hqk,khd->qhd', weights, values, precision=lax.Precision.HIGHEST)

def layer(stream, gain_attn, gain_ffn, w_query, w_key, w_value, w_out, w_gate, w_up, w_down):
    seq_count = stream.shape[0] // SEQ_LEN
    normed = low(rms_scale(stream, gain_attn))
    queries = low_back(matmul(normed, w_query)).reshape(seq_count, SEQ_LEN, HEADS, HEAD_DIM)
    key_rows = low_back(matmul(normed, w_key)).reshape(seq_count, SEQ_LEN, HEADS, HEAD_DIM)
    values = low(low_back(matmul(normed, w_value))).reshape(seq_count, SEQ_LEN, HEADS, HEAD_DIM)
    queries = low(rotary(queries))
    key_rows = low(rotary(key_rows))
    attended = lax.map(jax.checkpoint(attend), (queries, key_rows, values))
    attended = low(low_back(attended.reshape(seq_count * SEQ_LEN, D)))
    residual = stream + low_back(matmul(attended, w_out))
    normed_ffn = low(rms_scale(residual, gain_ffn))
    gate_rows = low_back(matmul(normed_ffn, w_gate))
    up_rows = low_back(matmul(normed_ffn, w_up))
    hidden = low(jax.nn.silu(gate_rows) * up_rows)
    return residual + low_back(matmul(hidden, w_down))

def reference(tokens, gain_attn, gain_ffn, w_query, w_key, w_value, w_out, w_gate, w_up, w_down, cotangent):
    weights = (gain_attn.astype(jnp.float32), gain_ffn.astype(jnp.float32), w_query.astype(jnp.float32), w_key.astype(jnp.float32), w_value.astype(jnp.float32), w_out.astype(jnp.float32), w_gate.astype(jnp.float32), w_up.astype(jnp.float32), w_down.astype(jnp.float32))
    streams = tokens.astype(jnp.float32).reshape(N_DP, GROUP, D)
    upstream = cotangent.astype(jnp.float32).reshape(N_DP, GROUP, D)

    def group_step(summed, inputs):
        stream, grad_out = inputs
        result, pullback = jax.vjp(layer, stream, *weights)
        gradients = pullback(grad_out)
        summed = tuple((accum + extra for accum, extra in zip(summed, gradients[1:])))
        return (summed, (result.astype(jnp.bfloat16), gradients[0]))
    initial = tuple((jnp.zeros_like(weight) for weight in weights))
    summed, (results, input_grads) = lax.scan(group_step, initial, (streams, upstream))
    return (results.reshape(TOKENS, D), input_grads.reshape(TOKENS, D), summed[0], summed[1], summed[2], summed[3], summed[4], summed[5], summed[6], summed[7], summed[8])
```

```python
import jax
import jax.numpy as jnp
from jax import lax
from jax.experimental import pallas as pl
from jax.experimental.pallas import tpu as pltpu
from jax.sharding import PartitionSpec as P

D = 2048
HEAD_DIM = 64
SEQ_LEN = 1024
LANES = 128
EPS = 1e-05
ROPE_BASE = 130000.0
VMEM = 60 * 1024 * 1024
UNIT_TILE = 512
QB = 256
COST = 10**12
F32 = jnp.float32
BF16 = jnp.bfloat16


def dot(a, b, ca, cb):
    return lax.dot_general(a, b, (((ca,), (cb,)), ((), ())), preferred_element_type=F32)


def of(shape, dtype=BF16):
    return jax.ShapeDtypeStruct(tuple(shape), dtype)


class Line:
    waiting = []

    def __init__(self):
        self.last, self.marks = [], []

    def run(self, call, *values):
        Line.waiting = list(self.last)
        result = call(*values)
        self.last = jax.tree.leaves(result)[:1] + self.marks
        self.marks = []
        return result

    def tied(self, value):
        if not self.last:
            return value
        value, *self.last = lax.optimization_barrier((value, *self.last))
        return value

    def mix(self, call, first, *values):
        first = self.tied(first)
        result = call(first, *values)
        self.last = jax.tree.leaves(result)[:1] + list(self.last)
        return result

    def send(self, move, value):
        return move(self.tied(value))

    def ship(self, move, value):
        return move(value)

    def post(self, move, value):
        sent = move(value)
        mark = other_core(self.tied(self.stamp))
        self.run(short_kernel, self.stamp)
        self.last = self.last + [mark]
        return sent

    def swap(self, value):
        value = lax.all_to_all(self.tied(value), "row", split_axis=0, concat_axis=0, tiled=True)
        self.last = [value, *self.last]
        return value


def launch(kernel, arrays, in_specs, name, prefetch=(), **rest):
    held, Line.waiting = Line.waiting, []
    skip, count = len(held), len(prefetch) + len(arrays)

    def body(*refs):
        kernel(*refs[:count], *refs[count + skip :])

    in_specs = list(in_specs) + [pl.BlockSpec(memory_space=pl.ANY)] * skip
    out_shape = rest.pop("out_shape")
    if prefetch:
        layout = dict(
            grid_spec=pltpu.PrefetchScalarGridSpec(num_scalar_prefetch=len(prefetch), in_specs=in_specs, **rest)
        )
    else:
        layout = dict(in_specs=in_specs, **rest)
    return pl.pallas_call(
        body,
        out_shape=out_shape,
        compiler_params=pltpu.CompilerParams(vmem_limit_bytes=VMEM),
        cost_estimate=pl.CostEstimate(flops=COST, bytes_accessed=1, transcendentals=0),
        name=name,
        **layout,
    )(*prefetch, *arrays, *held)


def short_kernel(values):
    def kernel(in_ref, out_ref):
        out_ref[...] = in_ref[...]

    spec = pl.BlockSpec(values.shape, lambda: (0, 0))
    return launch(kernel, [values], [spec], "short", grid=(), out_specs=spec, out_shape=of(values.shape, values.dtype))


def extent(shape, index):
    sizes = []
    for size, at in zip(shape, index):
        if not isinstance(at, int):
            sizes.append(size if isinstance(at, slice) else at.size)
    return tuple(sizes)


def place(sources, outs, phases, where, name, kept=0):
    moves = [m for phase in phases for m in phase]
    shapes = [extent((sources[src] if src >= 0 else outs[-1 - src]).shape, src_at([0] * 8)) for src, src_at, _, _ in moves]
    count = len(sources)

    def kernel(where_ref, *refs):
        ins, out_refs, held = refs[:count], refs[count : count + len(outs)], refs[count + len(outs) : -2]
        in_sems, out_sems = refs[-2:]
        base = 0
        for phase in phases:
            loads, stores = [], []
            for n, (src, src_at, dst, dst_at) in enumerate(phase, base):
                src_ref = out_refs[-1 - src] if src < 0 else ins[src]
                loads.append(pltpu.make_async_copy(src_ref.at[src_at(where_ref)], held[n], in_sems.at[n]))
                stores.append(pltpu.make_async_copy(held[n], out_refs[dst].at[dst_at(where_ref)], out_sems.at[n]))
            for load in loads:
                load.start()
            for load, store in zip(loads, stores):
                load.wait()
                store.start()
            for store in stores:
                store.wait()
            base += len(phase)

    return launch(
        kernel,
        [where, *sources],
        [pl.BlockSpec(memory_space=pltpu.SMEM)] + [pl.BlockSpec(memory_space=pl.ANY)] * count,
        name,
        out_specs=[pl.BlockSpec(memory_space=pl.ANY)] * len(outs),
        out_shape=list(outs),
        scratch_shapes=[pltpu.VMEM(s, outs[m[2]].dtype) for s, m in zip(shapes, moves)] + [pltpu.SemaphoreType.DMA((len(moves),))] * 2,
        input_output_aliases={1 + count - kept + i: i for i in range(kept)},
    )


CORE, OTHER, QUARTER = 0, 1, 2


def full(_):
    return (slice(None), slice(None))


def rows_at(scalar, size, base=0):
    return lambda w: (pl.ds(pl.multiple_of(base + w[scalar] * size, size), size), slice(None))


def cols_at(scalar, size, lo=0, width=None):
    width = width or size
    return lambda w: (slice(None), pl.ds(pl.multiple_of(w[scalar] * size + lo, width), width))


def rows_span(scalar, size, lo, count):
    return lambda w: (pl.ds(pl.multiple_of(w[scalar] * size + lo, count), count), slice(None))


def rows_fixed(lo, count):
    return lambda w: (pl.ds(lo, count), slice(None))


def block_at(row_scalar, height, lo, width):
    return lambda w: (pl.ds(pl.multiple_of(w[row_scalar] * height, height), height), pl.ds(lo, width))


def rope_tables():
    half = HEAD_DIM // 2
    frequency = jnp.exp(-jnp.log(ROPE_BASE) * jnp.arange(half, dtype=F32) * (2.0 / HEAD_DIM))
    frequency = jnp.tile(frequency, 4)
    sign = jnp.where(jnp.arange(LANES) % HEAD_DIM < half, -1.0, 1.0)
    angles = jnp.arange(SEQ_LEN, dtype=F32)[:, None] * frequency[None, :]
    return jnp.cos(angles), jnp.sin(angles) * sign[None, :]


def swap_halves(values):
    half = HEAD_DIM // 2
    lane = lax.broadcasted_iota(jnp.int32, values.shape, 1)
    return jnp.where(lane % HEAD_DIM < half, pltpu.roll(values, LANES - half, 1), pltpu.roll(values, half, 1))


def qkv_kernel(first, x_ref, gain_ref, cos_ref, sin_ref, w_ref, *refs):
    q_ref, k_ref, v_ref = refs[-3:]
    if first:
        x = x_ref[...].astype(F32)
        scale = lax.rsqrt(jnp.sum(x * x, axis=1, keepdims=True) / D + EPS)
        refs[0][...] = (x * scale * gain_ref[...]).astype(BF16)
        normed = refs[0][...]
    else:
        normed = x_ref[...]
    cos, sin = cos_ref[...], sin_ref[...]
    width = q_ref.shape[1]
    projected = dot(normed, w_ref[...], 1, 0)
    for part, (out_ref, mult) in enumerate(((q_ref, HEAD_DIM**-0.5), (k_ref, 1.0))):
        for lo in range(0, width, LANES):
            piece = projected[:, part * width + lo : part * width + lo + LANES]
            out_ref[:, lo : lo + LANES] = ((piece * cos + swap_halves(piece) * sin).astype(BF16) * mult).astype(BF16)
    v_ref[...] = projected[:, 2 * width :].astype(BF16)


def project_qkv(x, gain, cos, sin, weight, first):
    rows, width = x.shape[0], weight.shape[1] // 3
    tile = min(512, rows)
    row_block = lambda n: pl.BlockSpec((tile, n), lambda i: (i, 0))
    whole = lambda a: pl.BlockSpec(a.shape, lambda i: (0, 0))
    outs = [D] * first + [width] * 3
    return launch(
        lambda *refs: qkv_kernel(first, *refs),
        [x, gain, cos, sin, weight],
        [row_block(D), whole(gain), row_block(LANES), row_block(LANES), whole(weight)],
        "qkv",
        grid=(rows // tile,),
        out_specs=[row_block(n) for n in outs],
        out_shape=[of((rows, n)) for n in outs],
    )


def head_of(values, head):
    lane = lax.broadcasted_iota(jnp.int32, values.shape, 1)
    return jnp.where((lane >= HEAD_DIM) == (head == 1), values, jnp.zeros_like(values))


def causal_scores(keys, queries, start):
    scores = dot(keys, queries, 1, 1)
    last = scores[start:]
    key_at = lax.broadcasted_iota(jnp.int32, last.shape, 0)
    query_at = lax.broadcasted_iota(jnp.int32, last.shape, 1)
    last = jnp.where(key_at <= query_at, last, -1e30)
    return last if start == 0 else jnp.concatenate((scores[:start], last), axis=0)


def attend_kernel(q_ref, k_ref, v_ref, o_ref, lse_ref):
    v_t = v_ref[...].T
    for start in range(0, SEQ_LEN, QB):
        stop = start + QB
        queries = q_ref[start:stop, :]
        outs = []
        for head in range(2):
            scores = causal_scores(k_ref[:stop, :], head_of(queries, head), start)
            top = jnp.max(scores, axis=0, keepdims=True)
            weights = jnp.exp(scores - top)
            total = jnp.sum(weights, axis=0, keepdims=True)
            lse_ref[0, 0, head : head + 1, start:stop] = top + jnp.log(total)
            out = dot(v_t[head * HEAD_DIM : (head + 1) * HEAD_DIM, :stop], weights.astype(BF16), 1, 0)
            outs.append(out / total)
        o_ref[start:stop, :] = jnp.concatenate(outs, axis=0).T.astype(BF16)


def attend(q, k, v):
    rows, width = q.shape
    seqs, pairs = rows // SEQ_LEN, width // LANES
    block = pl.BlockSpec((SEQ_LEN, LANES), lambda s, h: (s, h))
    return launch(
        attend_kernel,
        [q, k, v],
        [block] * 3,
        "attend",
        grid=(seqs, pairs),
        out_specs=[block, pl.BlockSpec((1, 1, 8, SEQ_LEN), lambda s, h: (s, h, 0, 0))],
        out_shape=[of((rows, width)), of((seqs, pairs, 8, SEQ_LEN), F32)],
    )


def attend_back_kernel(do_ref, q_ref, k_ref, v_ref, o_ref, lse_ref, cos_ref, sin_ref, dq_ref, dk_ref, dv_ref, dk_acc, dv_acc):
    k_t = k_ref[...].T
    dk_acc[...] = jnp.zeros_like(dk_acc)
    dv_acc[...] = jnp.zeros_like(dv_acc)
    for start in range(0, SEQ_LEN, QB):
        stop = start + QB
        queries, grads = q_ref[start:stop, :], do_ref[start:stop, :]
        inner = (grads.astype(F32) * o_ref[start:stop, :].astype(F32)).T
        back = []
        for head in range(2):
            one_q, one_g = head_of(queries, head), head_of(grads, head)
            scores = causal_scores(k_ref[:stop, :], one_q, start)
            weights = jnp.exp(scores - lse_ref[0, 0, head : head + 1, start:stop])
            grad_weights = dot(v_ref[:stop, :], one_g, 1, 1)
            delta = jnp.sum(inner[head * HEAD_DIM : (head + 1) * HEAD_DIM], axis=0, keepdims=True)
            grad_scores = (weights * (grad_weights - delta)).astype(BF16)
            dv_acc[:stop, :] += dot(weights.astype(BF16), one_g, 1, 0)
            dk_acc[:stop, :] += dot(grad_scores, one_q, 1, 0)
            back.append(dot(k_t[head * HEAD_DIM : (head + 1) * HEAD_DIM, :stop], grad_scores, 1, 0))
        dq = jnp.concatenate(back, axis=0).T * HEAD_DIM**-0.5
        cos, sin = cos_ref[start:stop, :], sin_ref[start:stop, :]
        dq_ref[start:stop, :] = (dq * cos - swap_halves(dq) * sin).astype(BF16)
    dk = dk_acc[...]
    dk_ref[...] = (dk * cos_ref[...] - swap_halves(dk) * sin_ref[...]).astype(BF16)
    dv_ref[...] = dv_acc[...].astype(BF16)


def attend_back(do, q, k, v, o, lse, cos, sin):
    rows, width = q.shape
    seqs, pairs = rows // SEQ_LEN, width // LANES
    block = pl.BlockSpec((SEQ_LEN, LANES), lambda s, h: (s, h))
    table = pl.BlockSpec((SEQ_LEN, LANES), lambda s, h: (0, 0))
    return launch(
        attend_back_kernel,
        [do, q, k, v, o, lse, cos, sin],
        [block] * 5 + [pl.BlockSpec((1, 1, 8, SEQ_LEN), lambda s, h: (s, h, 0, 0)), table, table],
        "attend_back",
        grid=(seqs, pairs),
        out_specs=[block] * 3,
        out_shape=[of((rows, width))] * 3,
        scratch_shapes=[pltpu.VMEM((SEQ_LEN, LANES), F32)] * 2,
    )


def ffn_kernel(nf_ref, cot_ref, wgu_ref, wd_ref, hidden_ref, ggu_ref):
    tile = wd_ref.shape[0]
    chunk = 256
    for lo in range(0, nf_ref.shape[0], chunk):
        rows = slice(lo, lo + chunk)
        both = dot(nf_ref[rows, :], wgu_ref[...], 1, 0)
        grad_hidden = dot(cot_ref[rows, :], wd_ref[...], 1, 1)
        gate, up = both[:, :tile], both[:, tile:]
        sig = jax.nn.sigmoid(gate)
        act = gate * sig
        hidden_ref[rows, :] = (act * up).astype(BF16)
        ggu_ref[rows, :tile] = (grad_hidden * up * (sig * (1.0 + gate * (1.0 - sig)))).astype(BF16)
        ggu_ref[rows, tile:] = (grad_hidden * act).astype(BF16)


def ffn(nf, cot, w_gu, w_down):
    rows, units = nf.shape[0], w_down.shape[0]
    tile = min(UNIT_TILE, units)
    whole = pl.BlockSpec((rows, D), lambda j: (0, 0))
    return launch(
        ffn_kernel,
        [nf, cot, w_gu, w_down],
        [
            whole,
            whole,
            pl.BlockSpec((D, 2 * tile), lambda j: (0, j)),
            pl.BlockSpec((tile, D), lambda j: (j, 0)),
        ],
        "ffn",
        grid=(units // tile,),
        out_specs=[pl.BlockSpec((rows, tile), lambda j: (0, j)), pl.BlockSpec((rows, 2 * tile), lambda j: (0, j))],
        out_shape=[of((rows, units)), of((rows, 2 * units))],
    )


def product(lhs, rhs, where=None, turned=False, name="product"):
    count = len(lhs)
    rows = lhs[0].shape[0]
    columns = rhs[0].shape[0 if turned else 1]
    wide = sum(a.shape[1] for a in lhs)
    tile = min(columns, 512 if wide > 1024 else 1024)
    parts = 1 if where is None else 2
    size = rows // parts

    def kernel(*refs):
        refs = refs[parts - 1 :]
        lhs_refs, rhs_refs, out_refs = refs[: parts * count], refs[parts * count : -parts], refs[-parts:]
        for i, out_ref in enumerate(out_refs):
            total = None
            for a, b in zip(lhs_refs[i * count : (i + 1) * count], rhs_refs):
                extra = dot(a[...], b[...], 1, 1 if turned else 0)
                total = extra if total is None else total + extra
            out_ref[...] = total.astype(BF16)

    if parts == 1:
        lhs_specs = [pl.BlockSpec((rows, a.shape[1]), lambda n, *w: (0, 0)) for a in lhs]
    else:
        lhs_specs = [
            pl.BlockSpec((size, a.shape[1]), (lambda s: lambda n, w: (w[s], 0))(s)) for s in (OTHER, CORE) for a in lhs
        ]
    if turned:
        rhs_specs = [pl.BlockSpec((tile, b.shape[1]), lambda n, *w: (n, 0)) for b in rhs]
    else:
        rhs_specs = [pl.BlockSpec((b.shape[0], tile), lambda n, *w: (0, n)) for b in rhs]
    result = launch(
        kernel,
        [*list(lhs) * parts, *rhs],
        lhs_specs + rhs_specs,
        name,
        [] if where is None else [where],
        grid=(columns // tile,),
        out_specs=[pl.BlockSpec((size, tile), lambda n, *w: (0, n))] * parts,
        out_shape=[of((size, columns))] * parts,
    )
    return result[0] if parts == 1 else result


def quarter_product(sets, kinds, near, far, where, scalars, name):
    rows = near[0].shape[0]
    part = D // 8
    width = near[0].shape[1]
    tile = min(width, 512)
    tiles = width // tile
    pieces = len(near)
    first, stride = scalars
    fixed_specs = [
        pl.BlockSpec((rows, part), (lambda k, h: lambda t, w: (0, 4 * h + w[first + stride * k]))(k, h))
        for _ in sets
        for _ in range(2)
        for k in range(2)
        for h in range(2)
    ]
    piece_specs = [
        pl.BlockSpec((rows, tile), (lambda i: lambda t, w: (0, jnp.clip(t - i * tiles, 0, tiles - 1)))(i))
        for i in range(pieces)
    ]
    count = len(fixed_specs)

    def kernel(where_ref, *refs):
        fixed, near_refs, far_refs = refs[:count], refs[count : count + pieces], refs[count + pieces : -2]
        out_ref, flat = refs[-2:]
        step = pl.program_id(0)

        @pl.when(step == 0)
        def _():
            for n, ref in enumerate(fixed):
                kind, chip, at = n // 8, n // 4 % 2, n % 4
                flat[kind, at * part : (at + 1) * part, chip * rows : (chip + 1) * rows] = ref[...].T

        for i, kind in enumerate(kinds):

            @pl.when((step >= i * tiles) & (step < (i + 1) * tiles))
            def _():
                total = dot(flat[kind, :, :rows], near_refs[i][...], 1, 0)
                total += dot(flat[kind, :, rows:], far_refs[i][...], 1, 0)
                out_ref[0] = total[: 2 * part].astype(BF16)
                out_ref[1] = total[2 * part :].astype(BF16)

    return launch(
        kernel,
        [*[a for pair in sets for a in pair for _ in range(4)], *near, *far],
        fixed_specs + piece_specs * 2,
        name,
        [where],
        grid=(tiles * pieces,),
        out_specs=pl.BlockSpec((2, 2 * part, tile), lambda t, w: (0, 0, t)),
        out_shape=of((2, 2 * part, width * pieces)),
        scratch_shapes=[pltpu.VMEM((len(sets), 4 * part, 2 * rows), BF16)],
    )


def row_call(kernel, rows, where, ins, outs, sums, name):
    tile = min(256, rows)
    steps = rows // tile
    specs, arrays = [], []
    for item in ins:
        array, scalar = item if isinstance(item, tuple) else (item, None)
        if scalar is not None:
            specs.append(pl.BlockSpec((tile, D), (lambda s: lambda i, w: (w[s] * steps + i, 0))(scalar)))
        elif array.shape[0] == 1:
            specs.append(pl.BlockSpec((1, D), lambda i, w: (0, 0)))
        else:
            specs.append(pl.BlockSpec((tile, D), lambda i, w: (i, 0)))
        arrays.append(array)
    out_specs = [pl.BlockSpec((tile, width), lambda i, w: (i, 0)) for _, width in outs]
    out_shape = [of((rows, width), dtype) for dtype, width in outs]
    return launch(
        kernel,
        arrays,
        specs,
        name,
        [where],
        grid=(steps,),
        out_specs=out_specs + [pl.BlockSpec((8, D), lambda i, w: (0, 0))] * sums,
        out_shape=out_shape + [of((8, D), F32)] * sums,
    )


def add_refs(*refs):
    total = refs[0][...].astype(F32)
    for ref in refs[1:]:
        total += ref[...].astype(F32)
    return total


def split_features(where_ref, total, mine_ref, other_ref):
    first = where_ref[CORE] == 0
    low, high = total[:, : D // 2], total[:, D // 2 :]
    mine_ref[...] = jnp.where(first, low, high).astype(mine_ref.dtype)
    other_ref[...] = jnp.where(first, high, low).astype(other_ref.dtype)


def norm_kernel(where_ref, one_ref, two_ref, far_ref, x_ref, gain_ref, residual_ref, normed_ref):
    residual = add_refs(x_ref, one_ref, two_ref, far_ref)
    scale = lax.rsqrt(jnp.sum(residual * residual, axis=1, keepdims=True) / D + EPS)
    residual_ref[...] = residual
    normed_ref[...] = (residual * scale * gain_ref[...]).astype(BF16)


def norm_back(stream, gain, upstream, sum_ref):
    scale = lax.rsqrt(jnp.sum(stream * stream, axis=1, keepdims=True) / D + EPS)
    weighted = upstream * gain
    inner = jnp.sum(weighted * stream, axis=1, keepdims=True)
    part = jnp.sum((upstream * stream * scale).reshape(-1, 8, D), axis=0)

    @pl.when(pl.program_id(0) == 0)
    def _():
        sum_ref[...] = jnp.zeros_like(sum_ref)

    sum_ref[...] += part
    return scale * weighted - stream * (scale * scale * scale) * (inner / D)


def ffn_back_kernel(where_ref, one_ref, two_ref, far_ref, residual_ref, cot_ref, gain_ref, grad_ref, low_ref, sum_ref):
    back = norm_back(residual_ref[...], gain_ref[...], add_refs(one_ref, two_ref, far_ref), sum_ref)
    grad = cot_ref[...].astype(F32) + back
    grad_ref[...] = grad
    low_ref[...] = grad.astype(BF16)


def input_back_kernel(where_ref, one_ref, two_ref, far_ref, x_ref, grad_ref, gain_ref, mine_ref, other_ref, sum_ref):
    back = norm_back(x_ref[...].astype(F32), gain_ref[...], add_refs(one_ref, two_ref, far_ref), sum_ref)
    split_features(where_ref, grad_ref[...] + back, mine_ref, other_ref)


def mixed_kernel(where_ref, *refs):
    split_features(where_ref, add_refs(*refs[:-2]), *refs[-2:])


def finish(pieces, spans, turned, where, name):
    shape = pieces[0].shape
    part = shape[1]
    sizes = [2 * sum(hi - lo for lo, hi in mine) for mine in spans]

    def kernel(where_ref, *refs):
        ins, outs = refs[:4], refs[4:]
        for k in range(4):

            @pl.when(pl.program_id(0) == k)
            def _():
                for out_ref, mine, flip in zip(outs, spans, turned):
                    at = 0
                    for core in range(2):
                        for lo, hi in mine:
                            block = ins[k][core, :, lo:hi]
                            if flip:
                                out_ref[at : at + hi - lo, :] = block.T.astype(F32)
                            else:
                                out_ref[:, at : at + hi - lo] = block.astype(F32)
                            at += hi - lo

    return launch(
        kernel,
        pieces,
        [pl.BlockSpec(shape, lambda k, w: (0, 0, 0))] * 4,
        name,
        [where],
        grid=(4,),
        out_specs=[
            pl.BlockSpec((n, part), lambda k, w: (0, w[QUARTER + k]))
            if flip
            else pl.BlockSpec((part, n), lambda k, w: (w[QUARTER + k], 0))
            for n, flip in zip(sizes, turned)
        ],
        out_shape=[of((n, 4 * part) if flip else (4 * part, n), F32) for n, flip in zip(sizes, turned)],
    )


def swap_axis(values, axis, distance):
    size = lax.axis_size(axis)
    return lax.ppermute(values, axis, [(i, i ^ distance) for i in range(size)])


def other_core(values):
    return swap_axis(values, "row", 1)


def other_chip(values):
    return swap_axis(values, "col", 1)


def far_plane(values):
    return swap_axis(values, "col", 2)


def hop(values, step):
    pairs = []
    for spot in range(4):
        for core in range(2):
            distance = 1 if (step == 1) == (core == 0) else 2
            pairs.append((spot * 2 + core, (spot ^ distance) * 2 + core))
    return lax.ppermute(values, ("dp", "row"), pairs)


def hop_one(values):
    return hop(values, 1)


def hop_two(values):
    return hop(values, 2)


def add32(*values):
    total = values[0].astype(F32)
    for value in values[1:]:
        total += value.astype(F32)
    return total


class Plan:
    def __init__(self, direct, blocks):
        self.blocks = blocks
        self.core = lax.axis_index("row")
        if direct:
            spot = lax.axis_index("dp")
            quarters = [spot ^ jnp.where(self.core == 0, k, (0, 2, 1, 3)[k]) for k in range(4)]
        else:
            quarters = [jnp.int32(k) for k in range(4)]
        self.where = jnp.stack([self.core, 1 - self.core] + quarters).astype(jnp.int32)
        self.line = Line()

    def run(self, call, *values):
        return self.line.run(call, *values)

    def mix(self, call, *values):
        return self.line.mix(call, *values)

    def send(self, move, value):
        return self.line.send(move, value)

    def ship(self, move, value):
        return self.line.ship(move, value)

    def post(self, move, value):
        return self.line.post(move, value)

    def pause(self):
        self.run(short_kernel, self.line.stamp)

    def swap(self, value):
        return self.line.swap(value)

    def place(self, sources, outs, phases, name, kept=0):
        return self.run(lambda first, *rest: place([first, *rest], outs, phases, self.where, name, kept), *sources)

    def by_core(self, low, high):
        return jnp.where(self.core == 0, low, high), jnp.where(self.core == 0, high, low)


class Group:
    def __init__(self, name, plan, sets, kinds, near, far, spans, turned):
        self.name, self.plan, self.sets, self.kinds = name, plan, sets, kinds
        self.near, self.far, self.spans, self.turned = near, far, spans, turned
        self.block = sum(a.shape[1] for a in near) // plan.blocks

    def produce(self, scalars):
        plan, count = self.plan, len(self.near)
        return plan.run(
            lambda first, *rest: quarter_product(
                self.sets, self.kinds, (first,) + rest[: count - 1], rest[count - 1 :], plan.where, scalars, self.name
            ),
            *self.near, *self.far,
        )

    def make(self):
        self.sent = self.produce((QUARTER + 1, 2))

    def leave(self):
        self.came = self.plan.post(hop_one, self.sent)

    def stay(self):
        self.kept = self.produce((QUARTER, 2))

    def second(self):
        def add(kept, came):
            return add32(kept[1], came[1]).astype(BF16)

        self.back = self.plan.post(hop_two, self.plan.mix(add, self.kept, self.came))

    def cross_plane(self):
        n = self.block

        def add(kept, came, back):
            return add32(kept[0, :, n:], came[0, :, n:], back[:, n:]).astype(BF16)

        self.arrived = self.plan.post(far_plane, self.plan.mix(add, self.kept, self.came, self.back))

    def total(self):
        n = self.block

        def add(arrived, kept, came, back):
            return add32(kept[0, :, :n], came[0, :, :n], back[:, :n], arrived).astype(BF16)

        whole = self.plan.swap(self.plan.mix(add, self.arrived, self.kept, self.came, self.back))
        self.both = whole.reshape(2, -1, n)

    def spread(self):
        self.one = self.plan.ship(hop_one, self.both)
        self.two = self.plan.ship(hop_two, self.both)

    def spread_last(self):
        self.three = self.plan.send(hop_two, self.one)

    def finish(self):
        return self.plan.run(
            lambda first, *rest: finish((first,) + rest, self.spans, self.turned, self.plan.where, "finish"),
            self.both, self.one, self.two, self.three,
        )

    def whole(self, groups):
        plan = self.plan
        pieces = []
        for k in range(2):
            made = self.produce((QUARTER + 2 * k, 1))
            for one in made:
                total = jnp.stack(jnp.split(one.astype(F32), plan.blocks, axis=1))
                total = lax.psum_scatter(total, "col", scatter_dimension=0, axis_index_groups=groups)
                total = lax.psum(total, "dp").astype(BF16)
                pieces.append(plan.swap(total).reshape(2, -1, total.shape[1]))
        return finish(pieces, self.spans, self.turned, plan.where, "finish")


class Sizes:
    def __init__(self, tokens, w_query, w_gate):
        self.rows = tokens.shape[0]
        self.half = self.rows // 2
        self.width = w_query.shape[1] // 2
        self.units = w_gate.shape[1] // 2
        self.tile = min(UNIT_TILE, self.units)
        self.split = D // 2


def interleaved(s):
    return [(p, lo) for lo in range(0, s.units, s.tile) for p in range(2)]


def gu_spans(s):
    return [[(lo + p * s.tile, lo + (p + 1) * s.tile) for lo in range(0, 2 * s.units, 2 * s.tile)] for p in range(2)]


def columns(lo, size):
    return lambda w: (slice(None), pl.ds(lo, size))


def join_features(plan, s, mine, theirs):
    return plan.place(
        [mine, theirs], [of((s.rows, D))],
        [[(0, full, 0, cols_at(CORE, s.split)), (1, full, 0, cols_at(OTHER, s.split))]], "join",
    )[0]


def join_rows(plan, s, mine, theirs):
    return plan.place(
        [mine, theirs], [of((s.rows, D))], [[(0, full, 0, rows_at(CORE, s.half)), (1, full, 0, rows_at(OTHER, s.half))]], "join"
    )[0]


def pack_in(plan, s, weights, parts, name):
    total = sum(size for _, _, size, _ in parts)
    moves, at = [], 0
    for i, lo, size, step in parts:
        moves.append((i, cols_at(OTHER, step, lo, size), 0, columns(at, size)))
        at += size
    return plan.place(weights, [of((s.split, total))], [moves], name)[0]


def own_in(plan, s, weights, got, parts):
    total = got.shape[1]
    moves, at = [], 0
    for i, lo, size, step in parts:
        moves.append((i, cols_at(CORE, step, lo, size), 0, block_at(CORE, s.split, at, size)))
        at += size
    moves.append((len(weights), full, 0, rows_at(OTHER, s.split)))
    return plan.place([*weights, got], [of((D, total))], [moves], "own")[0]


def own_out(plan, s, weight, got):
    rows = got.shape[0]
    return plan.place(
        [weight, got], [of((rows, D))], [[(0, rows_at(CORE, rows), 0, cols_at(CORE, s.split)), (1, full, 0, cols_at(OTHER, s.split))]],
        "own",
    )[0]


def both_gains(plan, mine, other):
    joined = plan.mix(lambda a, b: jnp.concatenate(plan.by_core(a, b), axis=1), mine, other)
    return joined[:1], joined[1:]


def norm_first(plan, s, near, far, x_near, gains):
    return plan.run(
        lambda *a: row_call(
            norm_kernel, s.half, plan.where, [*a[:3], (a[3], CORE), a[4]], [(F32, D), (BF16, D)], 0, "norm"
        ),
        *near, far, x_near, gains,
    )


def norm_ffn_back(plan, s, near, far, residual, cot_near, gains):
    return plan.run(
        lambda *a: row_call(
            ffn_back_kernel, s.half, plan.where, [*a[:4], (a[4], CORE), a[5]], [(F32, D), (BF16, D)], 1, "ffn_back"
        ),
        *near, far, residual, cot_near, gains,
    )


def norm_input_back(plan, s, near, far, x_near, grad_residual, gains):
    return plan.run(
        lambda *a: row_call(
            input_back_kernel, s.half, plan.where, [*a[:3], (a[3], CORE), *a[4:]],
            [(F32, D // 2), (F32, D // 2)], 1, "input_back",
        ),
        *near, far, x_near, grad_residual, gains,
    )


def add_mixed(plan, s, near, *others):
    return plan.run(
        lambda *a: row_call(mixed_kernel, s.half, plan.where, list(a), [(BF16, D // 2), (BF16, D // 2)], 0, "mixed"),
        *near, *others,
    )


def core_sum(plan, lhs, weights, turned, name):
    count = len(lhs)
    other, mine = plan.run(lambda *a: product(a[:count], a[count:], plan.where, turned, name), *lhs, *weights)
    return mine, plan.ship(other_core, other)


def add_pair(plan, pair):
    return plan.mix(lambda a, b: add32(a, b).astype(BF16), pair[1], pair[0])


def side_by_side(plan, s, mine, got):
    width = mine.shape[1]
    return plan.place(
        [mine, got], [of((s.rows, width), mine.dtype)],
        [[(0, full, 0, rows_at(CORE, s.half)), (1, full, 0, rows_at(OTHER, s.half))]], "sides",
    )[0]


def grad_attended(plan, gr, weight):
    return plan.run(lambda a: product([a], [weight], turned=True, name="grad_att"), gr)


def square(tokens, gain_attn, gain_ffn, w_query, w_key, w_value, w_out, w_gate, w_up, w_down, cotangent):
    plan = Plan(True, 2)
    s = Sizes(tokens, w_query, w_gate)
    run, mix, send, ship, post, where = plan.run, plan.mix, plan.send, plan.ship, plan.post, plan.where
    cos, sin = rope_tables()
    cos_rows, sin_rows = jnp.tile(cos, (s.rows // SEQ_LEN, 1)), jnp.tile(sin, (s.rows // SEQ_LEN, 1))
    qkv_parts = [(p, 0, s.width, s.width) for p in range(3)]
    gu_parts = [(p, lo, s.tile, s.units) for p, lo in interleaved(s)]
    eighth = D // 4 // 8

    far_tokens = other_chip(tokens)
    near_tokens = other_core(tokens)
    gains_mine = jnp.stack((gain_attn, gain_ffn))
    gains_other = other_core(gains_mine)
    plan.line.stamp = gains_mine[:, :LANES]
    got_qkv = ship(other_core, pack_in(plan, s, [w_query, w_key, w_value], qkv_parts, "pack"))
    pack_out = plan.place([w_out], [of((s.width, s.split))], [[(0, rows_at(OTHER, s.width), 0, full)]], "pack")[0]
    got_out = ship(other_core, pack_out)
    own_qkv = own_in(plan, s, [w_query, w_key, w_value], got_qkv, qkv_parts)
    own_o = own_out(plan, s, w_out, got_out)
    quarter, out_rows = D // 4, s.width // 4
    slots = quarter // out_rows
    out_cols = D // slots
    qkvo = plan.place(
        [own_qkv, own_o], [of((quarter, 3 * s.width + out_cols))],
        [
            [(0, rows_at(QUARTER, quarter), 0, columns(0, 3 * s.width))]
            + [
                (
                    1, (lambda j: lambda w: (pl.ds(pl.multiple_of(w[QUARTER] * out_rows, out_rows), out_rows), pl.ds(j * out_cols, out_cols)))(j),
                    0, (lambda j: lambda w: (pl.ds(j * out_rows, out_rows), pl.ds(3 * s.width, out_cols)))(j),
                )
                for j in range(slots)
            ]
        ],
        "quarter",
    )[0]
    qkvo_zero = ship(far_plane, qkvo)
    gains_attn, gains_ffn = both_gains(plan, gains_mine, gains_other)
    got_gu = ship(other_core, pack_in(plan, s, [w_gate, w_up], gu_parts, "pack"))
    pack_down = plan.place([w_down], [of((s.units, s.split))], [[(0, rows_at(OTHER, s.units), 0, full)]], "pack")[0]
    got_down = ship(other_core, pack_down)
    x_near = join_features(plan, s, tokens, near_tokens)
    own_gu = own_in(plan, s, [w_gate, w_up], got_gu, gu_parts)
    own_d = own_out(plan, s, w_down, got_down)
    down_rows = s.units // 4
    mixed_rows = quarter // 2 + down_rows // 2
    gud = [
        plan.place(
            [own_gu, own_d], [of((mixed_rows, D))],
            [[
                (0, (lambda i: rows_span(QUARTER, quarter, i * (quarter // 2), quarter // 2))(i), 0, rows_fixed(0, quarter // 2)),
                (1, (lambda i: rows_span(QUARTER, down_rows, i * (down_rows // 2), down_rows // 2))(i), 0, rows_fixed(quarter // 2, down_rows // 2)),
            ]],
            "quarter",
        )[0]
        for i in range(2)
    ]
    gud_zero = [None, None]

    def project(x, weight, first):
        return run(lambda a: project_qkv(a, gains_attn, cos_rows, sin_rows, weight, first), x)

    normed_near, *near_own = project(x_near, own_qkv, True)
    far_half = send(other_core, far_tokens)
    o_near_own = run(attend, *near_own)
    qkvo_one, qkvo_two = send(hop_one, qkvo_zero), send(hop_two, qkvo_zero)
    gud_zero[0] = send(far_plane, gud[0])
    x_far = join_features(plan, s, far_tokens, far_half)
    normed_far, *far_own = project(x_far, own_qkv, True)
    qkvo_three = send(hop_two, qkvo_one)
    o_far_own = run(attend, *far_own)
    pieces = [qkvo_zero, qkvo_one, qkvo_two, qkvo_three]
    for_qkv, for_o = plan.place(
        pieces, [of((D, 3 * s.width)), of((s.width, D))],
        [
            [(k, columns(0, 3 * s.width), 0, rows_at(QUARTER + k, quarter)) for k in range(4)]
            + [
                (
                    k, (lambda j: lambda w: (pl.ds(j * out_rows, out_rows), pl.ds(3 * s.width, out_cols)))(j),
                    1, (lambda k, j: lambda w: (pl.ds(pl.multiple_of(w[QUARTER + k] * out_rows, out_rows), out_rows), pl.ds(j * out_cols, out_cols)))(k, j),
                )
                for k in range(4)
                for j in range(slots)
            ]
        ],
        "other",
    )
    w_qkv, w_o = [own_qkv, for_qkv], [own_o, for_o]

    far_for = project(normed_far, for_qkv, False)
    gud_one, gud_two, gud_three = [None, None], [None, None], [None, None]
    o_far = [o_far_own, run(attend, *far_for)]
    far = core_sum(plan, [o[0] for o in o_far], w_o, False, "out")
    near_for = project(normed_near, for_qkv, False)
    far = post(other_chip, add_pair(plan, far))
    gud_one[0], gud_two[0] = send(hop_one, gud_zero[0]), send(hop_two, gud_zero[0])
    gud_zero[1] = send(far_plane, gud[1])
    near_cot = send(other_core, cotangent)
    o_near = [o_near_own, run(attend, *near_for)]
    near = core_sum(plan, [o[0] for o in o_near], w_o, False, "out")
    gud_three[0] = send(hop_two, gud_one[0])
    cot_near = join_features(plan, s, cotangent, near_cot)
    residual, normed_ffn = norm_first(plan, s, near, far, x_near, gains_ffn)
    nf_row = ship(other_core, normed_ffn)
    nf_chip = post(other_chip, normed_ffn)
    def spread_out(i, outs):
        count = quarter // 2, down_rows // 2
        return plan.place(
            [g[i] for g in (gud_zero, gud_one, gud_two, gud_three)] + outs, [of(own_gu.shape), of(own_d.shape)],
            [
                [(k, rows_fixed(0, count[0]), 0, rows_span(QUARTER + k, quarter, i * count[0], count[0])) for k in range(4)]
                + [(k, rows_fixed(count[0], count[1]), 1, rows_span(QUARTER + k, down_rows, i * count[1], count[1])) for k in range(4)]
            ],
            "other", len(outs),
        )

    gud_one[1], gud_two[1] = send(hop_one, gud_zero[1]), send(hop_two, gud_zero[1])
    nf_near = join_rows(plan, s, normed_ffn, nf_row)
    fed_near = [run(ffn, nf_near, cot_near, own_gu, own_d)]
    halves = spread_out(0, [])
    nf_far_row = send(other_core, nf_chip)
    gud_three[1] = send(hop_two, gud_one[1])
    far_cot = send(other_chip, cotangent)
    plan.pause()
    nf_far = join_rows(plan, s, nf_chip, nf_far_row)
    for_gu, for_d = spread_out(1, list(halves))
    w_gu, w_d = [own_gu, for_gu], [own_d, for_d]
    fed_near.append(run(ffn, nf_near, cot_near, for_gu, for_d))
    hid_near, ggu_near = [f[0] for f in fed_near], [f[1] for f in fed_near]
    mixed_near = core_sum(plan, hid_near, w_d, False, "down")
    cot_far_row = send(other_core, far_cot)
    plan.pause()
    cot_far = join_features(plan, s, far_cot, cot_far_row)
    fed_far = [run(ffn, nf_far, cot_far, own_gu, own_d), run(ffn, nf_far, cot_far, for_gu, for_d)]
    hid_far, ggu_far = [f[0] for f in fed_far], [f[1] for f in fed_far]

    ups = Group("gu_grad", plan, [(nf_near, nf_far)], [0, 0], ggu_near, ggu_far, gu_spans(s), [False, False])
    down = Group("down_grad", plan, [(cot_near, cot_far)], [0, 0], hid_near, hid_far, [[(0, s.units)]], [True])
    ups.make()
    ups.leave()
    far = core_sum(plan, ggu_far, w_gu, True, "ffn_in")
    mixed_near = [add_pair(plan, mixed_near)]
    plan.pause()
    far = post(other_chip, add_pair(plan, far))
    near = core_sum(plan, ggu_near, w_gu, True, "ffn_in")
    ups.stay()
    grad_residual, grad_low, gain_ffn_part = norm_ffn_back(plan, s, near, far, residual, cot_near, gains_ffn)
    gr_row = ship(other_core, grad_low)
    gr_chip = post(other_chip, grad_low)
    gr_near = join_rows(plan, s, grad_low, gr_row)
    ups.second()

    def back_one(gr, heads, outs, b):
        return run(attend_back, grad_attended(plan, gr, w_o[b]), *heads[b], *outs[b], cos, sin)

    near_heads, far_heads = [near_own, near_for], [far_own, far_for]
    back_near = [back_one(gr_near, near_heads, o_near, b) for b in range(2)]
    gr_far_row = send(other_core, gr_chip)
    down.make()
    ups.cross_plane()
    down.leave()
    gr_far = join_rows(plan, s, gr_chip, gr_far_row)
    back_far = [back_one(gr_far, far_heads, o_far, b) for b in range(2)]
    dqkv_far = [jnp.concatenate(b, axis=1) for b in back_far]
    far = core_sum(plan, dqkv_far, w_qkv, True, "qkv_in")
    down.stay()
    down.second()
    far = post(other_chip, add_pair(plan, far))
    heads = Group(
        "head_grad", plan, [(normed_near, normed_far), (gr_near, gr_far)], [0, 0, 0, 1] * 2,
        [a for b in range(2) for a in (*back_near[b], o_near[b][0])],
        [a for b in range(2) for a in (*back_far[b], o_far[b][0])],
        [[(p * s.width, (p + 1) * s.width)] for p in range(4)], [False, False, False, True],
    )
    heads.make()
    heads.leave()
    down.cross_plane()
    dqkv_near = [jnp.concatenate(b, axis=1) for b in back_near]
    near = core_sum(plan, dqkv_near, w_qkv, True, "qkv_in")
    heads.stay()
    input_mine, input_other, gain_attn_part = norm_input_back(plan, s, near, far, x_near, grad_residual, gains_attn)
    input_got = ship(other_core, input_other)
    gains = mix(lambda a, b: jnp.stack((jnp.sum(a, axis=0), jnp.sum(b, axis=0))), gain_attn_part, gain_ffn_part)
    gains_got = ship(other_core, gains)
    heads.second()
    ups.total()
    ups.spread()
    gains = mix(jnp.add, gains, gains_got)
    gains_got = send(other_chip, gains)
    mixed_far = core_sum(plan, hid_far, w_d, False, "down")
    input_grad = side_by_side(plan, s, input_mine, input_got)
    mixed_far = post(other_chip, add_pair(plan, mixed_far))
    gains = mix(jnp.add, gains, gains_got)
    heads.cross_plane()
    down.total()
    ups.spread_last()
    down.spread()
    mixed_mine, mixed_other = add_mixed(plan, s, mixed_near, mixed_far, residual)
    gains_got = send(far_plane, gains)
    mixed_got = ship(other_core, mixed_other)
    gate_grad, up_grad = ups.finish()
    gains = mix(jnp.add, gains, gains_got)
    heads.total()
    heads.spread()
    down.spread_last()
    gains_got = send(hop_one, gains)
    mixed = side_by_side(plan, s, mixed_mine, mixed_got)
    (down_grad,) = down.finish()
    heads.spread_last()
    gains = mix(jnp.add, gains, gains_got)
    gains_got = send(hop_two, gains)
    gains = mix(jnp.add, gains, gains_got)
    gains = jnp.where(plan.core == 0, gains[:, : s.split], gains[:, s.split :])
    q_grad, k_grad, v_grad, out_grad = heads.finish()
    return mixed, input_grad, gains[0], gains[1], q_grad, k_grad, v_grad, out_grad, gate_grad, up_grad, down_grad


def pair_order(near, far):
    member = lax.axis_index("col") % 2
    return jnp.concatenate((jnp.where(member == 0, near, far), jnp.where(member == 0, far, near)), axis=0)


def from_pair(joined):
    member = lax.axis_index("col") % 2
    first, second = jnp.split(joined, 2, axis=0)
    return jnp.where(member == 0, first, second), jnp.where(member == 0, second, first)


def general(tokens, gain_attn, gain_ffn, w_query, w_key, w_value, w_out, w_gate, w_up, w_down, cotangent):
    blocks = lax.axis_size("col") // 2
    groups = [[i for i in range(2 * blocks) if i % 2 == m] for m in range(2)]
    plan = Plan(False, blocks)
    s = Sizes(tokens, w_query, w_gate)
    run, where = plan.run, plan.where
    cos, sin = rope_tables()
    shared = s.rows % SEQ_LEN != 0
    qkv_parts = [(p, 0, s.width, s.width) for p in range(3)]
    gu_parts = [(p, lo, s.tile, s.units) for p, lo in interleaved(s)]

    def gathered(own):
        every = lax.all_gather(own, "col", axis=0, axis_index_groups=groups)
        return [every[b] for b in range(blocks)]

    def pack_rows(weight, rows):
        return plan.place([weight], [of((rows, s.split))], [[(0, rows_at(OTHER, rows), 0, full)]], "pack")[0]

    got = other_core(pack_in(plan, s, [w_query, w_key, w_value], qkv_parts, "pack"))
    w_qkv = gathered(own_in(plan, s, [w_query, w_key, w_value], got, qkv_parts))
    got = other_core(pack_in(plan, s, [w_gate, w_up], gu_parts, "pack"))
    w_gu = gathered(own_in(plan, s, [w_gate, w_up], got, gu_parts))
    w_o = gathered(own_out(plan, s, w_out, other_core(pack_rows(w_out, s.width))))
    w_d = gathered(own_out(plan, s, w_down, other_core(pack_rows(w_down, s.units))))
    gains_mine = jnp.stack((gain_attn, gain_ffn))
    gains_attn, gains_ffn = both_gains(plan, gains_mine, other_core(gains_mine))

    def both_chips(values):
        far = other_chip(values)
        return join_features(plan, s, values, other_core(values)), join_features(plan, s, far, other_core(far))

    x_near, x_far = both_chips(tokens)
    cot_near, cot_far = both_chips(cotangent)

    def tables(offset):
        if shared:
            return [lax.dynamic_slice_in_dim(t, offset, s.rows) for t in (cos, sin)]
        return [jnp.tile(t, (s.rows // SEQ_LEN, 1)) for t in (cos, sin)]

    first = (lax.axis_index("col") % 2) * s.rows
    chips = []
    for x, offset in ((x_near, first), (x_far, s.rows - first)):
        turn = tables(offset)
        normed, *heads = run(lambda a: project_qkv(a, gains_attn, *turn, w_qkv[0], True), x)
        every = [heads]
        for w in w_qkv[1:]:
            every.append(run(lambda a: project_qkv(a, gains_attn, *turn, w, False), normed))
        chips.append((normed, every))
    (normed_near, heads_near), (normed_far, heads_far) = chips

    def together(near, far):
        return pair_order(near, far) if shared else jnp.concatenate((near, far), axis=0)

    def apart(joined):
        return from_pair(joined) if shared else jnp.split(joined, 2, axis=0)

    joined_heads = [[together(a, b) for a, b in zip(n, f)] for n, f in zip(heads_near, heads_far)]
    outs = [run(attend, *h) for h in joined_heads]
    att = [apart(o[0]) for o in outs]
    att_near, att_far = [a[0] for a in att], [a[1] for a in att]

    def four_core_sum(near, far, weights, turned, name):
        far = other_chip(add_pair(plan, core_sum(plan, far, weights, turned, name)))
        return core_sum(plan, near, weights, turned, name), far

    def gather_tokens(values):
        far = other_chip(values)
        return join_rows(plan, s, values, other_core(values)), join_rows(plan, s, far, other_core(far))

    residual, normed_ffn = norm_first(plan, s, *four_core_sum(att_near, att_far, w_o, False, "out"), x_near, gains_ffn)
    nf_near, nf_far = gather_tokens(normed_ffn)
    fed_near = [run(ffn, nf_near, cot_near, w_gu[b], w_d[b]) for b in range(blocks)]
    fed_far = [run(ffn, nf_far, cot_far, w_gu[b], w_d[b]) for b in range(blocks)]
    hid_near, ggu_near = [f[0] for f in fed_near], [f[1] for f in fed_near]
    hid_far, ggu_far = [f[0] for f in fed_far], [f[1] for f in fed_far]
    kinds = [0] * blocks
    ups = Group("gu_grad", plan, [(nf_near, nf_far)], kinds, ggu_near, ggu_far, gu_spans(s), [False, False])
    down = Group("down_grad", plan, [(cot_near, cot_far)], kinds, hid_near, hid_far, [[(0, s.units)]], [True])
    grad_residual, grad_low, gain_ffn_part = norm_ffn_back(
        plan, s, *four_core_sum(ggu_near, ggu_far, w_gu, True, "ffn_in"), residual, cot_near, gains_ffn
    )
    gr_near, gr_far = gather_tokens(grad_low)
    gr = together(gr_near, gr_far)
    backs = []
    for b in range(blocks):
        grads = run(attend_back, grad_attended(plan, gr, w_o[b]), *joined_heads[b], *outs[b], cos, sin)
        backs.append([apart(g) for g in grads])
    back_near = [[g[0] for g in b] for b in backs]
    back_far = [[g[1] for g in b] for b in backs]
    heads = Group(
        "head_grad", plan, [(normed_near, normed_far), (gr_near, gr_far)], [0, 0, 0, 1] * blocks,
        [a for b in range(blocks) for a in (*back_near[b], att_near[b])],
        [a for b in range(blocks) for a in (*back_far[b], att_far[b])],
        [[(p * s.width, (p + 1) * s.width)] for p in range(4)], [False, False, False, True],
    )
    dqkv_near = [jnp.concatenate(b, axis=1) for b in back_near]
    dqkv_far = [jnp.concatenate(b, axis=1) for b in back_far]
    input_mine, input_other, gain_attn_part = norm_input_back(
        plan, s, *four_core_sum(dqkv_near, dqkv_far, w_qkv, True, "qkv_in"), x_near, grad_residual, gains_attn
    )
    mixed_mine, mixed_other = add_mixed(plan, s, *four_core_sum(hid_near, hid_far, w_d, False, "down"), residual)
    gains = lax.psum(jnp.stack((jnp.sum(gain_attn_part, axis=0), jnp.sum(gain_ffn_part, axis=0))), ("dp", "col", "row"))
    gains = jnp.where(plan.core == 0, gains[:, : s.split], gains[:, s.split :])
    mixed = side_by_side(plan, s, mixed_mine, other_core(mixed_other))
    input_grad = side_by_side(plan, s, input_mine, other_core(input_other))
    q_grad, k_grad, v_grad, out_grad = heads.whole(groups)
    gate_grad, up_grad = ups.whole(groups)
    (down_grad,) = down.whole(groups)
    return mixed, input_grad, gains[0], gains[1], q_grad, k_grad, v_grad, out_grad, gate_grad, up_grad, down_grad


def solution(mesh):
    stream = P(("dp", "col"), "row")
    gain = P("row")
    inward, outward = P("row", "col"), P("col", "row")
    weights = (inward, inward, inward, outward, inward, inward, outward)
    fits = mesh.shape["dp"] == 4 and mesh.shape["col"] == 4
    return jax.shard_map(
        lambda *args: square(*args) if fits and args[0].shape[0] % SEQ_LEN == 0 else general(*args),
        mesh=mesh,
        in_specs=(stream, gain, gain, *weights, stream),
        out_specs=(stream, stream, gain, gain, *weights),
        check_vma=False,
    )
```

```python
import jax
import jax.numpy as jnp
from jax import lax
from jax.experimental import pallas as pl
from jax.experimental.pallas import tpu as pltpu
from jax.sharding import PartitionSpec as P

D = 2048
HEAD_DIM = 64
SEQ_LEN = 1024
LANES = 128
EPS = 1e-05
ROPE_BASE = 130000.0
VMEM = 60 * 1024 * 1024
UNIT_TILE = 256
QB = 256
COST = 10**12
F32 = jnp.float32
BF16 = jnp.bfloat16


def dot(a, b, ca, cb):
    return lax.dot_general(a, b, (((ca,), (cb,)), ((), ())), preferred_element_type=F32)


def of(shape, dtype=BF16):
    return jax.ShapeDtypeStruct(tuple(shape), dtype)


class Line:
    waiting = []

    def __init__(self):
        self.last, self.marks = [], []

    def run(self, call, *values):
        Line.waiting = list(self.last)
        result = call(*values)
        self.last = jax.tree.leaves(result)[:1] + self.marks
        self.marks = []
        return result

    def tied(self, value):
        if not self.last:
            return value
        value, *self.last = lax.optimization_barrier((value, *self.last))
        return value

    def mix(self, call, first, *values):
        first = self.tied(first)
        result = call(first, *values)
        self.last = jax.tree.leaves(result)[:1] + list(self.last)
        return result

    def send(self, move, value):
        return move(self.tied(value))

    def ship(self, move, value):
        return move(value)

    def post(self, move, value):
        sent = move(value)
        mark = other_core(self.tied(self.stamp))
        self.run(short_kernel, self.stamp)
        self.last = self.last + [mark]
        return sent

    def swap(self, value):
        value = lax.all_to_all(self.tied(value), "row", split_axis=0, concat_axis=0, tiled=True)
        self.last = [value, *self.last]
        return value


def launch(kernel, arrays, in_specs, name, prefetch=(), **rest):
    held, Line.waiting = Line.waiting, []
    skip, count = len(held), len(prefetch) + len(arrays)

    def body(*refs):
        kernel(*refs[:count], *refs[count + skip :])

    in_specs = list(in_specs) + [pl.BlockSpec(memory_space=pl.ANY)] * skip
    out_shape = rest.pop("out_shape")
    if prefetch:
        layout = dict(
            grid_spec=pltpu.PrefetchScalarGridSpec(num_scalar_prefetch=len(prefetch), in_specs=in_specs, **rest)
        )
    else:
        layout = dict(in_specs=in_specs, **rest)
    return pl.pallas_call(
        body,
        out_shape=out_shape,
        compiler_params=pltpu.CompilerParams(vmem_limit_bytes=VMEM),
        cost_estimate=pl.CostEstimate(flops=COST, bytes_accessed=1, transcendentals=0),
        name=name,
        **layout,
    )(*prefetch, *arrays, *held)


def short_kernel(values):
    def kernel(in_ref, out_ref):
        out_ref[0, 0] = 0.0

    return launch(
        kernel, [values], [pl.BlockSpec(memory_space=pl.ANY)], "short",
        out_specs=pl.BlockSpec(memory_space=pltpu.SMEM), out_shape=of((1, 1), F32),
    )


def extent(shape, index):
    sizes = []
    for size, at in zip(shape, index):
        if not isinstance(at, int):
            sizes.append(size if isinstance(at, slice) else at.size)
    return tuple(sizes)


def place(sources, outs, phases, where, name, kept=0):
    moves = [m for phase in phases for m in phase]
    shapes = [extent((sources[src] if src >= 0 else outs[-1 - src]).shape, src_at([0] * 8)) for src, src_at, _, _ in moves]
    count = len(sources)

    def kernel(where_ref, *refs):
        ins, out_refs, held = refs[:count], refs[count : count + len(outs)], refs[count + len(outs) : -2]
        in_sems, out_sems = refs[-2:]
        base = 0
        for phase in phases:
            loads, stores = [], []
            for n, (src, src_at, dst, dst_at) in enumerate(phase, base):
                src_ref = out_refs[-1 - src] if src < 0 else ins[src]
                loads.append(pltpu.make_async_copy(src_ref.at[src_at(where_ref)], held[n], in_sems.at[n]))
                stores.append(pltpu.make_async_copy(held[n], out_refs[dst].at[dst_at(where_ref)], out_sems.at[n]))
            for load in loads:
                load.start()
            for load, store in zip(loads, stores):
                load.wait()
                store.start()
            for store in stores:
                store.wait()
            base += len(phase)

    return launch(
        kernel,
        [where, *sources],
        [pl.BlockSpec(memory_space=pltpu.SMEM)] + [pl.BlockSpec(memory_space=pl.ANY)] * count,
        name,
        out_specs=[pl.BlockSpec(memory_space=pl.ANY)] * len(outs),
        out_shape=list(outs),
        scratch_shapes=[pltpu.VMEM(s, outs[m[2]].dtype) for s, m in zip(shapes, moves)] + [pltpu.SemaphoreType.DMA((len(moves),))] * 2,
        input_output_aliases={1 + count - kept + i: i for i in range(kept)},
    )


CORE, OTHER, QUARTER = 0, 1, 2


def full(_):
    return (slice(None), slice(None))


def rows_at(scalar, size, base=0):
    return lambda w: (pl.ds(pl.multiple_of(base + w[scalar] * size, size), size), slice(None))


def cols_at(scalar, size, lo=0, width=None):
    width = width or size
    return lambda w: (slice(None), pl.ds(pl.multiple_of(w[scalar] * size + lo, width), width))


def rows_span(scalar, size, lo, count):
    return lambda w: (pl.ds(pl.multiple_of(w[scalar] * size + lo, count), count), slice(None))


def rows_fixed(lo, count):
    return lambda w: (pl.ds(lo, count), slice(None))


def block_at(row_scalar, height, lo, width):
    return lambda w: (pl.ds(pl.multiple_of(w[row_scalar] * height, height), height), pl.ds(lo, width))


def rope_tables():
    half = HEAD_DIM // 2
    frequency = jnp.exp(-jnp.log(ROPE_BASE) * jnp.arange(half, dtype=F32) * (2.0 / HEAD_DIM))
    frequency = jnp.tile(frequency, 4)
    sign = jnp.where(jnp.arange(LANES) % HEAD_DIM < half, -1.0, 1.0)
    angles = jnp.arange(SEQ_LEN, dtype=F32)[:, None] * frequency[None, :]
    return jnp.cos(angles), jnp.sin(angles) * sign[None, :]


def swap_halves(values):
    half = HEAD_DIM // 2
    lane = lax.broadcasted_iota(jnp.int32, values.shape, 1)
    return jnp.where(lane % HEAD_DIM < half, pltpu.roll(values, LANES - half, 1), pltpu.roll(values, half, 1))


def qkv_kernel(first, x_ref, gain_ref, cos_ref, sin_ref, w_ref, *refs):
    q_ref, k_ref, v_ref = refs[-3:]
    if first:
        x = x_ref[...].astype(F32)
        scale = lax.rsqrt(jnp.sum(x * x, axis=1, keepdims=True) / D + EPS)
        refs[0][...] = (x * scale * gain_ref[...]).astype(BF16)
        normed = refs[0][...]
    else:
        normed = x_ref[...]
    cos, sin = cos_ref[...], sin_ref[...]
    width = q_ref.shape[1]
    projected = dot(normed, w_ref[...], 1, 0)
    for part, (out_ref, mult) in enumerate(((q_ref, HEAD_DIM**-0.5), (k_ref, 1.0))):
        for lo in range(0, width, LANES):
            piece = projected[:, part * width + lo : part * width + lo + LANES]
            out_ref[:, lo : lo + LANES] = ((piece * cos + swap_halves(piece) * sin).astype(BF16) * mult).astype(BF16)
    v_ref[...] = projected[:, 2 * width :].astype(BF16)


def project_qkv(x, gain, cos, sin, weight, first):
    rows, width = x.shape[0], weight.shape[1] // 3
    tile = min(512, rows)
    row_block = lambda n: pl.BlockSpec((tile, n), lambda i: (i, 0))
    whole = lambda a: pl.BlockSpec(a.shape, lambda i: (0, 0))
    outs = [D] * first + [width] * 3
    return launch(
        lambda *refs: qkv_kernel(first, *refs),
        [x, gain, cos, sin, weight],
        [row_block(D), whole(gain), row_block(LANES), row_block(LANES), whole(weight)],
        "qkv",
        grid=(rows // tile,),
        out_specs=[row_block(n) for n in outs],
        out_shape=[of((rows, n)) for n in outs],
    )


def head_of(values, head):
    lane = lax.broadcasted_iota(jnp.int32, values.shape, 1)
    return jnp.where((lane >= HEAD_DIM) == (head == 1), values, jnp.zeros_like(values))


def causal_scores(keys, queries, start):
    scores = dot(keys, queries, 1, 1)
    last = scores[start:]
    key_at = lax.broadcasted_iota(jnp.int32, last.shape, 0)
    query_at = lax.broadcasted_iota(jnp.int32, last.shape, 1)
    last = jnp.where(key_at <= query_at, last, -1e30)
    return last if start == 0 else jnp.concatenate((scores[:start], last), axis=0)


def attend_kernel(q_ref, k_ref, v_ref, o_ref, lse_ref):
    values = [head_of(v_ref[...], head) for head in range(2)]
    for start in range(0, SEQ_LEN, QB):
        stop = start + QB
        queries = q_ref[start:stop, :]
        outs, scales = [], []
        for head in range(2):
            scores = causal_scores(k_ref[:stop, :], head_of(queries, head), start)
            top = jnp.max(scores, axis=0, keepdims=True)
            weights = jnp.exp(scores - top)
            total = jnp.sum(weights, axis=0, keepdims=True)
            lse_ref[0, 0, head : head + 1, start:stop] = top + jnp.log(total)
            outs.append(dot(weights.astype(BF16), values[head][:stop], 0, 0))
            scales.append(jnp.broadcast_to(1.0 / total, (HEAD_DIM, QB)))
        o_ref[start:stop, :] = ((outs[0] + outs[1]) * jnp.concatenate(scales, axis=0).T).astype(BF16)


def attend(q, k, v):
    rows, width = q.shape
    seqs, pairs = rows // SEQ_LEN, width // LANES
    block = pl.BlockSpec((SEQ_LEN, LANES), lambda s, h: (s, h))
    return launch(
        attend_kernel,
        [q, k, v],
        [block] * 3,
        "attend",
        grid=(seqs, pairs),
        out_specs=[block, pl.BlockSpec((1, 1, 8, SEQ_LEN), lambda s, h: (s, h, 0, 0))],
        out_shape=[of((rows, width)), of((seqs, pairs, 8, SEQ_LEN), F32)],
    )


def attend_back_kernel(do_ref, q_ref, k_ref, v_ref, o_ref, lse_ref, cos_ref, sin_ref, dq_ref, dk_ref, dv_ref, dk_acc, dv_acc):
    k_t = k_ref[...].T
    dk_acc[...] = jnp.zeros_like(dk_acc)
    dv_acc[...] = jnp.zeros_like(dv_acc)
    for start in range(0, SEQ_LEN, QB):
        stop = start + QB
        queries, grads = q_ref[start:stop, :], do_ref[start:stop, :]
        inner = (grads.astype(F32) * o_ref[start:stop, :].astype(F32)).T
        back = []
        for head in range(2):
            one_q, one_g = head_of(queries, head), head_of(grads, head)
            scores = causal_scores(k_ref[:stop, :], one_q, start)
            weights = jnp.exp(scores - lse_ref[0, 0, head : head + 1, start:stop])
            grad_weights = dot(v_ref[:stop, :], one_g, 1, 1)
            delta = jnp.sum(inner[head * HEAD_DIM : (head + 1) * HEAD_DIM], axis=0, keepdims=True)
            grad_scores = (weights * (grad_weights - delta)).astype(BF16)
            dv_acc[:stop, :] += dot(weights.astype(BF16), one_g, 1, 0)
            dk_acc[:stop, :] += dot(grad_scores, one_q, 1, 0)
            back.append(dot(k_t[head * HEAD_DIM : (head + 1) * HEAD_DIM, :stop], grad_scores, 1, 0))
        dq = jnp.concatenate(back, axis=0).T * HEAD_DIM**-0.5
        cos, sin = cos_ref[start:stop, :], sin_ref[start:stop, :]
        dq_ref[start:stop, :] = (dq * cos - swap_halves(dq) * sin).astype(BF16)
    dk = dk_acc[...]
    dk_ref[...] = (dk * cos_ref[...] - swap_halves(dk) * sin_ref[...]).astype(BF16)
    dv_ref[...] = dv_acc[...].astype(BF16)


def attend_back(do, q, k, v, o, lse, cos, sin):
    rows, width = q.shape
    seqs, pairs = rows // SEQ_LEN, width // LANES
    block = pl.BlockSpec((SEQ_LEN, LANES), lambda s, h: (s, h))
    table = pl.BlockSpec((SEQ_LEN, LANES), lambda s, h: (0, 0))
    return launch(
        attend_back_kernel,
        [do, q, k, v, o, lse, cos, sin],
        [block] * 5 + [pl.BlockSpec((1, 1, 8, SEQ_LEN), lambda s, h: (s, h, 0, 0)), table, table],
        "attend_back",
        grid=(seqs, pairs),
        out_specs=[block] * 3,
        out_shape=[of((rows, width))] * 3,
        scratch_shapes=[pltpu.VMEM((SEQ_LEN, LANES), F32)] * 2,
    )


def ffn_kernel(nf_ref, cot_ref, wgu_ref, wd_ref, hidden_ref, ggu_ref):
    tile = wd_ref.shape[0]
    chunk = 256
    for lo in range(0, nf_ref.shape[0], chunk):
        rows = slice(lo, lo + chunk)
        both = dot(nf_ref[rows, :], wgu_ref[...], 1, 0)
        grad_hidden = dot(cot_ref[rows, :], wd_ref[...], 1, 1)
        gate, up = both[:, :tile], both[:, tile:]
        sig = jax.nn.sigmoid(gate)
        act = gate * sig
        hidden_ref[rows, :] = (act * up).astype(BF16)
        ggu_ref[rows, :tile] = (grad_hidden * up * (sig * (1.0 + gate * (1.0 - sig)))).astype(BF16)
        ggu_ref[rows, tile:] = (grad_hidden * act).astype(BF16)


def ffn(nf, cot, w_gu, w_down):
    rows, units = nf.shape[0], w_down.shape[0]
    tile = min(UNIT_TILE, units)
    whole = pl.BlockSpec((rows, D), lambda j: (0, 0))
    return launch(
        ffn_kernel,
        [nf, cot, w_gu, w_down],
        [
            whole,
            whole,
            pl.BlockSpec((D, 2 * tile), lambda j: (0, j)),
            pl.BlockSpec((tile, D), lambda j: (j, 0)),
        ],
        "ffn",
        grid=(units // tile,),
        out_specs=[pl.BlockSpec((rows, tile), lambda j: (0, j)), pl.BlockSpec((rows, 2 * tile), lambda j: (0, j))],
        out_shape=[of((rows, units)), of((rows, 2 * units))],
    )


def product(lhs, rhs, where=None, turned=False, name="product"):
    count = len(lhs)
    rows = lhs[0].shape[0]
    columns = rhs[0].shape[0 if turned else 1]
    wide = sum(a.shape[1] for a in lhs)
    tile = min(columns, 512 if wide > 1024 else 1024)
    parts = 1 if where is None else 2
    size = rows // parts

    def kernel(*refs):
        refs = refs[parts - 1 :]
        lhs_refs, rhs_refs, out_refs = refs[: parts * count], refs[parts * count : -parts], refs[-parts:]
        for i, out_ref in enumerate(out_refs):
            total = None
            for a, b in zip(lhs_refs[i * count : (i + 1) * count], rhs_refs):
                extra = dot(a[...], b[...], 1, 1 if turned else 0)
                total = extra if total is None else total + extra
            out_ref[...] = total.astype(BF16)

    if parts == 1:
        lhs_specs = [pl.BlockSpec((rows, a.shape[1]), lambda n, *w: (0, 0)) for a in lhs]
    else:
        lhs_specs = [
            pl.BlockSpec((size, a.shape[1]), (lambda s: lambda n, w: (w[s], 0))(s)) for s in (OTHER, CORE) for a in lhs
        ]
    if turned:
        rhs_specs = [pl.BlockSpec((tile, b.shape[1]), lambda n, *w: (n, 0)) for b in rhs]
    else:
        rhs_specs = [pl.BlockSpec((b.shape[0], tile), lambda n, *w: (0, n)) for b in rhs]
    result = launch(
        kernel,
        [*list(lhs) * parts, *rhs],
        lhs_specs + rhs_specs,
        name,
        [] if where is None else [where],
        grid=(columns // tile,),
        out_specs=[pl.BlockSpec((size, tile), lambda n, *w: (0, n))] * parts,
        out_shape=[of((size, columns))] * parts,
    )
    return result[0] if parts == 1 else result


def quarter_product(sets, kinds, near, far, where, scalars, name):
    rows = near[0].shape[0]
    part = D // 8
    width = near[0].shape[1]
    tile = min(width, 512)
    tiles = width // tile
    pieces = len(near)
    first, stride = scalars
    fixed_specs = [
        pl.BlockSpec((rows, part), (lambda k, h: lambda t, w: (0, 4 * h + w[first + stride * k]))(k, h))
        for _ in sets
        for _ in range(2)
        for k in range(2)
        for h in range(2)
    ]
    piece_specs = [
        pl.BlockSpec((rows, tile), (lambda i: lambda t, w: (0, jnp.clip(t - i * tiles, 0, tiles - 1)))(i))
        for i in range(pieces)
    ]
    count = len(fixed_specs)

    def kernel(where_ref, *refs):
        fixed, near_refs, far_refs = refs[:count], refs[count : count + pieces], refs[count + pieces : -2]
        out_ref, flat = refs[-2:]
        step = pl.program_id(0)

        @pl.when(step == 0)
        def _():
            for n, ref in enumerate(fixed):
                kind, chip, at = n // 8, n // 4 % 2, n % 4
                flat[kind, at * part : (at + 1) * part, chip * rows : (chip + 1) * rows] = ref[...].T

        for i, kind in enumerate(kinds):

            @pl.when((step >= i * tiles) & (step < (i + 1) * tiles))
            def _():
                total = dot(flat[kind, :, :rows], near_refs[i][...], 1, 0)
                total += dot(flat[kind, :, rows:], far_refs[i][...], 1, 0)
                out_ref[0] = total[: 2 * part].astype(BF16)
                out_ref[1] = total[2 * part :].astype(BF16)

    return launch(
        kernel,
        [*[a for pair in sets for a in pair for _ in range(4)], *near, *far],
        fixed_specs + piece_specs * 2,
        name,
        [where],
        grid=(tiles * pieces,),
        out_specs=pl.BlockSpec((2, 2 * part, tile), lambda t, w: (0, 0, t)),
        out_shape=of((2, 2 * part, width * pieces)),
        scratch_shapes=[pltpu.VMEM((len(sets), 4 * part, 2 * rows), BF16)],
    )


def row_call(kernel, rows, where, ins, outs, sums, name):
    tile = min(256, rows)
    steps = rows // tile
    specs, arrays = [], []
    for item in ins:
        array, scalar = item if isinstance(item, tuple) else (item, None)
        if scalar is not None:
            specs.append(pl.BlockSpec((tile, D), (lambda s: lambda i, w: (w[s] * steps + i, 0))(scalar)))
        elif array.shape[0] == 1:
            specs.append(pl.BlockSpec((1, D), lambda i, w: (0, 0)))
        else:
            specs.append(pl.BlockSpec((tile, D), lambda i, w: (i, 0)))
        arrays.append(array)
    out_specs = [pl.BlockSpec((tile, width), lambda i, w: (i, 0)) for _, width in outs]
    out_shape = [of((rows, width), dtype) for dtype, width in outs]
    return launch(
        kernel,
        arrays,
        specs,
        name,
        [where],
        grid=(steps,),
        out_specs=out_specs + [pl.BlockSpec((8, D), lambda i, w: (0, 0))] * sums,
        out_shape=out_shape + [of((8, D), F32)] * sums,
    )


def add_refs(*refs):
    total = refs[0][...].astype(F32)
    for ref in refs[1:]:
        total += ref[...].astype(F32)
    return total


def split_features(where_ref, total, mine_ref, other_ref):
    first = where_ref[CORE] == 0
    low, high = total[:, : D // 2], total[:, D // 2 :]
    mine_ref[...] = jnp.where(first, low, high).astype(mine_ref.dtype)
    other_ref[...] = jnp.where(first, high, low).astype(other_ref.dtype)


def norm_kernel(where_ref, one_ref, two_ref, far_ref, x_ref, gain_ref, residual_ref, normed_ref):
    residual = add_refs(x_ref, one_ref, two_ref, far_ref)
    scale = lax.rsqrt(jnp.sum(residual * residual, axis=1, keepdims=True) / D + EPS)
    residual_ref[...] = residual
    normed_ref[...] = (residual * scale * gain_ref[...]).astype(BF16)


def norm_back(stream, gain, upstream, sum_ref):
    scale = lax.rsqrt(jnp.sum(stream * stream, axis=1, keepdims=True) / D + EPS)
    weighted = upstream * gain
    inner = jnp.sum(weighted * stream, axis=1, keepdims=True)
    part = jnp.sum((upstream * stream * scale).reshape(-1, 8, D), axis=0)

    @pl.when(pl.program_id(0) == 0)
    def _():
        sum_ref[...] = jnp.zeros_like(sum_ref)

    sum_ref[...] += part
    return scale * weighted - stream * (scale * scale * scale) * (inner / D)


def ffn_back_kernel(where_ref, one_ref, two_ref, far_ref, residual_ref, cot_ref, gain_ref, grad_ref, low_ref, sum_ref):
    back = norm_back(residual_ref[...], gain_ref[...], add_refs(one_ref, two_ref, far_ref), sum_ref)
    grad = cot_ref[...].astype(F32) + back
    grad_ref[...] = grad
    low_ref[...] = grad.astype(BF16)


def input_back_kernel(where_ref, one_ref, two_ref, far_ref, x_ref, grad_ref, gain_ref, mine_ref, other_ref, sum_ref):
    back = norm_back(x_ref[...].astype(F32), gain_ref[...], add_refs(one_ref, two_ref, far_ref), sum_ref)
    split_features(where_ref, grad_ref[...] + back, mine_ref, other_ref)


def mixed_kernel(where_ref, *refs):
    split_features(where_ref, add_refs(*refs[:-2]), *refs[-2:])


def finish(pieces, spans, turned, where, name):
    shape = pieces[0].shape
    part = shape[1]
    sizes = [2 * sum(hi - lo for lo, hi in mine) for mine in spans]

    def kernel(where_ref, *refs):
        ins, outs = refs[:4], refs[4:]
        for k in range(4):

            @pl.when(pl.program_id(0) == k)
            def _():
                for out_ref, mine, flip in zip(outs, spans, turned):
                    at = 0
                    for core in range(2):
                        for lo, hi in mine:
                            block = ins[k][core, :, lo:hi]
                            if flip:
                                out_ref[at : at + hi - lo, :] = block.T.astype(F32)
                            else:
                                out_ref[:, at : at + hi - lo] = block.astype(F32)
                            at += hi - lo

    return launch(
        kernel,
        pieces,
        [pl.BlockSpec(shape, lambda k, w: (0, 0, 0))] * 4,
        name,
        [where],
        grid=(4,),
        out_specs=[
            pl.BlockSpec((n, part), lambda k, w: (0, w[QUARTER + k]))
            if flip
            else pl.BlockSpec((part, n), lambda k, w: (w[QUARTER + k], 0))
            for n, flip in zip(sizes, turned)
        ],
        out_shape=[of((n, 4 * part) if flip else (4 * part, n), F32) for n, flip in zip(sizes, turned)],
    )


def swap_axis(values, axis, distance):
    size = lax.axis_size(axis)
    return lax.ppermute(values, axis, [(i, i ^ distance) for i in range(size)])


def other_core(values):
    return swap_axis(values, "row", 1)


def other_chip(values):
    return swap_axis(values, "col", 1)


def far_plane(values):
    return swap_axis(values, "col", 2)


def hop(values, step):
    pairs = []
    for spot in range(4):
        for core in range(2):
            distance = 1 if (step == 1) == (core == 0) else 2
            pairs.append((spot * 2 + core, (spot ^ distance) * 2 + core))
    return lax.ppermute(values, ("dp", "row"), pairs)


def hop_one(values):
    return hop(values, 1)


def hop_two(values):
    return hop(values, 2)


def add32(*values):
    total = values[0].astype(F32)
    for value in values[1:]:
        total += value.astype(F32)
    return total


class Plan:
    def __init__(self, direct, blocks):
        self.blocks = blocks
        self.core = lax.axis_index("row")
        if direct:
            spot = lax.axis_index("dp")
            quarters = [spot ^ jnp.where(self.core == 0, k, (0, 2, 1, 3)[k]) for k in range(4)]
        else:
            quarters = [jnp.int32(k) for k in range(4)]
        self.where = jnp.stack([self.core, 1 - self.core] + quarters).astype(jnp.int32)
        self.line = Line()

    def run(self, call, *values):
        return self.line.run(call, *values)

    def mix(self, call, *values):
        return self.line.mix(call, *values)

    def send(self, move, value):
        return self.line.send(move, value)

    def ship(self, move, value):
        return self.line.ship(move, value)

    def post(self, move, value):
        return self.line.post(move, value)

    def pause(self):
        self.run(short_kernel, self.line.stamp)

    def swap(self, value):
        return self.line.swap(value)

    def place(self, sources, outs, phases, name, kept=0):
        return self.run(lambda first, *rest: place([first, *rest], outs, phases, self.where, name, kept), *sources)

    def by_core(self, low, high):
        return jnp.where(self.core == 0, low, high), jnp.where(self.core == 0, high, low)


class Group:
    def __init__(self, name, plan, sets, kinds, near, far, spans, turned):
        self.name, self.plan, self.sets, self.kinds = name, plan, sets, kinds
        self.near, self.far, self.spans, self.turned = near, far, spans, turned
        self.block = sum(a.shape[1] for a in near) // plan.blocks

    def produce(self, scalars):
        plan, count = self.plan, len(self.near)
        return plan.run(
            lambda first, *rest: quarter_product(
                self.sets, self.kinds, (first,) + rest[: count - 1], rest[count - 1 :], plan.where, scalars, self.name
            ),
            *self.near, *self.far,
        )

    def make(self):
        self.sent = self.produce((QUARTER + 1, 2))

    def leave(self):
        self.came = self.plan.post(hop_one, self.sent)

    def stay(self):
        self.kept = self.produce((QUARTER, 2))

    def second(self):
        def add(kept, came):
            return add32(kept[1], came[1]).astype(BF16)

        self.back = self.plan.post(hop_two, self.plan.mix(add, self.kept, self.came))

    def cross_plane(self):
        n = self.block

        def add(kept, came, back):
            return add32(kept[0, :, n:], came[0, :, n:], back[:, n:]).astype(BF16)

        self.arrived = self.plan.post(far_plane, self.plan.mix(add, self.kept, self.came, self.back))

    def total(self):
        n = self.block

        def add(arrived, kept, came, back):
            return add32(kept[0, :, :n], came[0, :, :n], back[:, :n], arrived).astype(BF16)

        whole = self.plan.swap(self.plan.mix(add, self.arrived, self.kept, self.came, self.back))
        self.both = whole.reshape(2, -1, n)

    def spread(self):
        self.one = self.plan.ship(hop_one, self.both)

    def spread_last(self):
        self.two = self.plan.send(hop_two, self.both)
        self.three = self.plan.send(hop_two, self.one)

    def finish(self):
        return self.plan.run(
            lambda first, *rest: finish((first,) + rest, self.spans, self.turned, self.plan.where, "finish"),
            self.both, self.one, self.two, self.three,
        )

    def whole(self, groups):
        plan = self.plan
        pieces = []
        for k in range(2):
            made = self.produce((QUARTER + 2 * k, 1))
            for one in made:
                total = jnp.stack(jnp.split(one.astype(F32), plan.blocks, axis=1))
                total = lax.psum_scatter(total, "col", scatter_dimension=0, axis_index_groups=groups)
                total = lax.psum(total, "dp").astype(BF16)
                pieces.append(plan.swap(total).reshape(2, -1, total.shape[1]))
        return finish(pieces, self.spans, self.turned, plan.where, "finish")


class Sizes:
    def __init__(self, tokens, w_query, w_gate):
        self.rows = tokens.shape[0]
        self.half = self.rows // 2
        self.width = w_query.shape[1] // 2
        self.units = w_gate.shape[1] // 2
        self.tile = min(UNIT_TILE, self.units)
        self.split = D // 2


def interleaved(s):
    return [(p, lo) for lo in range(0, s.units, s.tile) for p in range(2)]


def gu_spans(s):
    return [[(lo + p * s.tile, lo + (p + 1) * s.tile) for lo in range(0, 2 * s.units, 2 * s.tile)] for p in range(2)]


def columns(lo, size):
    return lambda w: (slice(None), pl.ds(lo, size))


def join_features(plan, s, mine, theirs):
    return plan.place(
        [mine, theirs], [of((s.rows, D))],
        [[(0, full, 0, cols_at(CORE, s.split)), (1, full, 0, cols_at(OTHER, s.split))]], "join",
    )[0]


def join_rows(plan, s, mine, theirs):
    return plan.place(
        [mine, theirs], [of((s.rows, D))], [[(0, full, 0, rows_at(CORE, s.half)), (1, full, 0, rows_at(OTHER, s.half))]], "join"
    )[0]


def pack_in(plan, s, weights, parts, name):
    total = sum(size for _, _, size, _ in parts)
    moves, at = [], 0
    for i, lo, size, step in parts:
        moves.append((i, cols_at(OTHER, step, lo, size), 0, columns(at, size)))
        at += size
    return plan.place(weights, [of((s.split, total))], [moves], name)[0]


def own_in(plan, s, weights, got, parts):
    total = got.shape[1]
    moves, at = [], 0
    for i, lo, size, step in parts:
        moves.append((i, cols_at(CORE, step, lo, size), 0, block_at(CORE, s.split, at, size)))
        at += size
    moves.append((len(weights), full, 0, rows_at(OTHER, s.split)))
    return plan.place([*weights, got], [of((D, total))], [moves], "own")[0]


def own_out(plan, s, weight, got):
    rows = got.shape[0]
    return plan.place(
        [weight, got], [of((rows, D))], [[(0, rows_at(CORE, rows), 0, cols_at(CORE, s.split)), (1, full, 0, cols_at(OTHER, s.split))]],
        "own",
    )[0]


def both_gains(plan, mine, other):
    joined = plan.mix(lambda a, b: jnp.concatenate(plan.by_core(a, b), axis=1), mine, other)
    return joined[:1], joined[1:]


def norm_first(plan, s, near, far, x_near, gains):
    return plan.run(
        lambda *a: row_call(
            norm_kernel, s.half, plan.where, [*a[:3], (a[3], CORE), a[4]], [(F32, D), (BF16, D)], 0, "norm"
        ),
        *near, far, x_near, gains,
    )


def norm_ffn_back(plan, s, near, far, residual, cot_near, gains):
    return plan.run(
        lambda *a: row_call(
            ffn_back_kernel, s.half, plan.where, [*a[:4], (a[4], CORE), a[5]], [(F32, D), (BF16, D)], 1, "ffn_back"
        ),
        *near, far, residual, cot_near, gains,
    )


def norm_input_back(plan, s, near, far, x_near, grad_residual, gains):
    return plan.run(
        lambda *a: row_call(
            input_back_kernel, s.half, plan.where, [*a[:3], (a[3], CORE), *a[4:]],
            [(F32, D // 2), (F32, D // 2)], 1, "input_back",
        ),
        *near, far, x_near, grad_residual, gains,
    )


def add_mixed(plan, s, near, *others):
    return plan.run(
        lambda *a: row_call(mixed_kernel, s.half, plan.where, list(a), [(BF16, D // 2), (BF16, D // 2)], 0, "mixed"),
        *near, *others,
    )


def core_sum(plan, lhs, weights, turned, name):
    count = len(lhs)
    other, mine = plan.run(lambda *a: product(a[:count], a[count:], plan.where, turned, name), *lhs, *weights)
    return mine, plan.ship(other_core, other)


def add_pair(plan, pair):
    return plan.mix(lambda a, b: add32(a, b).astype(BF16), pair[1], pair[0])


def side_by_side(plan, s, mine, got):
    width = mine.shape[1]
    return plan.place(
        [mine, got], [of((s.rows, width), mine.dtype)],
        [[(0, full, 0, rows_at(CORE, s.half)), (1, full, 0, rows_at(OTHER, s.half))]], "sides",
    )[0]


def grad_attended(plan, gr, weight):
    return plan.run(lambda a: product([a], [weight], turned=True, name="grad_att"), gr)


def square(tokens, gain_attn, gain_ffn, w_query, w_key, w_value, w_out, w_gate, w_up, w_down, cotangent):
    plan = Plan(True, 2)
    s = Sizes(tokens, w_query, w_gate)
    run, mix, send, ship, post, where = plan.run, plan.mix, plan.send, plan.ship, plan.post, plan.where
    cos, sin = rope_tables()
    cos_rows, sin_rows = jnp.tile(cos, (s.rows // SEQ_LEN, 1)), jnp.tile(sin, (s.rows // SEQ_LEN, 1))
    qkv_parts = [(p, 0, s.width, s.width) for p in range(3)]
    gu_parts = [(p, lo, s.tile, s.units) for p, lo in interleaved(s)]
    eighth = D // 4 // 8

    far_tokens = other_chip(tokens)
    near_tokens = other_core(tokens)
    gains_mine = jnp.stack((gain_attn, gain_ffn))
    gains_other = other_core(gains_mine)
    plan.line.stamp = gains_mine[:, :LANES]
    got_qkv = ship(other_core, pack_in(plan, s, [w_query, w_key, w_value], qkv_parts, "pack"))
    pack_out = plan.place([w_out], [of((s.width, s.split))], [[(0, rows_at(OTHER, s.width), 0, full)]], "pack")[0]
    got_out = ship(other_core, pack_out)
    own_qkv = own_in(plan, s, [w_query, w_key, w_value], got_qkv, qkv_parts)
    own_o = own_out(plan, s, w_out, got_out)
    quarter, out_rows = D // 4, s.width // 4
    slots = quarter // out_rows
    out_cols = D // slots
    qkvo = plan.place(
        [own_qkv, own_o], [of((quarter, 3 * s.width + out_cols))],
        [
            [(0, rows_at(QUARTER, quarter), 0, columns(0, 3 * s.width))]
            + [
                (
                    1, (lambda j: lambda w: (pl.ds(pl.multiple_of(w[QUARTER] * out_rows, out_rows), out_rows), pl.ds(j * out_cols, out_cols)))(j),
                    0, (lambda j: lambda w: (pl.ds(j * out_rows, out_rows), pl.ds(3 * s.width, out_cols)))(j),
                )
                for j in range(slots)
            ]
        ],
        "quarter",
    )[0]
    qkvo_zero = ship(far_plane, qkvo)
    gains_attn, gains_ffn = both_gains(plan, gains_mine, gains_other)
    got_gu = ship(other_core, pack_in(plan, s, [w_gate, w_up], gu_parts, "pack"))
    pack_down = plan.place([w_down], [of((s.units, s.split))], [[(0, rows_at(OTHER, s.units), 0, full)]], "pack")[0]
    got_down = ship(other_core, pack_down)
    x_near = join_features(plan, s, tokens, near_tokens)
    own_gu = own_in(plan, s, [w_gate, w_up], got_gu, gu_parts)
    own_d = own_out(plan, s, w_down, got_down)
    down_rows = s.units // 4
    mixed_rows = quarter // 2 + down_rows // 2
    gud = [
        plan.place(
            [own_gu, own_d], [of((mixed_rows, D))],
            [[
                (0, (lambda i: rows_span(QUARTER, quarter, i * (quarter // 2), quarter // 2))(i), 0, rows_fixed(0, quarter // 2)),
                (1, (lambda i: rows_span(QUARTER, down_rows, i * (down_rows // 2), down_rows // 2))(i), 0, rows_fixed(quarter // 2, down_rows // 2)),
            ]],
            "quarter",
        )[0]
        for i in range(2)
    ]
    gud_zero = [None, None]

    def project(x, weight, first):
        return run(lambda a: project_qkv(a, gains_attn, cos_rows, sin_rows, weight, first), x)

    normed_near, *near_own = project(x_near, own_qkv, True)
    far_half = send(other_core, far_tokens)
    o_near_own = run(attend, *near_own)
    qkvo_one, qkvo_two = send(hop_one, qkvo_zero), send(hop_two, qkvo_zero)
    gud_zero[0] = send(far_plane, gud[0])
    far_cot = send(other_chip, cotangent)
    x_far = join_features(plan, s, far_tokens, far_half)
    normed_far, *far_own = project(x_far, own_qkv, True)
    qkvo_three = send(hop_two, qkvo_one)
    o_far_own = run(attend, *far_own)
    pieces = [qkvo_zero, qkvo_one, qkvo_two, qkvo_three]
    for_qkv, for_o = plan.place(
        pieces, [of((D, 3 * s.width)), of((s.width, D))],
        [
            [(k, columns(0, 3 * s.width), 0, rows_at(QUARTER + k, quarter)) for k in range(4)]
            + [
                (
                    k, (lambda j: lambda w: (pl.ds(j * out_rows, out_rows), pl.ds(3 * s.width, out_cols)))(j),
                    1, (lambda k, j: lambda w: (pl.ds(pl.multiple_of(w[QUARTER + k] * out_rows, out_rows), out_rows), pl.ds(j * out_cols, out_cols)))(k, j),
                )
                for k in range(4)
                for j in range(slots)
            ]
        ],
        "other",
    )
    w_qkv, w_o = [own_qkv, for_qkv], [own_o, for_o]

    far_for = project(normed_far, for_qkv, False)
    gud_one, gud_two, gud_three = [None, None], [None, None], [None, None]
    o_far = [o_far_own, run(attend, *far_for)]
    far = core_sum(plan, [o[0] for o in o_far], w_o, False, "out")
    near_for = project(normed_near, for_qkv, False)
    far = post(other_chip, add_pair(plan, far))
    gud_one[0], gud_two[0] = send(hop_one, gud_zero[0]), send(hop_two, gud_zero[0])
    gud_zero[1] = send(far_plane, gud[1])
    near_cot = send(other_core, cotangent)
    o_near = [o_near_own, run(attend, *near_for)]
    near = core_sum(plan, [o[0] for o in o_near], w_o, False, "out")
    gud_three[0] = send(hop_two, gud_one[0])
    cot_near = join_features(plan, s, cotangent, near_cot)
    cot_far_row = send(other_core, far_cot)
    plan.pause()
    cot_far = join_features(plan, s, far_cot, cot_far_row)
    def spread_out(i, outs):
        count = quarter // 2, down_rows // 2
        return plan.place(
            [g[i] for g in (gud_zero, gud_one, gud_two, gud_three)] + outs, [of(own_gu.shape), of(own_d.shape)],
            [
                [(k, rows_fixed(0, count[0]), 0, rows_span(QUARTER + k, quarter, i * count[0], count[0])) for k in range(4)]
                + [(k, rows_fixed(count[0], count[1]), 1, rows_span(QUARTER + k, down_rows, i * count[1], count[1])) for k in range(4)]
            ],
            "other", len(outs),
        )

    halves = spread_out(0, [])
    residual, normed_ffn = norm_first(plan, s, near, far, x_near, gains_ffn)
    nf_row = ship(other_core, normed_ffn)
    nf_chip = post(other_chip, normed_ffn)
    gud_one[1], gud_two[1] = send(hop_one, gud_zero[1]), send(hop_two, gud_zero[1])
    nf_near = join_rows(plan, s, normed_ffn, nf_row)
    fed_near = [run(ffn, nf_near, cot_near, own_gu, own_d)]
    nf_far_row = send(other_core, nf_chip)
    gud_three[1] = send(hop_two, gud_one[1])
    plan.pause()
    nf_far = join_rows(plan, s, nf_chip, nf_far_row)
    fed_far = [run(ffn, nf_far, cot_far, own_gu, own_d)]
    for_gu, for_d = spread_out(1, list(halves))
    w_gu, w_d = [own_gu, for_gu], [own_d, for_d]
    fed_far.append(run(ffn, nf_far, cot_far, for_gu, for_d))
    fed_near.append(run(ffn, nf_near, cot_near, for_gu, for_d))
    hid_near, ggu_near = [f[0] for f in fed_near], [f[1] for f in fed_near]
    hid_far, ggu_far = [f[0] for f in fed_far], [f[1] for f in fed_far]

    ups = Group("gu_grad", plan, [(nf_near, nf_far)], [0, 0], ggu_near, ggu_far, gu_spans(s), [False, False])
    down = Group("down_grad", plan, [(cot_near, cot_far)], [0, 0], hid_near, hid_far, [[(0, s.units)]], [True])
    ups.make()
    ups.leave()
    far = core_sum(plan, ggu_far, w_gu, True, "ffn_in")
    plan.pause()
    far = post(other_chip, add_pair(plan, far))
    near = core_sum(plan, ggu_near, w_gu, True, "ffn_in")
    ups.stay()
    grad_residual, grad_low, gain_ffn_part = norm_ffn_back(plan, s, near, far, residual, cot_near, gains_ffn)
    gr_row = ship(other_core, grad_low)
    gr_chip = post(other_chip, grad_low)
    gr_near = join_rows(plan, s, grad_low, gr_row)
    ups.second()

    def back_one(gr, heads, outs, b):
        return run(attend_back, grad_attended(plan, gr, w_o[b]), *heads[b], *outs[b], cos, sin)

    near_heads, far_heads = [near_own, near_for], [far_own, far_for]
    back_near = [back_one(gr_near, near_heads, o_near, b) for b in range(2)]
    gr_far_row = send(other_core, gr_chip)
    down.make()
    ups.cross_plane()
    down.leave()
    gr_far = join_rows(plan, s, gr_chip, gr_far_row)
    back_far = [back_one(gr_far, far_heads, o_far, b) for b in range(2)]
    dqkv_far = [jnp.concatenate(b, axis=1) for b in back_far]
    far = core_sum(plan, dqkv_far, w_qkv, True, "qkv_in")
    heads = Group(
        "head_grad", plan, [(normed_near, normed_far), (gr_near, gr_far)], [0, 0, 0, 1] * 2,
        [a for b in range(2) for a in (*back_near[b], o_near[b][0])],
        [a for b in range(2) for a in (*back_far[b], o_far[b][0])],
        [[(p * s.width, (p + 1) * s.width)] for p in range(4)], [False, False, False, True],
    )
    heads.make()
    heads.leave()
    far = post(other_chip, add_pair(plan, far))
    down.stay()
    down.second()
    ups.total()
    dqkv_near = [jnp.concatenate(b, axis=1) for b in back_near]
    near = core_sum(plan, dqkv_near, w_qkv, True, "qkv_in")
    heads.stay()
    heads.second()
    down.cross_plane()
    input_mine, input_other, gain_attn_part = norm_input_back(plan, s, near, far, x_near, grad_residual, gains_attn)
    input_got = ship(other_core, input_other)
    gains = mix(lambda a, b: jnp.stack((jnp.sum(a, axis=0), jnp.sum(b, axis=0))), gain_attn_part, gain_ffn_part)
    gains_got = ship(other_core, gains)
    mixed_near = core_sum(plan, hid_near, w_d, False, "down")
    input_grad = side_by_side(plan, s, input_mine, input_got)
    gains = mix(jnp.add, gains, gains_got)
    gains_got = ship(hop_one, gains)
    heads.cross_plane()
    mixed_far = core_sum(plan, hid_far, w_d, False, "down")
    gains = mix(jnp.add, gains, gains_got)
    gains_got = ship(hop_two, gains)
    ups.spread()
    plan.pause()
    mixed_far = post(other_chip, add_pair(plan, mixed_far))
    down.total()
    down.spread()
    gains = mix(jnp.add, gains, gains_got)
    gains_got = ship(other_chip, gains)
    ups.spread_last()
    plan.pause()
    gains = mix(jnp.add, gains, gains_got)
    heads.total()
    heads.spread()
    down.spread_last()
    gains_got = ship(far_plane, gains)
    gate_grad, up_grad = ups.finish()
    mixed_mine, mixed_other = add_mixed(plan, s, mixed_near, mixed_far, residual)
    mixed_got = ship(other_core, mixed_other)
    heads.spread_last()
    (down_grad,) = down.finish()
    mixed = side_by_side(plan, s, mixed_mine, mixed_got)
    gains = mix(jnp.add, gains, gains_got)
    gains = jnp.where(plan.core == 0, gains[:, : s.split], gains[:, s.split :])
    q_grad, k_grad, v_grad, out_grad = heads.finish()
    return mixed, input_grad, gains[0], gains[1], q_grad, k_grad, v_grad, out_grad, gate_grad, up_grad, down_grad


def pair_order(near, far):
    member = lax.axis_index("col") % 2
    return jnp.concatenate((jnp.where(member == 0, near, far), jnp.where(member == 0, far, near)), axis=0)


def from_pair(joined):
    member = lax.axis_index("col") % 2
    first, second = jnp.split(joined, 2, axis=0)
    return jnp.where(member == 0, first, second), jnp.where(member == 0, second, first)


def general(tokens, gain_attn, gain_ffn, w_query, w_key, w_value, w_out, w_gate, w_up, w_down, cotangent):
    blocks = lax.axis_size("col") // 2
    groups = [[i for i in range(2 * blocks) if i % 2 == m] for m in range(2)]
    plan = Plan(False, blocks)
    s = Sizes(tokens, w_query, w_gate)
    run, where = plan.run, plan.where
    cos, sin = rope_tables()
    shared = s.rows % SEQ_LEN != 0
    qkv_parts = [(p, 0, s.width, s.width) for p in range(3)]
    gu_parts = [(p, lo, s.tile, s.units) for p, lo in interleaved(s)]

    def gathered(own):
        every = lax.all_gather(own, "col", axis=0, axis_index_groups=groups)
        return [every[b] for b in range(blocks)]

    def pack_rows(weight, rows):
        return plan.place([weight], [of((rows, s.split))], [[(0, rows_at(OTHER, rows), 0, full)]], "pack")[0]

    got = other_core(pack_in(plan, s, [w_query, w_key, w_value], qkv_parts, "pack"))
    w_qkv = gathered(own_in(plan, s, [w_query, w_key, w_value], got, qkv_parts))
    got = other_core(pack_in(plan, s, [w_gate, w_up], gu_parts, "pack"))
    w_gu = gathered(own_in(plan, s, [w_gate, w_up], got, gu_parts))
    w_o = gathered(own_out(plan, s, w_out, other_core(pack_rows(w_out, s.width))))
    w_d = gathered(own_out(plan, s, w_down, other_core(pack_rows(w_down, s.units))))
    gains_mine = jnp.stack((gain_attn, gain_ffn))
    gains_attn, gains_ffn = both_gains(plan, gains_mine, other_core(gains_mine))

    def both_chips(values):
        far = other_chip(values)
        return join_features(plan, s, values, other_core(values)), join_features(plan, s, far, other_core(far))

    x_near, x_far = both_chips(tokens)
    cot_near, cot_far = both_chips(cotangent)

    def tables(offset):
        if shared:
            return [lax.dynamic_slice_in_dim(t, offset, s.rows) for t in (cos, sin)]
        return [jnp.tile(t, (s.rows // SEQ_LEN, 1)) for t in (cos, sin)]

    first = (lax.axis_index("col") % 2) * s.rows
    chips = []
    for x, offset in ((x_near, first), (x_far, s.rows - first)):
        turn = tables(offset)
        normed, *heads = run(lambda a: project_qkv(a, gains_attn, *turn, w_qkv[0], True), x)
        every = [heads]
        for w in w_qkv[1:]:
            every.append(run(lambda a: project_qkv(a, gains_attn, *turn, w, False), normed))
        chips.append((normed, every))
    (normed_near, heads_near), (normed_far, heads_far) = chips

    def together(near, far):
        return pair_order(near, far) if shared else jnp.concatenate((near, far), axis=0)

    def apart(joined):
        return from_pair(joined) if shared else jnp.split(joined, 2, axis=0)

    joined_heads = [[together(a, b) for a, b in zip(n, f)] for n, f in zip(heads_near, heads_far)]
    outs = [run(attend, *h) for h in joined_heads]
    att = [apart(o[0]) for o in outs]
    att_near, att_far = [a[0] for a in att], [a[1] for a in att]

    def four_core_sum(near, far, weights, turned, name):
        far = other_chip(add_pair(plan, core_sum(plan, far, weights, turned, name)))
        return core_sum(plan, near, weights, turned, name), far

    def gather_tokens(values):
        far = other_chip(values)
        return join_rows(plan, s, values, other_core(values)), join_rows(plan, s, far, other_core(far))

    residual, normed_ffn = norm_first(plan, s, *four_core_sum(att_near, att_far, w_o, False, "out"), x_near, gains_ffn)
    nf_near, nf_far = gather_tokens(normed_ffn)
    fed_near = [run(ffn, nf_near, cot_near, w_gu[b], w_d[b]) for b in range(blocks)]
    fed_far = [run(ffn, nf_far, cot_far, w_gu[b], w_d[b]) for b in range(blocks)]
    hid_near, ggu_near = [f[0] for f in fed_near], [f[1] for f in fed_near]
    hid_far, ggu_far = [f[0] for f in fed_far], [f[1] for f in fed_far]
    kinds = [0] * blocks
    ups = Group("gu_grad", plan, [(nf_near, nf_far)], kinds, ggu_near, ggu_far, gu_spans(s), [False, False])
    down = Group("down_grad", plan, [(cot_near, cot_far)], kinds, hid_near, hid_far, [[(0, s.units)]], [True])
    grad_residual, grad_low, gain_ffn_part = norm_ffn_back(
        plan, s, *four_core_sum(ggu_near, ggu_far, w_gu, True, "ffn_in"), residual, cot_near, gains_ffn
    )
    gr_near, gr_far = gather_tokens(grad_low)
    gr = together(gr_near, gr_far)
    backs = []
    for b in range(blocks):
        grads = run(attend_back, grad_attended(plan, gr, w_o[b]), *joined_heads[b], *outs[b], cos, sin)
        backs.append([apart(g) for g in grads])
    back_near = [[g[0] for g in b] for b in backs]
    back_far = [[g[1] for g in b] for b in backs]
    heads = Group(
        "head_grad", plan, [(normed_near, normed_far), (gr_near, gr_far)], [0, 0, 0, 1] * blocks,
        [a for b in range(blocks) for a in (*back_near[b], att_near[b])],
        [a for b in range(blocks) for a in (*back_far[b], att_far[b])],
        [[(p * s.width, (p + 1) * s.width)] for p in range(4)], [False, False, False, True],
    )
    dqkv_near = [jnp.concatenate(b, axis=1) for b in back_near]
    dqkv_far = [jnp.concatenate(b, axis=1) for b in back_far]
    input_mine, input_other, gain_attn_part = norm_input_back(
        plan, s, *four_core_sum(dqkv_near, dqkv_far, w_qkv, True, "qkv_in"), x_near, grad_residual, gains_attn
    )
    mixed_mine, mixed_other = add_mixed(plan, s, *four_core_sum(hid_near, hid_far, w_d, False, "down"), residual)
    gains = lax.psum(jnp.stack((jnp.sum(gain_attn_part, axis=0), jnp.sum(gain_ffn_part, axis=0))), ("dp", "col", "row"))
    gains = jnp.where(plan.core == 0, gains[:, : s.split], gains[:, s.split :])
    mixed = side_by_side(plan, s, mixed_mine, other_core(mixed_other))
    input_grad = side_by_side(plan, s, input_mine, other_core(input_other))
    q_grad, k_grad, v_grad, out_grad = heads.whole(groups)
    gate_grad, up_grad = ups.whole(groups)
    (down_grad,) = down.whole(groups)
    return mixed, input_grad, gains[0], gains[1], q_grad, k_grad, v_grad, out_grad, gate_grad, up_grad, down_grad


def solution(mesh):
    stream = P(("dp", "col"), "row")
    gain = P("row")
    inward, outward = P("row", "col"), P("col", "row")
    weights = (inward, inward, inward, outward, inward, inward, outward)
    fits = mesh.shape["dp"] == 4 and mesh.shape["col"] == 4
    return jax.shard_map(
        lambda *args: square(*args) if fits and args[0].shape[0] % SEQ_LEN == 0 else general(*args),
        mesh=mesh,
        in_specs=(stream, gain, gain, *weights, stream),
        out_specs=(stream, stream, gain, gain, *weights),
        check_vma=False,
    )
```

```python
import jax
import jax.numpy as jnp
from jax import lax
from jax.experimental import pallas as pl
from jax.experimental.pallas import tpu as pltpu
from jax.sharding import PartitionSpec as P

D = 2048
HEAD_DIM = 64
SEQ_LEN = 1024
LANES = 128
EPS = 1e-05
ROPE_BASE = 130000.0
VMEM = 40 * 1024 * 1024
UNIT_TILE = 256
QB = 256
COST = 10**12
F32 = jnp.float32
BF16 = jnp.bfloat16


def dot(a, b, ca, cb):
    return lax.dot_general(a, b, (((ca,), (cb,)), ((), ())), preferred_element_type=F32)


def of(shape, dtype=BF16):
    return jax.ShapeDtypeStruct(tuple(shape), dtype)


class Line:
    waiting = []

    def __init__(self):
        self.last, self.marks = [], []

    def run(self, call, *values):
        Line.waiting = list(self.last)
        result = call(*values)
        self.last = jax.tree.leaves(result)[:1] + self.marks
        self.marks = []
        return result

    def tied(self, value):
        if not self.last:
            return value
        value, *self.last = lax.optimization_barrier((value, *self.last))
        return value

    def mix(self, call, first, *values):
        first = self.tied(first)
        result = call(first, *values)
        self.last = jax.tree.leaves(result)[:1] + list(self.last)
        return result

    def send(self, move, value):
        return move(self.tied(value))

    def ship(self, move, value):
        return move(value)

    def post(self, move, value):
        sent = move(value)
        mark = other_core(self.tied(self.stamp))
        self.run(short_kernel, self.stamp)
        self.last = self.last + [mark]
        return sent

    def swap(self, value):
        value = lax.all_to_all(self.tied(value), "row", split_axis=0, concat_axis=0, tiled=True)
        self.last = [value, *self.last]
        return value


ONCE = pl.Buffered(1)


def launch(kernel, arrays, in_specs, name, prefetch=(), **rest):
    held, Line.waiting = Line.waiting, []
    skip, count = len(held), len(prefetch) + len(arrays)

    def body(*refs):
        kernel(*refs[:count], *refs[count + skip :])

    in_specs = list(in_specs) + [pl.BlockSpec(memory_space=pl.ANY)] * skip
    out_shape = rest.pop("out_shape")
    if prefetch:
        layout = dict(
            grid_spec=pltpu.PrefetchScalarGridSpec(num_scalar_prefetch=len(prefetch), in_specs=in_specs, **rest)
        )
    else:
        layout = dict(in_specs=in_specs, **rest)
    return pl.pallas_call(
        body,
        out_shape=out_shape,
        compiler_params=pltpu.CompilerParams(vmem_limit_bytes=VMEM),
        cost_estimate=pl.CostEstimate(flops=COST, bytes_accessed=1, transcendentals=0),
        name=name,
        **layout,
    )(*prefetch, *arrays, *held)


def short_kernel(values):
    def kernel(in_ref, out_ref):
        out_ref[0, 0] = 0.0

    return launch(
        kernel, [values], [pl.BlockSpec(memory_space=pl.ANY)], "short",
        out_specs=pl.BlockSpec(memory_space=pltpu.SMEM), out_shape=of((1, 1), F32),
    )


def extent(shape, index):
    sizes = []
    for size, at in zip(shape, index):
        if not isinstance(at, int):
            sizes.append(size if isinstance(at, slice) else at.size)
    return tuple(sizes)


def place(sources, outs, phases, where, name, kept=0):
    moves = [m for phase in phases for m in phase]
    shapes = [extent((sources[src] if src >= 0 else outs[-1 - src]).shape, src_at([0] * 8)) for src, src_at, _, _ in moves]
    count = len(sources)

    def kernel(where_ref, *refs):
        ins, out_refs, held = refs[:count], refs[count : count + len(outs)], refs[count + len(outs) : -2]
        in_sems, out_sems = refs[-2:]
        base = 0
        for phase in phases:
            loads, stores = [], []
            for n, (src, src_at, dst, dst_at) in enumerate(phase, base):
                src_ref = out_refs[-1 - src] if src < 0 else ins[src]
                loads.append(pltpu.make_async_copy(src_ref.at[src_at(where_ref)], held[n], in_sems.at[n]))
                stores.append(pltpu.make_async_copy(held[n], out_refs[dst].at[dst_at(where_ref)], out_sems.at[n]))
            for load in loads:
                load.start()
            for load, store in zip(loads, stores):
                load.wait()
                store.start()
            for store in stores:
                store.wait()
            base += len(phase)

    return launch(
        kernel,
        [where, *sources],
        [pl.BlockSpec(memory_space=pltpu.SMEM)] + [pl.BlockSpec(memory_space=pl.ANY)] * count,
        name,
        out_specs=[pl.BlockSpec(memory_space=pl.ANY)] * len(outs),
        out_shape=list(outs),
        scratch_shapes=[pltpu.VMEM(s, outs[m[2]].dtype) for s, m in zip(shapes, moves)] + [pltpu.SemaphoreType.DMA((len(moves),))] * 2,
        input_output_aliases={1 + count - kept + i: i for i in range(kept)},
    )


CORE, OTHER, QUARTER = 0, 1, 2


def full(_):
    return (slice(None), slice(None))


def rows_at(scalar, size, base=0):
    return lambda w: (pl.ds(pl.multiple_of(base + w[scalar] * size, size), size), slice(None))


def cols_at(scalar, size, lo=0, width=None):
    width = width or size
    return lambda w: (slice(None), pl.ds(pl.multiple_of(w[scalar] * size + lo, width), width))


def rows_span(scalar, size, lo, count):
    return lambda w: (pl.ds(pl.multiple_of(w[scalar] * size + lo, count), count), slice(None))


def rows_fixed(lo, count):
    return lambda w: (pl.ds(lo, count), slice(None))


def block_at(row_scalar, height, lo, width):
    return lambda w: (pl.ds(pl.multiple_of(w[row_scalar] * height, height), height), pl.ds(lo, width))


def rope_tables():
    half = HEAD_DIM // 2
    frequency = jnp.exp(-jnp.log(ROPE_BASE) * jnp.arange(half, dtype=F32) * (2.0 / HEAD_DIM))
    frequency = jnp.tile(frequency, 4)
    sign = jnp.where(jnp.arange(LANES) % HEAD_DIM < half, -1.0, 1.0)
    angles = jnp.arange(SEQ_LEN, dtype=F32)[:, None] * frequency[None, :]
    return jnp.cos(angles), jnp.sin(angles) * sign[None, :]


def swap_halves(values):
    half = HEAD_DIM // 2
    lane = lax.broadcasted_iota(jnp.int32, values.shape, 1)
    return jnp.where(lane % HEAD_DIM < half, pltpu.roll(values, LANES - half, 1), pltpu.roll(values, half, 1))


def qkv_kernel(first, x_ref, gain_ref, cos_ref, sin_ref, w_ref, *refs):
    q_ref, k_ref, v_ref = refs[-3:]
    if first:
        x = x_ref[...].astype(F32)
        scale = lax.rsqrt(jnp.sum(x * x, axis=1, keepdims=True) / D + EPS)
        refs[0][...] = (x * scale * gain_ref[...]).astype(BF16)
        normed = refs[0][...]
    else:
        normed = x_ref[...]
    cos, sin = cos_ref[...], sin_ref[...]
    width = q_ref.shape[1]
    projected = dot(normed, w_ref[...], 1, 0)
    for part, (out_ref, mult) in enumerate(((q_ref, HEAD_DIM**-0.5), (k_ref, 1.0))):
        for lo in range(0, width, LANES):
            piece = projected[:, part * width + lo : part * width + lo + LANES]
            out_ref[:, lo : lo + LANES] = ((piece * cos + swap_halves(piece) * sin).astype(BF16) * mult).astype(BF16)
    v_ref[...] = projected[:, 2 * width :].astype(BF16)


def project_qkv(x, gain, cos, sin, weight, first):
    rows, width = x.shape[0], weight.shape[1] // 3
    tile = min(512, rows)
    row_block = lambda n: pl.BlockSpec((tile, n), lambda i: (i, 0))
    whole = lambda a: pl.BlockSpec(a.shape, lambda i: (0, 0), pipeline_mode=ONCE)
    outs = [D] * first + [width] * 3
    return launch(
        lambda *refs: qkv_kernel(first, *refs),
        [x, gain, cos, sin, weight],
        [row_block(D), whole(gain), row_block(LANES), row_block(LANES), whole(weight)],
        "qkv",
        grid=(rows // tile,),
        out_specs=[row_block(n) for n in outs],
        out_shape=[of((rows, n)) for n in outs],
    )


def head_of(values, head):
    lane = lax.broadcasted_iota(jnp.int32, values.shape, 1)
    return jnp.where((lane >= HEAD_DIM) == (head == 1), values, jnp.zeros_like(values))


def causal_scores(keys, queries, start):
    scores = dot(keys, queries, 1, 1)
    last = scores[start:]
    key_at = lax.broadcasted_iota(jnp.int32, last.shape, 0)
    query_at = lax.broadcasted_iota(jnp.int32, last.shape, 1)
    last = jnp.where(key_at <= query_at, last, -1e30)
    return last if start == 0 else jnp.concatenate((scores[:start], last), axis=0)


def attend_kernel(q_ref, k_ref, v_ref, o_ref, lse_ref):
    values = [head_of(v_ref[...], head) for head in range(2)]
    for start in range(0, SEQ_LEN, QB):
        stop = start + QB
        queries = q_ref[start:stop, :]
        outs, scales = [], []
        for head in range(2):
            scores = causal_scores(k_ref[:stop, :], head_of(queries, head), start)
            top = jnp.max(scores, axis=0, keepdims=True)
            weights = jnp.exp(scores - top)
            total = jnp.sum(weights, axis=0, keepdims=True)
            lse_ref[0, 0, head : head + 1, start:stop] = top + jnp.log(total)
            outs.append(dot(weights.astype(BF16), values[head][:stop], 0, 0))
            scales.append(jnp.broadcast_to(1.0 / total, (HEAD_DIM, QB)))
        o_ref[start:stop, :] = ((outs[0] + outs[1]) * jnp.concatenate(scales, axis=0).T).astype(BF16)


def attend(q, k, v):
    rows, width = q.shape
    seqs, pairs = rows // SEQ_LEN, width // LANES
    block = pl.BlockSpec((SEQ_LEN, LANES), lambda s, h: (s, h))
    return launch(
        attend_kernel,
        [q, k, v],
        [block] * 3,
        "attend",
        grid=(seqs, pairs),
        out_specs=[block, pl.BlockSpec((1, 1, 8, SEQ_LEN), lambda s, h: (s, h, 0, 0))],
        out_shape=[of((rows, width)), of((seqs, pairs, 8, SEQ_LEN), F32)],
    )


def attend_back_kernel(do_ref, q_ref, k_ref, v_ref, o_ref, lse_ref, cos_ref, sin_ref, dq_ref, dk_ref, dv_ref, dk_acc, dv_acc):
    k_t = k_ref[...].T
    dk_acc[...] = jnp.zeros_like(dk_acc)
    dv_acc[...] = jnp.zeros_like(dv_acc)
    for start in range(0, SEQ_LEN, QB):
        stop = start + QB
        queries, grads = q_ref[start:stop, :], do_ref[start:stop, :]
        inner = (grads.astype(F32) * o_ref[start:stop, :].astype(F32)).T
        back = []
        for head in range(2):
            one_q, one_g = head_of(queries, head), head_of(grads, head)
            scores = causal_scores(k_ref[:stop, :], one_q, start)
            weights = jnp.exp(scores - lse_ref[0, 0, head : head + 1, start:stop])
            grad_weights = dot(v_ref[:stop, :], one_g, 1, 1)
            delta = jnp.sum(inner[head * HEAD_DIM : (head + 1) * HEAD_DIM], axis=0, keepdims=True)
            grad_scores = (weights * (grad_weights - delta)).astype(BF16)
            dv_acc[:stop, :] += dot(weights.astype(BF16), one_g, 1, 0)
            dk_acc[:stop, :] += dot(grad_scores, one_q, 1, 0)
            back.append(dot(k_t[head * HEAD_DIM : (head + 1) * HEAD_DIM, :stop], grad_scores, 1, 0))
        dq = jnp.concatenate(back, axis=0).T * HEAD_DIM**-0.5
        cos, sin = cos_ref[start:stop, :], sin_ref[start:stop, :]
        dq_ref[start:stop, :] = (dq * cos - swap_halves(dq) * sin).astype(BF16)
    dk = dk_acc[...]
    dk_ref[...] = (dk * cos_ref[...] - swap_halves(dk) * sin_ref[...]).astype(BF16)
    dv_ref[...] = dv_acc[...].astype(BF16)


def attend_back(do, q, k, v, o, lse, cos, sin):
    rows, width = q.shape
    seqs, pairs = rows // SEQ_LEN, width // LANES
    block = pl.BlockSpec((SEQ_LEN, LANES), lambda s, h: (s, h))
    table = pl.BlockSpec((SEQ_LEN, LANES), lambda s, h: (0, 0))
    return launch(
        attend_back_kernel,
        [do, q, k, v, o, lse, cos, sin],
        [block] * 5 + [pl.BlockSpec((1, 1, 8, SEQ_LEN), lambda s, h: (s, h, 0, 0)), table, table],
        "attend_back",
        grid=(seqs, pairs),
        out_specs=[block] * 3,
        out_shape=[of((rows, width))] * 3,
        scratch_shapes=[pltpu.VMEM((SEQ_LEN, LANES), F32)] * 2,
    )


def ffn_kernel(nf_ref, cot_ref, wgu_ref, wd_ref, hidden_ref, ggu_ref):
    tile = wd_ref.shape[0]
    chunk = 256
    for lo in range(0, nf_ref.shape[0], chunk):
        rows = slice(lo, lo + chunk)
        both = dot(nf_ref[rows, :], wgu_ref[...], 1, 0)
        grad_hidden = dot(cot_ref[rows, :], wd_ref[...], 1, 1)
        gate, up = both[:, :tile], both[:, tile:]
        sig = jax.nn.sigmoid(gate)
        act = gate * sig
        hidden_ref[rows, :] = (act * up).astype(BF16)
        ggu_ref[rows, :tile] = (grad_hidden * up * (sig * (1.0 + gate * (1.0 - sig)))).astype(BF16)
        ggu_ref[rows, tile:] = (grad_hidden * act).astype(BF16)


def ffn(nf, cot, w_gu, w_down):
    rows, units = nf.shape[0], w_down.shape[0]
    tile = min(UNIT_TILE, units)
    whole = pl.BlockSpec((rows, D), lambda j: (0, 0), pipeline_mode=ONCE)
    return launch(
        ffn_kernel,
        [nf, cot, w_gu, w_down],
        [
            whole,
            whole,
            pl.BlockSpec((D, 2 * tile), lambda j: (0, j)),
            pl.BlockSpec((tile, D), lambda j: (j, 0)),
        ],
        "ffn",
        grid=(units // tile,),
        out_specs=[pl.BlockSpec((rows, tile), lambda j: (0, j)), pl.BlockSpec((rows, 2 * tile), lambda j: (0, j))],
        out_shape=[of((rows, units)), of((rows, 2 * units))],
    )


def product(lhs, rhs, where=None, turned=False, name="product"):
    count = len(lhs)
    rows = lhs[0].shape[0]
    columns = rhs[0].shape[0 if turned else 1]
    wide = sum(a.shape[1] for a in lhs)
    tile = min(columns, 512 if wide > 1024 else 1024)
    parts = 1 if where is None else 2
    size = rows // parts

    def kernel(*refs):
        refs = refs[parts - 1 :]
        lhs_refs, rhs_refs, out_refs = refs[: parts * count], refs[parts * count : -parts], refs[-parts:]
        for i, out_ref in enumerate(out_refs):
            total = None
            for a, b in zip(lhs_refs[i * count : (i + 1) * count], rhs_refs):
                extra = dot(a[...], b[...], 1, 1 if turned else 0)
                total = extra if total is None else total + extra
            out_ref[...] = total.astype(BF16)

    if parts == 1:
        lhs_specs = [pl.BlockSpec((rows, a.shape[1]), lambda n, *w: (0, 0), pipeline_mode=ONCE) for a in lhs]
    else:
        lhs_specs = [
            pl.BlockSpec((size, a.shape[1]), (lambda s: lambda n, w: (w[s], 0))(s), pipeline_mode=ONCE)
            for s in (OTHER, CORE)
            for a in lhs
        ]
    if turned:
        rhs_specs = [pl.BlockSpec((tile, b.shape[1]), lambda n, *w: (n, 0)) for b in rhs]
    else:
        rhs_specs = [pl.BlockSpec((b.shape[0], tile), lambda n, *w: (0, n)) for b in rhs]
    result = launch(
        kernel,
        [*list(lhs) * parts, *rhs],
        lhs_specs + rhs_specs,
        name,
        [] if where is None else [where],
        grid=(columns // tile,),
        out_specs=[pl.BlockSpec((size, tile), lambda n, *w: (0, n))] * parts,
        out_shape=[of((size, columns))] * parts,
    )
    return result[0] if parts == 1 else result


def quarter_product(sets, kinds, near, far, where, scalars, name):
    rows = near[0].shape[0]
    part = D // 8
    width = near[0].shape[1]
    tile = min(width, 512)
    tiles = width // tile
    pieces = len(near)
    first, stride = scalars
    fixed_specs = [
        pl.BlockSpec((rows, part), (lambda k, h: lambda t, w: (0, 4 * h + w[first + stride * k]))(k, h), pipeline_mode=ONCE)
        for _ in sets
        for _ in range(2)
        for k in range(2)
        for h in range(2)
    ]
    piece_specs = [
        pl.BlockSpec((rows, tile), (lambda i: lambda t, w: (0, jnp.clip(t - i * tiles, 0, tiles - 1)))(i))
        for i in range(pieces)
    ]
    count = len(fixed_specs)

    def kernel(where_ref, *refs):
        fixed, near_refs, far_refs = refs[:count], refs[count : count + pieces], refs[count + pieces : -2]
        out_ref, flat = refs[-2:]
        step = pl.program_id(0)

        @pl.when(step == 0)
        def _():
            for n, ref in enumerate(fixed):
                kind, chip, at = n // 8, n // 4 % 2, n % 4
                flat[kind, at * part : (at + 1) * part, chip * rows : (chip + 1) * rows] = ref[...].T

        for i, kind in enumerate(kinds):

            @pl.when((step >= i * tiles) & (step < (i + 1) * tiles))
            def _():
                total = dot(flat[kind, :, :rows], near_refs[i][...], 1, 0)
                total += dot(flat[kind, :, rows:], far_refs[i][...], 1, 0)
                out_ref[0] = total[: 2 * part].astype(BF16)
                out_ref[1] = total[2 * part :].astype(BF16)

    return launch(
        kernel,
        [*[a for pair in sets for a in pair for _ in range(4)], *near, *far],
        fixed_specs + piece_specs * 2,
        name,
        [where],
        grid=(tiles * pieces,),
        out_specs=pl.BlockSpec((2, 2 * part, tile), lambda t, w: (0, 0, t)),
        out_shape=of((2, 2 * part, width * pieces)),
        scratch_shapes=[pltpu.VMEM((len(sets), 4 * part, 2 * rows), BF16)],
    )


def row_call(kernel, rows, where, ins, outs, sums, name):
    tile = min(256, rows)
    steps = rows // tile
    specs, arrays = [], []
    for item in ins:
        array, scalar = item if isinstance(item, tuple) else (item, None)
        if scalar is not None:
            specs.append(pl.BlockSpec((tile, D), (lambda s: lambda i, w: (w[s] * steps + i, 0))(scalar)))
        elif array.shape[0] == 1:
            specs.append(pl.BlockSpec((1, D), lambda i, w: (0, 0)))
        else:
            specs.append(pl.BlockSpec((tile, D), lambda i, w: (i, 0)))
        arrays.append(array)
    out_specs = [pl.BlockSpec((tile, width), lambda i, w: (i, 0)) for _, width in outs]
    out_shape = [of((rows, width), dtype) for dtype, width in outs]
    return launch(
        kernel,
        arrays,
        specs,
        name,
        [where],
        grid=(steps,),
        out_specs=out_specs + [pl.BlockSpec((8, D), lambda i, w: (0, 0))] * sums,
        out_shape=out_shape + [of((8, D), F32)] * sums,
    )


def add_refs(*refs):
    total = refs[0][...].astype(F32)
    for ref in refs[1:]:
        total += ref[...].astype(F32)
    return total


def split_features(where_ref, total, mine_ref, other_ref):
    first = where_ref[CORE] == 0
    low, high = total[:, : D // 2], total[:, D // 2 :]
    mine_ref[...] = jnp.where(first, low, high).astype(mine_ref.dtype)
    other_ref[...] = jnp.where(first, high, low).astype(other_ref.dtype)


def norm_kernel(where_ref, one_ref, two_ref, far_ref, x_ref, gain_ref, residual_ref, normed_ref):
    residual = add_refs(x_ref, one_ref, two_ref, far_ref)
    scale = lax.rsqrt(jnp.sum(residual * residual, axis=1, keepdims=True) / D + EPS)
    residual_ref[...] = residual
    normed_ref[...] = (residual * scale * gain_ref[...]).astype(BF16)


def norm_back(stream, gain, upstream, sum_ref):
    scale = lax.rsqrt(jnp.sum(stream * stream, axis=1, keepdims=True) / D + EPS)
    weighted = upstream * gain
    inner = jnp.sum(weighted * stream, axis=1, keepdims=True)
    part = jnp.sum((upstream * stream * scale).reshape(-1, 8, D), axis=0)

    @pl.when(pl.program_id(0) == 0)
    def _():
        sum_ref[...] = jnp.zeros_like(sum_ref)

    sum_ref[...] += part
    return scale * weighted - stream * (scale * scale * scale) * (inner / D)


def ffn_back_kernel(where_ref, one_ref, two_ref, far_ref, residual_ref, cot_ref, gain_ref, grad_ref, low_ref, sum_ref):
    back = norm_back(residual_ref[...], gain_ref[...], add_refs(one_ref, two_ref, far_ref), sum_ref)
    grad = cot_ref[...].astype(F32) + back
    grad_ref[...] = grad
    low_ref[...] = grad.astype(BF16)


def input_back_kernel(where_ref, one_ref, two_ref, far_ref, x_ref, grad_ref, gain_ref, mine_ref, other_ref, sum_ref):
    back = norm_back(x_ref[...].astype(F32), gain_ref[...], add_refs(one_ref, two_ref, far_ref), sum_ref)
    split_features(where_ref, grad_ref[...] + back, mine_ref, other_ref)


def mixed_kernel(where_ref, *refs):
    split_features(where_ref, add_refs(*refs[:-2]), *refs[-2:])


def finish(pieces, spans, turned, where, name):
    shape = pieces[0].shape
    part = shape[1]
    sizes = [2 * sum(hi - lo for lo, hi in mine) for mine in spans]

    def kernel(where_ref, *refs):
        ins, outs = refs[:4], refs[4:]
        for k in range(4):

            @pl.when(pl.program_id(0) == k)
            def _():
                for out_ref, mine, flip in zip(outs, spans, turned):
                    at = 0
                    for core in range(2):
                        for lo, hi in mine:
                            block = ins[k][core, :, lo:hi]
                            if flip:
                                out_ref[at : at + hi - lo, :] = block.T.astype(F32)
                            else:
                                out_ref[:, at : at + hi - lo] = block.astype(F32)
                            at += hi - lo

    return launch(
        kernel,
        pieces,
        [pl.BlockSpec(shape, lambda k, w: (0, 0, 0), pipeline_mode=ONCE)] * 4,
        name,
        [where],
        grid=(4,),
        out_specs=[
            pl.BlockSpec((n, part), lambda k, w: (0, w[QUARTER + k]))
            if flip
            else pl.BlockSpec((part, n), lambda k, w: (w[QUARTER + k], 0))
            for n, flip in zip(sizes, turned)
        ],
        out_shape=[of((n, 4 * part) if flip else (4 * part, n), F32) for n, flip in zip(sizes, turned)],
    )


def swap_axis(values, axis, distance):
    size = lax.axis_size(axis)
    return lax.ppermute(values, axis, [(i, i ^ distance) for i in range(size)])


def other_core(values):
    return swap_axis(values, "row", 1)


def other_chip(values):
    return swap_axis(values, "col", 1)


def far_plane(values):
    return swap_axis(values, "col", 2)


def hop(values, step):
    pairs = []
    for spot in range(4):
        for core in range(2):
            distance = 1 if (step == 1) == (core == 0) else 2
            pairs.append((spot * 2 + core, (spot ^ distance) * 2 + core))
    return lax.ppermute(values, ("dp", "row"), pairs)


def hop_one(values):
    return hop(values, 1)


def hop_two(values):
    return hop(values, 2)


def add32(*values):
    total = values[0].astype(F32)
    for value in values[1:]:
        total += value.astype(F32)
    return total


class Plan:
    def __init__(self, direct, blocks):
        self.blocks = blocks
        self.core = lax.axis_index("row")
        if direct:
            spot = lax.axis_index("dp")
            quarters = [spot ^ jnp.where(self.core == 0, k, (0, 2, 1, 3)[k]) for k in range(4)]
        else:
            quarters = [jnp.int32(k) for k in range(4)]
        self.where = jnp.stack([self.core, 1 - self.core] + quarters).astype(jnp.int32)
        self.line = Line()

    def run(self, call, *values):
        return self.line.run(call, *values)

    def mix(self, call, *values):
        return self.line.mix(call, *values)

    def send(self, move, value):
        return self.line.send(move, value)

    def ship(self, move, value):
        return self.line.ship(move, value)

    def post(self, move, value):
        return self.line.post(move, value)

    def pause(self):
        self.run(short_kernel, self.line.stamp)

    def swap(self, value):
        return self.line.swap(value)

    def place(self, sources, outs, phases, name, kept=0):
        return self.run(lambda first, *rest: place([first, *rest], outs, phases, self.where, name, kept), *sources)

    def by_core(self, low, high):
        return jnp.where(self.core == 0, low, high), jnp.where(self.core == 0, high, low)


class Group:
    def __init__(self, name, plan, sets, kinds, near, far, spans, turned):
        self.name, self.plan, self.sets, self.kinds = name, plan, sets, kinds
        self.near, self.far, self.spans, self.turned = near, far, spans, turned
        self.block = sum(a.shape[1] for a in near) // plan.blocks

    def produce(self, scalars):
        plan, count = self.plan, len(self.near)
        return plan.run(
            lambda first, *rest: quarter_product(
                self.sets, self.kinds, (first,) + rest[: count - 1], rest[count - 1 :], plan.where, scalars, self.name
            ),
            *self.near, *self.far,
        )

    def make(self):
        self.sent = self.produce((QUARTER + 1, 2))

    def leave(self):
        self.came = self.plan.post(hop_one, self.sent)

    def stay(self):
        self.kept = self.produce((QUARTER, 2))

    def second(self):
        def add(kept, came):
            return add32(kept[1], came[1]).astype(BF16)

        self.back = self.plan.post(hop_two, self.plan.mix(add, self.kept, self.came))

    def cross_plane(self):
        n = self.block

        def add(kept, came, back):
            return add32(kept[0, :, n:], came[0, :, n:], back[:, n:]).astype(BF16)

        self.arrived = self.plan.post(far_plane, self.plan.mix(add, self.kept, self.came, self.back))

    def total(self):
        n = self.block

        def add(arrived, kept, came, back):
            return add32(kept[0, :, :n], came[0, :, :n], back[:, :n], arrived).astype(BF16)

        whole = self.plan.swap(self.plan.mix(add, self.arrived, self.kept, self.came, self.back))
        self.both = whole.reshape(2, -1, n)

    def spread(self):
        self.one = self.plan.ship(hop_one, self.both)

    def spread_last(self):
        self.two = self.plan.send(hop_two, self.both)
        self.three = self.plan.send(hop_two, self.one)

    def finish(self):
        return self.plan.run(
            lambda first, *rest: finish((first,) + rest, self.spans, self.turned, self.plan.where, "finish"),
            self.both, self.one, self.two, self.three,
        )

    def whole(self, groups):
        plan = self.plan
        pieces = []
        for k in range(2):
            made = self.produce((QUARTER + 2 * k, 1))
            for one in made:
                total = jnp.stack(jnp.split(one.astype(F32), plan.blocks, axis=1))
                total = lax.psum_scatter(total, "col", scatter_dimension=0, axis_index_groups=groups)
                total = lax.psum(total, "dp").astype(BF16)
                pieces.append(plan.swap(total).reshape(2, -1, total.shape[1]))
        return finish(pieces, self.spans, self.turned, plan.where, "finish")


class Sizes:
    def __init__(self, tokens, w_query, w_gate):
        self.rows = tokens.shape[0]
        self.half = self.rows // 2
        self.width = w_query.shape[1] // 2
        self.units = w_gate.shape[1] // 2
        self.tile = min(UNIT_TILE, self.units)
        self.split = D // 2


def interleaved(s):
    return [(p, lo) for lo in range(0, s.units, s.tile) for p in range(2)]


def gu_spans(s):
    return [[(lo + p * s.tile, lo + (p + 1) * s.tile) for lo in range(0, 2 * s.units, 2 * s.tile)] for p in range(2)]


def columns(lo, size):
    return lambda w: (slice(None), pl.ds(lo, size))


def join_features(plan, s, mine, theirs):
    return plan.place(
        [mine, theirs], [of((s.rows, D))],
        [[(0, full, 0, cols_at(CORE, s.split)), (1, full, 0, cols_at(OTHER, s.split))]], "join",
    )[0]


def join_rows(plan, s, mine, theirs):
    return plan.place(
        [mine, theirs], [of((s.rows, D))], [[(0, full, 0, rows_at(CORE, s.half)), (1, full, 0, rows_at(OTHER, s.half))]], "join"
    )[0]


def pack_in(plan, s, weights, parts, name):
    total = sum(size for _, _, size, _ in parts)
    moves, at = [], 0
    for i, lo, size, step in parts:
        moves.append((i, cols_at(OTHER, step, lo, size), 0, columns(at, size)))
        at += size
    return plan.place(weights, [of((s.split, total))], [moves], name)[0]


def own_in(plan, s, weights, got, parts):
    total = got.shape[1]
    moves, at = [], 0
    for i, lo, size, step in parts:
        moves.append((i, cols_at(CORE, step, lo, size), 0, block_at(CORE, s.split, at, size)))
        at += size
    moves.append((len(weights), full, 0, rows_at(OTHER, s.split)))
    return plan.place([*weights, got], [of((D, total))], [moves], "own")[0]


def own_out(plan, s, weight, got):
    rows = got.shape[0]
    return plan.place(
        [weight, got], [of((rows, D))], [[(0, rows_at(CORE, rows), 0, cols_at(CORE, s.split)), (1, full, 0, cols_at(OTHER, s.split))]],
        "own",
    )[0]


def both_gains(plan, mine, other):
    joined = plan.mix(lambda a, b: jnp.concatenate(plan.by_core(a, b), axis=1), mine, other)
    return joined[:1], joined[1:]


def norm_first(plan, s, near, far, x_near, gains):
    return plan.run(
        lambda *a: row_call(
            norm_kernel, s.half, plan.where, [*a[:3], (a[3], CORE), a[4]], [(F32, D), (BF16, D)], 0, "norm"
        ),
        *near, far, x_near, gains,
    )


def norm_ffn_back(plan, s, near, far, residual, cot_near, gains):
    return plan.run(
        lambda *a: row_call(
            ffn_back_kernel, s.half, plan.where, [*a[:4], (a[4], CORE), a[5]], [(F32, D), (BF16, D)], 1, "ffn_back"
        ),
        *near, far, residual, cot_near, gains,
    )


def norm_input_back(plan, s, near, far, x_near, grad_residual, gains):
    return plan.run(
        lambda *a: row_call(
            input_back_kernel, s.half, plan.where, [*a[:3], (a[3], CORE), *a[4:]],
            [(F32, D // 2), (F32, D // 2)], 1, "input_back",
        ),
        *near, far, x_near, grad_residual, gains,
    )


def add_mixed(plan, s, near, *others):
    return plan.run(
        lambda *a: row_call(mixed_kernel, s.half, plan.where, list(a), [(BF16, D // 2), (BF16, D // 2)], 0, "mixed"),
        *near, *others,
    )


def core_sum(plan, lhs, weights, turned, name):
    count = len(lhs)
    other, mine = plan.run(lambda *a: product(a[:count], a[count:], plan.where, turned, name), *lhs, *weights)
    return mine, plan.ship(other_core, other)


def add_pair(plan, pair):
    return plan.mix(lambda a, b: add32(a, b).astype(BF16), pair[1], pair[0])


def side_by_side(plan, s, mine, got):
    width = mine.shape[1]
    return plan.place(
        [mine, got], [of((s.rows, width), mine.dtype)],
        [[(0, full, 0, rows_at(CORE, s.half)), (1, full, 0, rows_at(OTHER, s.half))]], "sides",
    )[0]


def grad_attended(plan, gr, weight):
    return plan.run(lambda a: product([a], [weight], turned=True, name="grad_att"), gr)


def square(tokens, gain_attn, gain_ffn, w_query, w_key, w_value, w_out, w_gate, w_up, w_down, cotangent):
    plan = Plan(True, 2)
    s = Sizes(tokens, w_query, w_gate)
    run, mix, send, ship, post, where = plan.run, plan.mix, plan.send, plan.ship, plan.post, plan.where
    cos, sin = rope_tables()
    cos_rows, sin_rows = jnp.tile(cos, (s.rows // SEQ_LEN, 1)), jnp.tile(sin, (s.rows // SEQ_LEN, 1))
    qkv_parts = [(p, 0, s.width, s.width) for p in range(3)]
    gu_parts = [(p, lo, s.tile, s.units) for p, lo in interleaved(s)]
    eighth = D // 4 // 8

    far_tokens = other_chip(tokens)
    near_tokens = other_core(tokens)
    gains_mine = jnp.stack((gain_attn, gain_ffn))
    gains_other = other_core(gains_mine)
    plan.line.stamp = gains_mine[:, :LANES]
    got_qkv = ship(other_core, pack_in(plan, s, [w_query, w_key, w_value], qkv_parts, "pack"))
    pack_out = plan.place([w_out], [of((s.width, s.split))], [[(0, rows_at(OTHER, s.width), 0, full)]], "pack")[0]
    got_out = ship(other_core, pack_out)
    own_qkv = own_in(plan, s, [w_query, w_key, w_value], got_qkv, qkv_parts)
    own_o = own_out(plan, s, w_out, got_out)
    quarter, out_rows = D // 4, s.width // 4
    slots = quarter // out_rows
    out_cols = D // slots
    qkvo = plan.place(
        [own_qkv, own_o], [of((quarter, 3 * s.width + out_cols))],
        [
            [(0, rows_at(QUARTER, quarter), 0, columns(0, 3 * s.width))]
            + [
                (
                    1, (lambda j: lambda w: (pl.ds(pl.multiple_of(w[QUARTER] * out_rows, out_rows), out_rows), pl.ds(j * out_cols, out_cols)))(j),
                    0, (lambda j: lambda w: (pl.ds(j * out_rows, out_rows), pl.ds(3 * s.width, out_cols)))(j),
                )
                for j in range(slots)
            ]
        ],
        "quarter",
    )[0]
    qkvo_zero = ship(far_plane, qkvo)
    gains_attn, gains_ffn = both_gains(plan, gains_mine, gains_other)
    got_gu = ship(other_core, pack_in(plan, s, [w_gate, w_up], gu_parts, "pack"))
    pack_down = plan.place([w_down], [of((s.units, s.split))], [[(0, rows_at(OTHER, s.units), 0, full)]], "pack")[0]
    got_down = ship(other_core, pack_down)
    x_near = join_features(plan, s, tokens, near_tokens)
    own_gu = own_in(plan, s, [w_gate, w_up], got_gu, gu_parts)
    own_d = own_out(plan, s, w_down, got_down)
    down_rows = s.units // 4
    mixed_rows = quarter // 2 + down_rows // 2
    gud = [
        plan.place(
            [own_gu, own_d], [of((mixed_rows, D))],
            [[
                (0, (lambda i: rows_span(QUARTER, quarter, i * (quarter // 2), quarter // 2))(i), 0, rows_fixed(0, quarter // 2)),
                (1, (lambda i: rows_span(QUARTER, down_rows, i * (down_rows // 2), down_rows // 2))(i), 0, rows_fixed(quarter // 2, down_rows // 2)),
            ]],
            "quarter",
        )[0]
        for i in range(2)
    ]
    gud_zero = [None, None]

    def project(x, weight, first):
        return run(lambda a: project_qkv(a, gains_attn, cos_rows, sin_rows, weight, first), x)

    normed_near, *near_own = project(x_near, own_qkv, True)
    far_half = send(other_core, far_tokens)
    o_near_own = run(attend, *near_own)
    qkvo_one, qkvo_two = send(hop_one, qkvo_zero), send(hop_two, qkvo_zero)
    gud_zero[0] = send(far_plane, gud[0])
    far_cot = send(other_chip, cotangent)
    x_far = join_features(plan, s, far_tokens, far_half)
    normed_far, *far_own = project(x_far, own_qkv, True)
    qkvo_three = send(hop_two, qkvo_one)
    o_far_own = run(attend, *far_own)
    pieces = [qkvo_zero, qkvo_one, qkvo_two, qkvo_three]
    for_qkv, for_o = plan.place(
        pieces, [of((D, 3 * s.width)), of((s.width, D))],
        [
            [(k, columns(0, 3 * s.width), 0, rows_at(QUARTER + k, quarter)) for k in range(4)]
            + [
                (
                    k, (lambda j: lambda w: (pl.ds(j * out_rows, out_rows), pl.ds(3 * s.width, out_cols)))(j),
                    1, (lambda k, j: lambda w: (pl.ds(pl.multiple_of(w[QUARTER + k] * out_rows, out_rows), out_rows), pl.ds(j * out_cols, out_cols)))(k, j),
                )
                for k in range(4)
                for j in range(slots)
            ]
        ],
        "other",
    )
    w_qkv, w_o = [own_qkv, for_qkv], [own_o, for_o]

    far_for = project(normed_far, for_qkv, False)
    gud_one, gud_two, gud_three = [None, None], [None, None], [None, None]
    o_far = [o_far_own, run(attend, *far_for)]
    far = core_sum(plan, [o[0] for o in o_far], w_o, False, "out")
    near_for = project(normed_near, for_qkv, False)
    far = post(other_chip, add_pair(plan, far))
    gud_one[0], gud_two[0] = send(hop_one, gud_zero[0]), send(hop_two, gud_zero[0])
    gud_zero[1] = send(far_plane, gud[1])
    near_cot = send(other_core, cotangent)
    o_near = [o_near_own, run(attend, *near_for)]
    near = core_sum(plan, [o[0] for o in o_near], w_o, False, "out")
    gud_three[0] = send(hop_two, gud_one[0])
    cot_near = join_features(plan, s, cotangent, near_cot)
    cot_far_row = send(other_core, far_cot)
    plan.pause()
    cot_far = join_features(plan, s, far_cot, cot_far_row)
    def spread_out(i, outs):
        count = quarter // 2, down_rows // 2
        return plan.place(
            [g[i] for g in (gud_zero, gud_one, gud_two, gud_three)] + outs, [of(own_gu.shape), of(own_d.shape)],
            [
                [(k, rows_fixed(0, count[0]), 0, rows_span(QUARTER + k, quarter, i * count[0], count[0])) for k in range(4)]
                + [(k, rows_fixed(count[0], count[1]), 1, rows_span(QUARTER + k, down_rows, i * count[1], count[1])) for k in range(4)]
            ],
            "other", len(outs),
        )

    halves = spread_out(0, [])
    residual, normed_ffn = norm_first(plan, s, near, far, x_near, gains_ffn)
    nf_row = ship(other_core, normed_ffn)
    nf_chip = post(other_chip, normed_ffn)
    gud_one[1], gud_two[1] = send(hop_one, gud_zero[1]), send(hop_two, gud_zero[1])
    nf_near = join_rows(plan, s, normed_ffn, nf_row)
    fed_near = [run(ffn, nf_near, cot_near, own_gu, own_d)]
    nf_far_row = send(other_core, nf_chip)
    gud_three[1] = send(hop_two, gud_one[1])
    plan.pause()
    nf_far = join_rows(plan, s, nf_chip, nf_far_row)
    fed_far = [run(ffn, nf_far, cot_far, own_gu, own_d)]
    for_gu, for_d = spread_out(1, list(halves))
    w_gu, w_d = [own_gu, for_gu], [own_d, for_d]
    fed_far.append(run(ffn, nf_far, cot_far, for_gu, for_d))
    fed_near.append(run(ffn, nf_near, cot_near, for_gu, for_d))
    hid_near, ggu_near = [f[0] for f in fed_near], [f[1] for f in fed_near]
    hid_far, ggu_far = [f[0] for f in fed_far], [f[1] for f in fed_far]

    ups = Group("gu_grad", plan, [(nf_near, nf_far)], [0, 0], ggu_near, ggu_far, gu_spans(s), [False, False])
    down = Group("down_grad", plan, [(cot_near, cot_far)], [0, 0], hid_near, hid_far, [[(0, s.units)]], [True])
    ups.make()
    ups.leave()
    far = core_sum(plan, ggu_far, w_gu, True, "ffn_in")
    plan.pause()
    far = post(other_chip, add_pair(plan, far))
    near = core_sum(plan, ggu_near, w_gu, True, "ffn_in")
    ups.stay()
    grad_residual, grad_low, gain_ffn_part = norm_ffn_back(plan, s, near, far, residual, cot_near, gains_ffn)
    gr_row = ship(other_core, grad_low)
    gr_chip = post(other_chip, grad_low)
    gr_near = join_rows(plan, s, grad_low, gr_row)
    ups.second()

    def back_one(gr, heads, outs, b):
        return run(attend_back, grad_attended(plan, gr, w_o[b]), *heads[b], *outs[b], cos, sin)

    near_heads, far_heads = [near_own, near_for], [far_own, far_for]
    back_near = [back_one(gr_near, near_heads, o_near, b) for b in range(2)]
    gr_far_row = send(other_core, gr_chip)
    down.make()
    ups.cross_plane()
    down.leave()
    down.stay()
    gr_far = join_rows(plan, s, gr_chip, gr_far_row)
    back_far = [back_one(gr_far, far_heads, o_far, b) for b in range(2)]
    down.second()
    dqkv_far = [jnp.concatenate(b, axis=1) for b in back_far]
    far = core_sum(plan, dqkv_far, w_qkv, True, "qkv_in")
    heads = Group(
        "head_grad", plan, [(normed_near, normed_far), (gr_near, gr_far)], [0, 0, 0, 1] * 2,
        [a for b in range(2) for a in (*back_near[b], o_near[b][0])],
        [a for b in range(2) for a in (*back_far[b], o_far[b][0])],
        [[(p * s.width, (p + 1) * s.width)] for p in range(4)], [False, False, False, True],
    )
    heads.make()
    heads.leave()
    far = post(other_chip, add_pair(plan, far))
    dqkv_near = [jnp.concatenate(b, axis=1) for b in back_near]
    near = core_sum(plan, dqkv_near, w_qkv, True, "qkv_in")
    down.cross_plane()
    heads.stay()
    heads.second()
    mixed_far = core_sum(plan, hid_far, w_d, False, "down")
    ups.total()
    input_mine, input_other, gain_attn_part = norm_input_back(plan, s, near, far, x_near, grad_residual, gains_attn)
    input_got = ship(other_core, input_other)
    gains = mix(lambda a, b: jnp.stack((jnp.sum(a, axis=0), jnp.sum(b, axis=0))), gain_attn_part, gain_ffn_part)
    gains_got = ship(other_core, gains)
    heads.cross_plane()
    mixed_far = post(other_chip, add_pair(plan, mixed_far))
    ups.spread()
    input_grad = side_by_side(plan, s, input_mine, input_got)
    gains = mix(jnp.add, gains, gains_got)
    gains_got = ship(hop_one, gains)
    ups.spread_last()
    mixed_near = core_sum(plan, hid_near, w_d, False, "down")
    gains = mix(jnp.add, gains, gains_got)
    down.total()
    down.spread()
    gains_got = ship(hop_two, gains)
    plan.pause()
    mixed_near = [add_pair(plan, mixed_near)]
    gains = mix(jnp.add, gains, gains_got)
    gains_got = ship(other_chip, gains)
    plan.pause()
    heads.total()
    heads.spread()
    down.spread_last()
    gains = mix(jnp.add, gains, gains_got)
    gains_got = ship(far_plane, gains)
    gate_grad, up_grad = ups.finish()
    mixed_mine, mixed_other = add_mixed(plan, s, mixed_near, mixed_far, residual)
    mixed_got = ship(other_core, mixed_other)
    heads.spread_last()
    (down_grad,) = down.finish()
    mixed = side_by_side(plan, s, mixed_mine, mixed_got)
    gains = mix(jnp.add, gains, gains_got)
    gains = jnp.where(plan.core == 0, gains[:, : s.split], gains[:, s.split :])
    q_grad, k_grad, v_grad, out_grad = heads.finish()
    return mixed, input_grad, gains[0], gains[1], q_grad, k_grad, v_grad, out_grad, gate_grad, up_grad, down_grad


def pair_order(near, far):
    member = lax.axis_index("col") % 2
    return jnp.concatenate((jnp.where(member == 0, near, far), jnp.where(member == 0, far, near)), axis=0)


def from_pair(joined):
    member = lax.axis_index("col") % 2
    first, second = jnp.split(joined, 2, axis=0)
    return jnp.where(member == 0, first, second), jnp.where(member == 0, second, first)


def general(tokens, gain_attn, gain_ffn, w_query, w_key, w_value, w_out, w_gate, w_up, w_down, cotangent):
    blocks = lax.axis_size("col") // 2
    groups = [[i for i in range(2 * blocks) if i % 2 == m] for m in range(2)]
    plan = Plan(False, blocks)
    s = Sizes(tokens, w_query, w_gate)
    run, where = plan.run, plan.where
    cos, sin = rope_tables()
    shared = s.rows % SEQ_LEN != 0
    qkv_parts = [(p, 0, s.width, s.width) for p in range(3)]
    gu_parts = [(p, lo, s.tile, s.units) for p, lo in interleaved(s)]

    def gathered(own):
        every = lax.all_gather(own, "col", axis=0, axis_index_groups=groups)
        return [every[b] for b in range(blocks)]

    def pack_rows(weight, rows):
        return plan.place([weight], [of((rows, s.split))], [[(0, rows_at(OTHER, rows), 0, full)]], "pack")[0]

    got = other_core(pack_in(plan, s, [w_query, w_key, w_value], qkv_parts, "pack"))
    w_qkv = gathered(own_in(plan, s, [w_query, w_key, w_value], got, qkv_parts))
    got = other_core(pack_in(plan, s, [w_gate, w_up], gu_parts, "pack"))
    w_gu = gathered(own_in(plan, s, [w_gate, w_up], got, gu_parts))
    w_o = gathered(own_out(plan, s, w_out, other_core(pack_rows(w_out, s.width))))
    w_d = gathered(own_out(plan, s, w_down, other_core(pack_rows(w_down, s.units))))
    gains_mine = jnp.stack((gain_attn, gain_ffn))
    gains_attn, gains_ffn = both_gains(plan, gains_mine, other_core(gains_mine))

    def both_chips(values):
        far = other_chip(values)
        return join_features(plan, s, values, other_core(values)), join_features(plan, s, far, other_core(far))

    x_near, x_far = both_chips(tokens)
    cot_near, cot_far = both_chips(cotangent)

    def tables(offset):
        if shared:
            return [lax.dynamic_slice_in_dim(t, offset, s.rows) for t in (cos, sin)]
        return [jnp.tile(t, (s.rows // SEQ_LEN, 1)) for t in (cos, sin)]

    first = (lax.axis_index("col") % 2) * s.rows
    chips = []
    for x, offset in ((x_near, first), (x_far, s.rows - first)):
        turn = tables(offset)
        normed, *heads = run(lambda a: project_qkv(a, gains_attn, *turn, w_qkv[0], True), x)
        every = [heads]
        for w in w_qkv[1:]:
            every.append(run(lambda a: project_qkv(a, gains_attn, *turn, w, False), normed))
        chips.append((normed, every))
    (normed_near, heads_near), (normed_far, heads_far) = chips

    def together(near, far):
        return pair_order(near, far) if shared else jnp.concatenate((near, far), axis=0)

    def apart(joined):
        return from_pair(joined) if shared else jnp.split(joined, 2, axis=0)

    joined_heads = [[together(a, b) for a, b in zip(n, f)] for n, f in zip(heads_near, heads_far)]
    outs = [run(attend, *h) for h in joined_heads]
    att = [apart(o[0]) for o in outs]
    att_near, att_far = [a[0] for a in att], [a[1] for a in att]

    def four_core_sum(near, far, weights, turned, name):
        far = other_chip(add_pair(plan, core_sum(plan, far, weights, turned, name)))
        return core_sum(plan, near, weights, turned, name), far

    def gather_tokens(values):
        far = other_chip(values)
        return join_rows(plan, s, values, other_core(values)), join_rows(plan, s, far, other_core(far))

    residual, normed_ffn = norm_first(plan, s, *four_core_sum(att_near, att_far, w_o, False, "out"), x_near, gains_ffn)
    nf_near, nf_far = gather_tokens(normed_ffn)
    fed_near = [run(ffn, nf_near, cot_near, w_gu[b], w_d[b]) for b in range(blocks)]
    fed_far = [run(ffn, nf_far, cot_far, w_gu[b], w_d[b]) for b in range(blocks)]
    hid_near, ggu_near = [f[0] for f in fed_near], [f[1] for f in fed_near]
    hid_far, ggu_far = [f[0] for f in fed_far], [f[1] for f in fed_far]
    kinds = [0] * blocks
    ups = Group("gu_grad", plan, [(nf_near, nf_far)], kinds, ggu_near, ggu_far, gu_spans(s), [False, False])
    down = Group("down_grad", plan, [(cot_near, cot_far)], kinds, hid_near, hid_far, [[(0, s.units)]], [True])
    grad_residual, grad_low, gain_ffn_part = norm_ffn_back(
        plan, s, *four_core_sum(ggu_near, ggu_far, w_gu, True, "ffn_in"), residual, cot_near, gains_ffn
    )
    gr_near, gr_far = gather_tokens(grad_low)
    gr = together(gr_near, gr_far)
    backs = []
    for b in range(blocks):
        grads = run(attend_back, grad_attended(plan, gr, w_o[b]), *joined_heads[b], *outs[b], cos, sin)
        backs.append([apart(g) for g in grads])
    back_near = [[g[0] for g in b] for b in backs]
    back_far = [[g[1] for g in b] for b in backs]
    heads = Group(
        "head_grad", plan, [(normed_near, normed_far), (gr_near, gr_far)], [0, 0, 0, 1] * blocks,
        [a for b in range(blocks) for a in (*back_near[b], att_near[b])],
        [a for b in range(blocks) for a in (*back_far[b], att_far[b])],
        [[(p * s.width, (p + 1) * s.width)] for p in range(4)], [False, False, False, True],
    )
    dqkv_near = [jnp.concatenate(b, axis=1) for b in back_near]
    dqkv_far = [jnp.concatenate(b, axis=1) for b in back_far]
    input_mine, input_other, gain_attn_part = norm_input_back(
        plan, s, *four_core_sum(dqkv_near, dqkv_far, w_qkv, True, "qkv_in"), x_near, grad_residual, gains_attn
    )
    mixed_mine, mixed_other = add_mixed(plan, s, *four_core_sum(hid_near, hid_far, w_d, False, "down"), residual)
    gains = lax.psum(jnp.stack((jnp.sum(gain_attn_part, axis=0), jnp.sum(gain_ffn_part, axis=0))), ("dp", "col", "row"))
    gains = jnp.where(plan.core == 0, gains[:, : s.split], gains[:, s.split :])
    mixed = side_by_side(plan, s, mixed_mine, other_core(mixed_other))
    input_grad = side_by_side(plan, s, input_mine, other_core(input_other))
    q_grad, k_grad, v_grad, out_grad = heads.whole(groups)
    gate_grad, up_grad = ups.whole(groups)
    (down_grad,) = down.whole(groups)
    return mixed, input_grad, gains[0], gains[1], q_grad, k_grad, v_grad, out_grad, gate_grad, up_grad, down_grad


def solution(mesh):
    stream = P(("dp", "col"), "row")
    gain = P("row")
    inward, outward = P("row", "col"), P("col", "row")
    weights = (inward, inward, inward, outward, inward, inward, outward)
    fits = mesh.shape["dp"] == 4 and mesh.shape["col"] == 4
    return jax.shard_map(
        lambda *args: square(*args) if fits and args[0].shape[0] % SEQ_LEN == 0 else general(*args),
        mesh=mesh,
        in_specs=(stream, gain, gain, *weights, stream),
        out_specs=(stream, stream, gain, gain, *weights),
        check_vma=False,
    )
```

```python
import jax
import jax.numpy as jnp
from jax import lax
from jax.experimental import pallas as pl
from jax.experimental.pallas import tpu as pltpu
from jax.sharding import PartitionSpec as P

D = 2048
HEAD_DIM = 64
SEQ_LEN = 1024
LANES = 128
EPS = 1e-05
ROPE_BASE = 130000.0
VMEM = 40 * 1024 * 1024
UNIT_TILE = 256
QB = 256
COST = 10**12
F32 = jnp.float32
BF16 = jnp.bfloat16


def dot(a, b, ca, cb):
    return lax.dot_general(a, b, (((ca,), (cb,)), ((), ())), preferred_element_type=F32)


def of(shape, dtype=BF16):
    return jax.ShapeDtypeStruct(tuple(shape), dtype)


class Line:
    waiting = []
    mark = None

    def __init__(self):
        self.last = []

    def run(self, call, *values):
        Line.waiting = list(self.last)
        result = call(*values)
        self.last = [Line.mark]
        return result

    def tied(self, value):
        if not self.last:
            return value
        value, *self.last = lax.optimization_barrier((value, *self.last))
        return value

    def mix(self, call, first, *values):
        return self.tied(call(self.tied(first), *values))

    def send(self, move, value):
        return move(self.tied(value))

    def ship(self, move, value):
        return move(value)

    def post(self, move, value):
        sent = move(value)
        mark = other_core(self.tied(self.stamp))
        self.run(short_kernel, self.stamp)
        self.last = self.last + [mark]
        return sent

    def swap(self, value):
        return self.tied(lax.all_to_all(self.tied(value), "row", split_axis=0, concat_axis=0, tiled=True))


ONCE = pl.Buffered(1)


def launch(kernel, arrays, in_specs, name, prefetch=(), **rest):
    held, Line.waiting = Line.waiting, []
    skip, count = len(held), len(prefetch) + len(arrays)
    out_shape, out_specs = rest.pop("out_shape"), rest.pop("out_specs")
    single = not isinstance(out_shape, (list, tuple))
    out_shape, out_specs = ([out_shape], [out_specs]) if single else (list(out_shape), list(out_specs))
    outs = count + skip + len(out_shape)

    def body(*refs):
        kernel(*refs[:count], *refs[count + skip : outs], *refs[outs + 1 :])

    in_specs = list(in_specs) + [pl.BlockSpec(memory_space=pl.ANY)] * skip
    out_specs = out_specs + [pl.BlockSpec(memory_space=pl.ANY)]
    if prefetch:
        layout = dict(
            grid_spec=pltpu.PrefetchScalarGridSpec(
                num_scalar_prefetch=len(prefetch), in_specs=in_specs, out_specs=out_specs, **rest
            )
        )
    else:
        layout = dict(in_specs=in_specs, out_specs=out_specs, **rest)
    *results, Line.mark = pl.pallas_call(
        body,
        out_shape=out_shape + [of((8, LANES), F32)],
        compiler_params=pltpu.CompilerParams(vmem_limit_bytes=VMEM),
        cost_estimate=pl.CostEstimate(flops=COST, bytes_accessed=1, transcendentals=0),
        name=name,
        **layout,
    )(*prefetch, *arrays, *held)
    return results[0] if single else results


def short_kernel(values):
    def kernel(in_ref, out_ref):
        out_ref[0, 0] = 0.0

    return launch(
        kernel, [values], [pl.BlockSpec(memory_space=pl.ANY)], "short",
        out_specs=pl.BlockSpec(memory_space=pltpu.SMEM), out_shape=of((1, 1), F32),
    )


def extent(shape, index):
    sizes = []
    for size, at in zip(shape, index):
        if not isinstance(at, int):
            sizes.append(size if isinstance(at, slice) else at.size)
    return tuple(sizes)


def place(sources, outs, phases, where, name, kept=0, fixed=0):
    moves = [m for phase in phases for m in phase]
    shapes = [extent((sources[src] if src >= 0 else outs[-1 - src]).shape, src_at([0] * 8)) for src, src_at, _, _ in moves]
    count = len(sources)

    def kernel(where_ref, *refs):
        ins, out_refs, held = refs[:count], refs[count : count + len(outs)], refs[count + len(outs) : -2]
        in_sems, out_sems = refs[-2:]
        base = 0
        for phase in phases:
            loads, stores = [], []
            for n, (src, src_at, dst, dst_at) in enumerate(phase, base):
                src_ref = out_refs[-1 - src] if src < 0 else ins[src]
                loads.append(pltpu.make_async_copy(src_ref.at[src_at(where_ref)], held[n], in_sems.at[n]))
                stores.append(pltpu.make_async_copy(held[n], out_refs[dst].at[dst_at(where_ref)], out_sems.at[n]))
            for load in loads:
                load.start()
            for load, store in zip(loads, stores):
                load.wait()
                store.start()
            for store in stores:
                store.wait()
            base += len(phase)

    sources = [pltpu.with_memory_space_constraint(a, pltpu.HBM) for a in sources[:fixed]] + list(sources[fixed:])
    return launch(
        kernel,
        [where, *sources],
        [pl.BlockSpec(memory_space=pltpu.SMEM)]
        + [pl.BlockSpec(memory_space=pltpu.HBM)] * fixed
        + [pl.BlockSpec(memory_space=pl.ANY)] * (count - fixed),
        name,
        out_specs=[pl.BlockSpec(memory_space=pl.ANY)] * len(outs),
        out_shape=list(outs),
        scratch_shapes=[pltpu.VMEM(s, outs[m[2]].dtype) for s, m in zip(shapes, moves)] + [pltpu.SemaphoreType.DMA((len(moves),))] * 2,
        input_output_aliases={1 + count - kept + i: i for i in range(kept)},
    )


CORE, OTHER, QUARTER = 0, 1, 2


def full(_):
    return (slice(None), slice(None))


def rows_at(scalar, size, base=0):
    return lambda w: (pl.ds(pl.multiple_of(base + w[scalar] * size, size), size), slice(None))


def cols_at(scalar, size, lo=0, width=None):
    width = width or size
    return lambda w: (slice(None), pl.ds(pl.multiple_of(w[scalar] * size + lo, width), width))


def rows_span(scalar, size, lo, count):
    return lambda w: (pl.ds(pl.multiple_of(w[scalar] * size + lo, count), count), slice(None))


def rows_fixed(lo, count):
    return lambda w: (pl.ds(lo, count), slice(None))


def block_at(row_scalar, height, lo, width):
    return lambda w: (pl.ds(pl.multiple_of(w[row_scalar] * height, height), height), pl.ds(lo, width))


def rope_tables():
    half = HEAD_DIM // 2
    frequency = jnp.exp(-jnp.log(ROPE_BASE) * jnp.arange(half, dtype=F32) * (2.0 / HEAD_DIM))
    frequency = jnp.tile(frequency, 4)
    sign = jnp.where(jnp.arange(LANES) % HEAD_DIM < half, -1.0, 1.0)
    angles = jnp.arange(SEQ_LEN, dtype=F32)[:, None] * frequency[None, :]
    return jnp.cos(angles), jnp.sin(angles) * sign[None, :]


def swap_halves(values):
    half = HEAD_DIM // 2
    lane = lax.broadcasted_iota(jnp.int32, values.shape, 1)
    return jnp.where(lane % HEAD_DIM < half, pltpu.roll(values, LANES - half, 1), pltpu.roll(values, half, 1))


def qkv_kernel(first, x_ref, gain_ref, cos_ref, sin_ref, w_ref, *refs):
    q_ref, k_ref, v_ref = refs[-3:]
    if first:
        x = x_ref[...].astype(F32)
        scale = lax.rsqrt(jnp.sum(x * x, axis=1, keepdims=True) / D + EPS)
        refs[0][...] = (x * scale * gain_ref[...]).astype(BF16)
        normed = refs[0][...]
    else:
        normed = x_ref[...]
    cos, sin = cos_ref[...], sin_ref[...]
    width = q_ref.shape[1]
    projected = dot(normed, w_ref[...], 1, 0)
    for part, (out_ref, mult) in enumerate(((q_ref, HEAD_DIM**-0.5), (k_ref, 1.0))):
        for lo in range(0, width, LANES):
            piece = projected[:, part * width + lo : part * width + lo + LANES]
            out_ref[:, lo : lo + LANES] = ((piece * cos + swap_halves(piece) * sin).astype(BF16) * mult).astype(BF16)
    v_ref[...] = projected[:, 2 * width :].astype(BF16)


def project_qkv(x, gain, cos, sin, weight, first):
    rows, width = x.shape[0], weight.shape[1] // 3
    tile = min(512, rows)
    row_block = lambda n: pl.BlockSpec((tile, n), lambda i: (i, 0))
    whole = lambda a: pl.BlockSpec(a.shape, lambda i: (0, 0), pipeline_mode=ONCE)
    outs = [D] * first + [width] * 3
    return launch(
        lambda *refs: qkv_kernel(first, *refs),
        [x, gain, cos, sin, weight],
        [row_block(D), whole(gain), row_block(LANES), row_block(LANES), whole(weight)],
        "qkv",
        grid=(rows // tile,),
        out_specs=[row_block(n) for n in outs],
        out_shape=[of((rows, n)) for n in outs],
    )


def head_of(values, head):
    lane = lax.broadcasted_iota(jnp.int32, values.shape, 1)
    return jnp.where((lane >= HEAD_DIM) == (head == 1), values, jnp.zeros_like(values))


def causal_scores(keys, queries, start):
    scores = dot(keys, queries, 1, 1)
    last = scores[start:]
    key_at = lax.broadcasted_iota(jnp.int32, last.shape, 0)
    query_at = lax.broadcasted_iota(jnp.int32, last.shape, 1)
    last = jnp.where(key_at <= query_at, last, -1e30)
    return last if start == 0 else jnp.concatenate((scores[:start], last), axis=0)


def attend_kernel(q_ref, k_ref, v_ref, o_ref, lse_ref):
    values = [head_of(v_ref[...], head) for head in range(2)]
    for start in range(0, SEQ_LEN, QB):
        stop = start + QB
        queries = q_ref[start:stop, :]
        outs, scales = [], []
        for head in range(2):
            scores = causal_scores(k_ref[:stop, :], head_of(queries, head), start)
            top = jnp.max(scores, axis=0, keepdims=True)
            weights = jnp.exp(scores - top)
            total = jnp.sum(weights, axis=0, keepdims=True)
            lse_ref[0, 0, head : head + 1, start:stop] = top + jnp.log(total)
            outs.append(dot(weights.astype(BF16), values[head][:stop], 0, 0))
            scales.append(jnp.broadcast_to(1.0 / total, (HEAD_DIM, QB)))
        o_ref[start:stop, :] = ((outs[0] + outs[1]) * jnp.concatenate(scales, axis=0).T).astype(BF16)


def attend(q, k, v):
    rows, width = q.shape
    seqs, pairs = rows // SEQ_LEN, width // LANES
    block = pl.BlockSpec((SEQ_LEN, LANES), lambda s, h: (s, h))
    return launch(
        attend_kernel,
        [q, k, v],
        [block] * 3,
        "attend",
        grid=(seqs, pairs),
        out_specs=[block, pl.BlockSpec((1, 1, 8, SEQ_LEN), lambda s, h: (s, h, 0, 0))],
        out_shape=[of((rows, width)), of((seqs, pairs, 8, SEQ_LEN), F32)],
    )


def attend_back_kernel(do_ref, q_ref, k_ref, v_ref, o_ref, lse_ref, cos_ref, sin_ref, dq_ref, dk_ref, dv_ref, dk_acc, dv_acc):
    k_t = k_ref[...].T
    dk_acc[...] = jnp.zeros_like(dk_acc)
    dv_acc[...] = jnp.zeros_like(dv_acc)
    for start in range(0, SEQ_LEN, QB):
        stop = start + QB
        queries, grads = q_ref[start:stop, :], do_ref[start:stop, :]
        inner = (grads.astype(F32) * o_ref[start:stop, :].astype(F32)).T
        back = []
        for head in range(2):
            one_q, one_g = head_of(queries, head), head_of(grads, head)
            scores = causal_scores(k_ref[:stop, :], one_q, start)
            weights = jnp.exp(scores - lse_ref[0, 0, head : head + 1, start:stop])
            grad_weights = dot(v_ref[:stop, :], one_g, 1, 1)
            delta = jnp.sum(inner[head * HEAD_DIM : (head + 1) * HEAD_DIM], axis=0, keepdims=True)
            grad_scores = (weights * (grad_weights - delta)).astype(BF16)
            dv_acc[:stop, :] += dot(weights.astype(BF16), one_g, 1, 0)
            dk_acc[:stop, :] += dot(grad_scores, one_q, 1, 0)
            back.append(dot(k_t[head * HEAD_DIM : (head + 1) * HEAD_DIM, :stop], grad_scores, 1, 0))
        dq = jnp.concatenate(back, axis=0).T * HEAD_DIM**-0.5
        cos, sin = cos_ref[start:stop, :], sin_ref[start:stop, :]
        dq_ref[start:stop, :] = (dq * cos - swap_halves(dq) * sin).astype(BF16)
    dk = dk_acc[...]
    dk_ref[...] = (dk * cos_ref[...] - swap_halves(dk) * sin_ref[...]).astype(BF16)
    dv_ref[...] = dv_acc[...].astype(BF16)


def attend_back(do, q, k, v, o, lse, cos, sin):
    rows, width = q.shape
    seqs, pairs = rows // SEQ_LEN, width // LANES
    block = pl.BlockSpec((SEQ_LEN, LANES), lambda s, h: (s, h))
    table = pl.BlockSpec((SEQ_LEN, LANES), lambda s, h: (0, 0))
    return launch(
        attend_back_kernel,
        [do, q, k, v, o, lse, cos, sin],
        [block] * 5 + [pl.BlockSpec((1, 1, 8, SEQ_LEN), lambda s, h: (s, h, 0, 0)), table, table],
        "attend_back",
        grid=(seqs, pairs),
        out_specs=[block] * 3,
        out_shape=[of((rows, width))] * 3,
        scratch_shapes=[pltpu.VMEM((SEQ_LEN, LANES), F32)] * 2,
    )


def ffn_kernel(nf_ref, cot_ref, wgu_ref, wd_ref, hidden_ref, ggu_ref):
    tile = wd_ref.shape[0]
    chunk = 256
    for lo in range(0, nf_ref.shape[0], chunk):
        rows = slice(lo, lo + chunk)
        both = dot(nf_ref[rows, :], wgu_ref[...], 1, 0)
        grad_hidden = dot(cot_ref[rows, :], wd_ref[...], 1, 1)
        gate, up = both[:, :tile], both[:, tile:]
        sig = jax.nn.sigmoid(gate)
        act = gate * sig
        hidden_ref[rows, :] = (act * up).astype(BF16)
        ggu_ref[rows, :tile] = (grad_hidden * up * (sig * (1.0 + gate * (1.0 - sig)))).astype(BF16)
        ggu_ref[rows, tile:] = (grad_hidden * act).astype(BF16)


def ffn(nf, cot, w_gu, w_down):
    rows, units = nf.shape[0], w_down.shape[0]
    tile = min(UNIT_TILE, units)
    whole = pl.BlockSpec((rows, D), lambda j: (0, 0), pipeline_mode=ONCE)
    return launch(
        ffn_kernel,
        [nf, cot, w_gu, w_down],
        [
            whole,
            whole,
            pl.BlockSpec((D, 2 * tile), lambda j: (0, j)),
            pl.BlockSpec((tile, D), lambda j: (j, 0)),
        ],
        "ffn",
        grid=(units // tile,),
        out_specs=[pl.BlockSpec((rows, tile), lambda j: (0, j)), pl.BlockSpec((rows, 2 * tile), lambda j: (0, j))],
        out_shape=[of((rows, units)), of((rows, 2 * units))],
    )


def product(lhs, rhs, where=None, turned=False, name="product"):
    count = len(lhs)
    rows = lhs[0].shape[0]
    columns = rhs[0].shape[0 if turned else 1]
    wide = sum(a.shape[1] for a in lhs)
    tile = min(columns, 512 if wide > 1024 else 1024)
    parts = 1 if where is None else 2
    size = rows // parts

    def kernel(*refs):
        refs = refs[parts - 1 :]
        lhs_refs, rhs_refs, out_refs = refs[: parts * count], refs[parts * count : -parts], refs[-parts:]
        for i, out_ref in enumerate(out_refs):
            total = None
            for a, b in zip(lhs_refs[i * count : (i + 1) * count], rhs_refs):
                extra = dot(a[...], b[...], 1, 1 if turned else 0)
                total = extra if total is None else total + extra
            out_ref[...] = total.astype(BF16)

    if parts == 1:
        lhs_specs = [pl.BlockSpec((rows, a.shape[1]), lambda n, *w: (0, 0), pipeline_mode=ONCE) for a in lhs]
    else:
        lhs_specs = [
            pl.BlockSpec((size, a.shape[1]), (lambda s: lambda n, w: (w[s], 0))(s), pipeline_mode=ONCE)
            for s in (OTHER, CORE)
            for a in lhs
        ]
    if turned:
        rhs_specs = [pl.BlockSpec((tile, b.shape[1]), lambda n, *w: (n, 0)) for b in rhs]
    else:
        rhs_specs = [pl.BlockSpec((b.shape[0], tile), lambda n, *w: (0, n)) for b in rhs]
    result = launch(
        kernel,
        [*list(lhs) * parts, *rhs],
        lhs_specs + rhs_specs,
        name,
        [] if where is None else [where],
        grid=(columns // tile,),
        out_specs=[pl.BlockSpec((size, tile), lambda n, *w: (0, n))] * parts,
        out_shape=[of((size, columns))] * parts,
    )
    return result[0] if parts == 1 else result


def quarter_product(sets, kinds, near, far, where, scalars, name):
    rows = near[0].shape[0]
    part = D // 8
    width = near[0].shape[1]
    tile = min(width, 512)
    tiles = width // tile
    pieces = len(near)
    first, stride = scalars
    fixed_specs = [
        pl.BlockSpec((rows, part), (lambda k, h: lambda t, w: (0, 4 * h + w[first + stride * k]))(k, h), pipeline_mode=ONCE)
        for _ in sets
        for _ in range(2)
        for k in range(2)
        for h in range(2)
    ]
    piece_specs = [
        pl.BlockSpec((rows, tile), (lambda i: lambda t, w: (0, jnp.clip(t - i * tiles, 0, tiles - 1)))(i))
        for i in range(pieces)
    ]
    count = len(fixed_specs)

    def kernel(where_ref, *refs):
        fixed, near_refs, far_refs = refs[:count], refs[count : count + pieces], refs[count + pieces : -2]
        out_ref, flat = refs[-2:]
        step = pl.program_id(0)

        @pl.when(step == 0)
        def _():
            for n, ref in enumerate(fixed):
                kind, chip, at = n // 8, n // 4 % 2, n % 4
                flat[kind, at * part : (at + 1) * part, chip * rows : (chip + 1) * rows] = ref[...].T

        for i, kind in enumerate(kinds):

            @pl.when((step >= i * tiles) & (step < (i + 1) * tiles))
            def _():
                total = dot(flat[kind, :, :rows], near_refs[i][...], 1, 0)
                total += dot(flat[kind, :, rows:], far_refs[i][...], 1, 0)
                out_ref[0] = total[: 2 * part].astype(BF16)
                out_ref[1] = total[2 * part :].astype(BF16)

    return launch(
        kernel,
        [*[a for pair in sets for a in pair for _ in range(4)], *near, *far],
        fixed_specs + piece_specs * 2,
        name,
        [where],
        grid=(tiles * pieces,),
        out_specs=pl.BlockSpec((2, 2 * part, tile), lambda t, w: (0, 0, t)),
        out_shape=of((2, 2 * part, width * pieces)),
        scratch_shapes=[pltpu.VMEM((len(sets), 4 * part, 2 * rows), BF16)],
    )


def row_call(kernel, rows, where, ins, outs, sums, name):
    tile = min(256, rows)
    steps = rows // tile
    specs, arrays = [], []
    for item in ins:
        array, scalar = item if isinstance(item, tuple) else (item, None)
        if scalar is not None:
            specs.append(pl.BlockSpec((tile, D), (lambda s: lambda i, w: (w[s] * steps + i, 0))(scalar)))
        elif array.shape[0] == 1:
            specs.append(pl.BlockSpec((1, D), lambda i, w: (0, 0)))
        else:
            specs.append(pl.BlockSpec((tile, D), lambda i, w: (i, 0)))
        arrays.append(array)
    out_specs = [pl.BlockSpec((tile, width), lambda i, w: (i, 0)) for _, width in outs]
    out_shape = [of((rows, width), dtype) for dtype, width in outs]
    return launch(
        kernel,
        arrays,
        specs,
        name,
        [where],
        grid=(steps,),
        out_specs=out_specs + [pl.BlockSpec((8, D), lambda i, w: (0, 0))] * sums,
        out_shape=out_shape + [of((8, D), F32)] * sums,
    )


def add_refs(*refs):
    total = refs[0][...].astype(F32)
    for ref in refs[1:]:
        total += ref[...].astype(F32)
    return total


def split_features(where_ref, total, mine_ref, other_ref):
    first = where_ref[CORE] == 0
    low, high = total[:, : D // 2], total[:, D // 2 :]
    mine_ref[...] = jnp.where(first, low, high).astype(mine_ref.dtype)
    other_ref[...] = jnp.where(first, high, low).astype(other_ref.dtype)


def norm_kernel(where_ref, one_ref, two_ref, far_ref, x_ref, gain_ref, residual_ref, normed_ref):
    residual = add_refs(x_ref, one_ref, two_ref, far_ref)
    scale = lax.rsqrt(jnp.sum(residual * residual, axis=1, keepdims=True) / D + EPS)
    residual_ref[...] = residual
    normed_ref[...] = (residual * scale * gain_ref[...]).astype(BF16)


def norm_back(stream, gain, upstream, sum_ref):
    scale = lax.rsqrt(jnp.sum(stream * stream, axis=1, keepdims=True) / D + EPS)
    weighted = upstream * gain
    inner = jnp.sum(weighted * stream, axis=1, keepdims=True)
    part = jnp.sum((upstream * stream * scale).reshape(-1, 8, D), axis=0)

    @pl.when(pl.program_id(0) == 0)
    def _():
        sum_ref[...] = jnp.zeros_like(sum_ref)

    sum_ref[...] += part
    return scale * weighted - stream * (scale * scale * scale) * (inner / D)


def ffn_back_kernel(where_ref, one_ref, two_ref, far_ref, residual_ref, cot_ref, gain_ref, grad_ref, low_ref, sum_ref):
    back = norm_back(residual_ref[...], gain_ref[...], add_refs(one_ref, two_ref, far_ref), sum_ref)
    grad = cot_ref[...].astype(F32) + back
    grad_ref[...] = grad
    low_ref[...] = grad.astype(BF16)


def input_back_kernel(where_ref, one_ref, two_ref, far_ref, x_ref, grad_ref, gain_ref, mine_ref, other_ref, sum_ref):
    back = norm_back(x_ref[...].astype(F32), gain_ref[...], add_refs(one_ref, two_ref, far_ref), sum_ref)
    split_features(where_ref, grad_ref[...] + back, mine_ref, other_ref)


def mixed_kernel(where_ref, *refs):
    split_features(where_ref, add_refs(*refs[:-2]), *refs[-2:])


def finish(pieces, spans, turned, where, name):
    shape = pieces[0].shape
    part = shape[1]
    sizes = [2 * sum(hi - lo for lo, hi in mine) for mine in spans]

    def kernel(where_ref, *refs):
        ins, outs = refs[:4], refs[4:]
        for k in range(4):

            @pl.when(pl.program_id(0) == k)
            def _():
                for out_ref, mine, flip in zip(outs, spans, turned):
                    at = 0
                    for core in range(2):
                        for lo, hi in mine:
                            block = ins[k][core, :, lo:hi]
                            if flip:
                                out_ref[at : at + hi - lo, :] = block.T.astype(F32)
                            else:
                                out_ref[:, at : at + hi - lo] = block.astype(F32)
                            at += hi - lo

    return launch(
        kernel,
        pieces,
        [pl.BlockSpec(shape, lambda k, w: (0, 0, 0), pipeline_mode=ONCE)] * 4,
        name,
        [where],
        grid=(4,),
        out_specs=[
            pl.BlockSpec((n, part), lambda k, w: (0, w[QUARTER + k]))
            if flip
            else pl.BlockSpec((part, n), lambda k, w: (w[QUARTER + k], 0))
            for n, flip in zip(sizes, turned)
        ],
        out_shape=[of((n, 4 * part) if flip else (4 * part, n), F32) for n, flip in zip(sizes, turned)],
    )


def swap_axis(values, axis, distance):
    size = lax.axis_size(axis)
    return lax.ppermute(values, axis, [(i, i ^ distance) for i in range(size)])


def other_core(values):
    return swap_axis(values, "row", 1)


def other_chip(values):
    return swap_axis(values, "col", 1)


def far_plane(values):
    return swap_axis(values, "col", 2)


def hop(values, step):
    pairs = []
    for spot in range(4):
        for core in range(2):
            distance = 1 if (step == 1) == (core == 0) else 2
            pairs.append((spot * 2 + core, (spot ^ distance) * 2 + core))
    return lax.ppermute(values, ("dp", "row"), pairs)


def hop_one(values):
    return hop(values, 1)


def hop_two(values):
    return hop(values, 2)


def add32(*values):
    total = values[0].astype(F32)
    for value in values[1:]:
        total += value.astype(F32)
    return total


class Plan:
    def __init__(self, direct, blocks):
        self.blocks = blocks
        self.core = lax.axis_index("row")
        if direct:
            spot = lax.axis_index("dp")
            quarters = [spot ^ jnp.where(self.core == 0, k, (0, 2, 1, 3)[k]) for k in range(4)]
        else:
            quarters = [jnp.int32(k) for k in range(4)]
        self.where = jnp.stack([self.core, 1 - self.core] + quarters).astype(jnp.int32)
        self.line = Line()

    def run(self, call, *values):
        return self.line.run(call, *values)

    def mix(self, call, *values):
        return self.line.mix(call, *values)

    def send(self, move, value):
        return self.line.send(move, value)

    def ship(self, move, value):
        return self.line.ship(move, value)

    def post(self, move, value):
        return self.line.post(move, value)

    def pause(self):
        self.run(short_kernel, self.line.stamp)

    def swap(self, value):
        return self.line.swap(value)

    def place(self, sources, outs, phases, name, kept=0, fixed=0):
        return self.run(lambda first, *rest: place([first, *rest], outs, phases, self.where, name, kept, fixed), *sources)

    def by_core(self, low, high):
        return jnp.where(self.core == 0, low, high), jnp.where(self.core == 0, high, low)


class Group:
    def __init__(self, name, plan, sets, kinds, near, far, spans, turned):
        self.name, self.plan, self.sets, self.kinds = name, plan, sets, kinds
        self.near, self.far, self.spans, self.turned = near, far, spans, turned
        self.block = sum(a.shape[1] for a in near) // plan.blocks

    def produce(self, scalars):
        plan, count = self.plan, len(self.near)
        return plan.run(
            lambda first, *rest: quarter_product(
                self.sets, self.kinds, (first,) + rest[: count - 1], rest[count - 1 :], plan.where, scalars, self.name
            ),
            *self.near, *self.far,
        )

    def make(self):
        self.sent = self.produce((QUARTER + 1, 2))

    def leave(self):
        self.came = self.plan.post(hop_one, self.sent)

    def stay(self):
        self.kept = self.produce((QUARTER, 2))

    def second(self):
        def add(kept, came):
            return add32(kept[1], came[1]).astype(BF16)

        self.back = self.plan.post(hop_two, self.plan.mix(add, self.kept, self.came))

    def cross_plane(self):
        n = self.block

        def add(kept, came, back):
            return add32(kept[0, :, n:], came[0, :, n:], back[:, n:]).astype(BF16)

        self.arrived = self.plan.post(far_plane, self.plan.mix(add, self.kept, self.came, self.back))

    def total(self):
        n = self.block

        def add(arrived, kept, came, back):
            return add32(kept[0, :, :n], came[0, :, :n], back[:, :n], arrived).astype(BF16)

        whole = self.plan.swap(self.plan.mix(add, self.arrived, self.kept, self.came, self.back))
        self.both = whole.reshape(2, -1, n)

    def spread(self):
        self.one = self.plan.ship(hop_one, self.both)

    def spread_last(self):
        self.two = self.plan.send(hop_two, self.both)
        self.three = self.plan.send(hop_two, self.one)

    def finish(self):
        return self.plan.run(
            lambda first, *rest: finish((first,) + rest, self.spans, self.turned, self.plan.where, "finish"),
            self.both, self.one, self.two, self.three,
        )

    def whole(self, groups):
        plan = self.plan
        pieces = []
        for k in range(2):
            made = self.produce((QUARTER + 2 * k, 1))
            for one in made:
                total = jnp.stack(jnp.split(one.astype(F32), plan.blocks, axis=1))
                total = lax.psum_scatter(total, "col", scatter_dimension=0, axis_index_groups=groups)
                total = lax.psum(total, "dp").astype(BF16)
                pieces.append(plan.swap(total).reshape(2, -1, total.shape[1]))
        return finish(pieces, self.spans, self.turned, plan.where, "finish")


class Sizes:
    def __init__(self, tokens, w_query, w_gate):
        self.rows = tokens.shape[0]
        self.half = self.rows // 2
        self.width = w_query.shape[1] // 2
        self.units = w_gate.shape[1] // 2
        self.tile = min(UNIT_TILE, self.units)
        self.split = D // 2


def interleaved(s):
    return [(p, lo) for lo in range(0, s.units, s.tile) for p in range(2)]


def gu_spans(s):
    return [[(lo + p * s.tile, lo + (p + 1) * s.tile) for lo in range(0, 2 * s.units, 2 * s.tile)] for p in range(2)]


def columns(lo, size):
    return lambda w: (slice(None), pl.ds(lo, size))


def join_features(plan, s, mine, theirs):
    return plan.place(
        [mine, theirs], [of((s.rows, D))],
        [[(0, full, 0, cols_at(CORE, s.split)), (1, full, 0, cols_at(OTHER, s.split))]], "join",
    )[0]


def join_rows(plan, s, mine, theirs):
    return plan.place(
        [mine, theirs], [of((s.rows, D))], [[(0, full, 0, rows_at(CORE, s.half)), (1, full, 0, rows_at(OTHER, s.half))]], "join"
    )[0]


def pack_in(plan, s, weights, parts, name):
    total = sum(size for _, _, size, _ in parts)
    moves, at = [], 0
    for i, lo, size, step in parts:
        moves.append((i, cols_at(OTHER, step, lo, size), 0, columns(at, size)))
        at += size
    return plan.place(weights, [of((s.split, total))], [moves], name, fixed=len(weights))[0]


def own_in(plan, s, weights, got, parts):
    total = got.shape[1]
    moves, at = [], 0
    for i, lo, size, step in parts:
        moves.append((i, cols_at(CORE, step, lo, size), 0, block_at(CORE, s.split, at, size)))
        at += size
    moves.append((len(weights), full, 0, rows_at(OTHER, s.split)))
    return plan.place([*weights, got], [of((D, total))], [moves], "own", fixed=len(weights))[0]


def own_out(plan, s, weight, got):
    rows = got.shape[0]
    return plan.place(
        [weight, got], [of((rows, D))], [[(0, rows_at(CORE, rows), 0, cols_at(CORE, s.split)), (1, full, 0, cols_at(OTHER, s.split))]],
        "own", fixed=1,
    )[0]


def both_gains(plan, mine, other):
    joined = plan.mix(lambda a, b: jnp.concatenate(plan.by_core(a, b), axis=1), mine, other)
    return joined[:1], joined[1:]


def norm_first(plan, s, near, far, x_near, gains):
    return plan.run(
        lambda *a: row_call(
            norm_kernel, s.half, plan.where, [*a[:3], (a[3], CORE), a[4]], [(F32, D), (BF16, D)], 0, "norm"
        ),
        *near, far, x_near, gains,
    )


def norm_ffn_back(plan, s, near, far, residual, cot_near, gains):
    return plan.run(
        lambda *a: row_call(
            ffn_back_kernel, s.half, plan.where, [*a[:4], (a[4], CORE), a[5]], [(F32, D), (BF16, D)], 1, "ffn_back"
        ),
        *near, far, residual, cot_near, gains,
    )


def norm_input_back(plan, s, near, far, x_near, grad_residual, gains):
    return plan.run(
        lambda *a: row_call(
            input_back_kernel, s.half, plan.where, [*a[:3], (a[3], CORE), *a[4:]],
            [(F32, D // 2), (F32, D // 2)], 1, "input_back",
        ),
        *near, far, x_near, grad_residual, gains,
    )


def add_mixed(plan, s, near, *others):
    return plan.run(
        lambda *a: row_call(mixed_kernel, s.half, plan.where, list(a), [(BF16, D // 2), (BF16, D // 2)], 0, "mixed"),
        *near, *others,
    )


def core_sum(plan, lhs, weights, turned, name):
    count = len(lhs)
    other, mine = plan.run(lambda *a: product(a[:count], a[count:], plan.where, turned, name), *lhs, *weights)
    return mine, plan.ship(other_core, other)


def add_pair(plan, pair):
    return plan.mix(lambda a, b: add32(a, b).astype(BF16), pair[1], pair[0])


def side_by_side(plan, s, mine, got):
    width = mine.shape[1]
    return plan.place(
        [mine, got], [of((s.rows, width), mine.dtype)],
        [[(0, full, 0, rows_at(CORE, s.half)), (1, full, 0, rows_at(OTHER, s.half))]], "sides",
    )[0]


def grad_attended(plan, gr, weight):
    return plan.run(lambda a: product([a], [weight], turned=True, name="grad_att"), gr)


def square(tokens, gain_attn, gain_ffn, w_query, w_key, w_value, w_out, w_gate, w_up, w_down, cotangent):
    plan = Plan(True, 2)
    s = Sizes(tokens, w_query, w_gate)
    run, mix, send, ship, post, where = plan.run, plan.mix, plan.send, plan.ship, plan.post, plan.where
    cos, sin = rope_tables()
    cos_rows, sin_rows = jnp.tile(cos, (s.rows // SEQ_LEN, 1)), jnp.tile(sin, (s.rows // SEQ_LEN, 1))
    qkv_parts = [(p, 0, s.width, s.width) for p in range(3)]
    gu_parts = [(p, lo, s.tile, s.units) for p, lo in interleaved(s)]
    eighth = D // 4 // 8

    far_tokens = other_chip(tokens)
    near_tokens = other_core(tokens)
    gains_mine = jnp.stack((gain_attn, gain_ffn))
    gains_other = other_core(gains_mine)
    plan.line.stamp = gains_mine[:, :LANES]
    got_qkv = ship(other_core, pack_in(plan, s, [w_query, w_key, w_value], qkv_parts, "pack"))
    pack_out = plan.place([w_out], [of((s.width, s.split))], [[(0, rows_at(OTHER, s.width), 0, full)]], "pack", fixed=1)[0]
    got_out = ship(other_core, pack_out)
    own_qkv = own_in(plan, s, [w_query, w_key, w_value], got_qkv, qkv_parts)
    own_o = own_out(plan, s, w_out, got_out)
    quarter, out_rows = D // 4, s.width // 4
    slots = quarter // out_rows
    out_cols = D // slots
    qkvo = plan.place(
        [own_qkv, own_o], [of((quarter, 3 * s.width + out_cols))],
        [
            [(0, rows_at(QUARTER, quarter), 0, columns(0, 3 * s.width))]
            + [
                (
                    1, (lambda j: lambda w: (pl.ds(pl.multiple_of(w[QUARTER] * out_rows, out_rows), out_rows), pl.ds(j * out_cols, out_cols)))(j),
                    0, (lambda j: lambda w: (pl.ds(j * out_rows, out_rows), pl.ds(3 * s.width, out_cols)))(j),
                )
                for j in range(slots)
            ]
        ],
        "quarter",
    )[0]
    qkvo_zero = ship(far_plane, qkvo)
    gains_attn, gains_ffn = both_gains(plan, gains_mine, gains_other)
    got_gu = ship(other_core, pack_in(plan, s, [w_gate, w_up], gu_parts, "pack"))
    pack_down = plan.place([w_down], [of((s.units, s.split))], [[(0, rows_at(OTHER, s.units), 0, full)]], "pack", fixed=1)[0]
    got_down = ship(other_core, pack_down)
    x_near = join_features(plan, s, tokens, near_tokens)
    own_gu = own_in(plan, s, [w_gate, w_up], got_gu, gu_parts)
    own_d = own_out(plan, s, w_down, got_down)
    down_rows = s.units // 4
    mixed_rows = quarter // 2 + down_rows // 2
    gud = [
        plan.place(
            [own_gu, own_d], [of((mixed_rows, D))],
            [[
                (0, (lambda i: rows_span(QUARTER, quarter, i * (quarter // 2), quarter // 2))(i), 0, rows_fixed(0, quarter // 2)),
                (1, (lambda i: rows_span(QUARTER, down_rows, i * (down_rows // 2), down_rows // 2))(i), 0, rows_fixed(quarter // 2, down_rows // 2)),
            ]],
            "quarter",
        )[0]
        for i in range(2)
    ]
    gud_zero = [None, None]

    def project(x, weight, first):
        return run(lambda a: project_qkv(a, gains_attn, cos_rows, sin_rows, weight, first), x)

    normed_near, *near_own = project(x_near, own_qkv, True)
    far_half = send(other_core, far_tokens)
    o_near_own = run(attend, *near_own)
    qkvo_one, qkvo_two = send(hop_one, qkvo_zero), send(hop_two, qkvo_zero)
    gud_zero[0] = send(far_plane, gud[0])
    far_cot = send(other_chip, cotangent)
    x_far = join_features(plan, s, far_tokens, far_half)
    normed_far, *far_own = project(x_far, own_qkv, True)
    qkvo_three = send(hop_two, qkvo_one)
    o_far_own = run(attend, *far_own)
    pieces = [qkvo_zero, qkvo_one, qkvo_two, qkvo_three]
    for_qkv, for_o = plan.place(
        pieces, [of((D, 3 * s.width)), of((s.width, D))],
        [
            [(k, columns(0, 3 * s.width), 0, rows_at(QUARTER + k, quarter)) for k in range(4)]
            + [
                (
                    k, (lambda j: lambda w: (pl.ds(j * out_rows, out_rows), pl.ds(3 * s.width, out_cols)))(j),
                    1, (lambda k, j: lambda w: (pl.ds(pl.multiple_of(w[QUARTER + k] * out_rows, out_rows), out_rows), pl.ds(j * out_cols, out_cols)))(k, j),
                )
                for k in range(4)
                for j in range(slots)
            ]
        ],
        "other",
    )
    w_qkv, w_o = [own_qkv, for_qkv], [own_o, for_o]

    far_for = project(normed_far, for_qkv, False)
    gud_one, gud_two, gud_three = [None, None], [None, None], [None, None]
    o_far = [o_far_own, run(attend, *far_for)]
    far = core_sum(plan, [o[0] for o in o_far], w_o, False, "out")
    near_for = project(normed_near, for_qkv, False)
    far = post(other_chip, add_pair(plan, far))
    gud_one[0], gud_two[0] = send(hop_one, gud_zero[0]), send(hop_two, gud_zero[0])
    gud_zero[1] = send(far_plane, gud[1])
    near_cot = send(other_core, cotangent)
    o_near = [o_near_own, run(attend, *near_for)]
    near = core_sum(plan, [o[0] for o in o_near], w_o, False, "out")
    gud_three[0] = send(hop_two, gud_one[0])
    cot_near = join_features(plan, s, cotangent, near_cot)
    cot_far_row = send(other_core, far_cot)
    plan.pause()
    cot_far = join_features(plan, s, far_cot, cot_far_row)
    def spread_out(i, outs):
        count = quarter // 2, down_rows // 2
        return plan.place(
            [g[i] for g in (gud_zero, gud_one, gud_two, gud_three)] + outs, [of(own_gu.shape), of(own_d.shape)],
            [
                [(k, rows_fixed(0, count[0]), 0, rows_span(QUARTER + k, quarter, i * count[0], count[0])) for k in range(4)]
                + [(k, rows_fixed(count[0], count[1]), 1, rows_span(QUARTER + k, down_rows, i * count[1], count[1])) for k in range(4)]
            ],
            "other", len(outs),
        )

    halves = spread_out(0, [])
    residual, normed_ffn = norm_first(plan, s, near, far, x_near, gains_ffn)
    nf_row = ship(other_core, normed_ffn)
    nf_chip = post(other_chip, normed_ffn)
    gud_one[1], gud_two[1] = send(hop_one, gud_zero[1]), send(hop_two, gud_zero[1])
    nf_near = join_rows(plan, s, normed_ffn, nf_row)
    fed_near = [run(ffn, nf_near, cot_near, own_gu, own_d)]
    nf_far_row = send(other_core, nf_chip)
    gud_three[1] = send(hop_two, gud_one[1])
    plan.pause()
    nf_far = join_rows(plan, s, nf_chip, nf_far_row)
    fed_far = [run(ffn, nf_far, cot_far, own_gu, own_d)]
    for_gu, for_d = spread_out(1, list(halves))
    w_gu, w_d = [own_gu, for_gu], [own_d, for_d]
    fed_far.append(run(ffn, nf_far, cot_far, for_gu, for_d))
    fed_near.append(run(ffn, nf_near, cot_near, for_gu, for_d))
    hid_near, ggu_near = [f[0] for f in fed_near], [f[1] for f in fed_near]
    hid_far, ggu_far = [f[0] for f in fed_far], [f[1] for f in fed_far]

    ups = Group("gu_grad", plan, [(nf_near, nf_far)], [0, 0], ggu_near, ggu_far, gu_spans(s), [False, False])
    down = Group("down_grad", plan, [(cot_near, cot_far)], [0, 0], hid_near, hid_far, [[(0, s.units)]], [True])
    ups.make()
    ups.leave()
    far = core_sum(plan, ggu_far, w_gu, True, "ffn_in")
    plan.pause()
    far = post(other_chip, add_pair(plan, far))
    near = core_sum(plan, ggu_near, w_gu, True, "ffn_in")
    ups.stay()
    grad_residual, grad_low, gain_ffn_part = norm_ffn_back(plan, s, near, far, residual, cot_near, gains_ffn)
    gr_row = ship(other_core, grad_low)
    gr_chip = post(other_chip, grad_low)
    gr_near = join_rows(plan, s, grad_low, gr_row)
    ups.second()

    def back_one(gr, heads, outs, b):
        return run(attend_back, grad_attended(plan, gr, w_o[b]), *heads[b], *outs[b], cos, sin)

    near_heads, far_heads = [near_own, near_for], [far_own, far_for]
    back_near = [back_one(gr_near, near_heads, o_near, b) for b in range(2)]
    gr_far_row = send(other_core, gr_chip)
    down.make()
    ups.cross_plane()
    down.leave()
    down.stay()
    gr_far = join_rows(plan, s, gr_chip, gr_far_row)
    back_far = [back_one(gr_far, far_heads, o_far, b) for b in range(2)]
    down.second()
    dqkv_far = [jnp.concatenate(b, axis=1) for b in back_far]
    far = core_sum(plan, dqkv_far, w_qkv, True, "qkv_in")
    heads = Group(
        "head_grad", plan, [(normed_near, normed_far), (gr_near, gr_far)], [0, 0, 0, 1] * 2,
        [a for b in range(2) for a in (*back_near[b], o_near[b][0])],
        [a for b in range(2) for a in (*back_far[b], o_far[b][0])],
        [[(p * s.width, (p + 1) * s.width)] for p in range(4)], [False, False, False, True],
    )
    heads.make()
    heads.leave()
    far = post(other_chip, add_pair(plan, far))
    dqkv_near = [jnp.concatenate(b, axis=1) for b in back_near]
    near = core_sum(plan, dqkv_near, w_qkv, True, "qkv_in")
    down.cross_plane()
    heads.stay()
    heads.second()
    mixed_far = core_sum(plan, hid_far, w_d, False, "down")
    ups.total()
    input_mine, input_other, gain_attn_part = norm_input_back(plan, s, near, far, x_near, grad_residual, gains_attn)
    input_got = ship(other_core, input_other)
    gains = mix(lambda a, b: jnp.stack((jnp.sum(a, axis=0), jnp.sum(b, axis=0))), gain_attn_part, gain_ffn_part)
    gains_got = ship(other_core, gains)
    heads.cross_plane()
    mixed_far = post(other_chip, add_pair(plan, mixed_far))
    ups.spread()
    input_grad = side_by_side(plan, s, input_mine, input_got)
    gains = mix(jnp.add, gains, gains_got)
    gains_got = ship(hop_one, gains)
    ups.spread_last()
    mixed_near = core_sum(plan, hid_near, w_d, False, "down")
    gains = mix(jnp.add, gains, gains_got)
    down.total()
    down.spread()
    gains_got = ship(hop_two, gains)
    plan.pause()
    mixed_near = [add_pair(plan, mixed_near)]
    gains = mix(jnp.add, gains, gains_got)
    gains_got = ship(other_chip, gains)
    plan.pause()
    heads.total()
    heads.spread()
    down.spread_last()
    gains = mix(jnp.add, gains, gains_got)
    gains_got = ship(far_plane, gains)
    gate_grad, up_grad = ups.finish()
    mixed_mine, mixed_other = add_mixed(plan, s, mixed_near, mixed_far, residual)
    mixed_got = ship(other_core, mixed_other)
    heads.spread_last()
    (down_grad,) = down.finish()
    mixed = side_by_side(plan, s, mixed_mine, mixed_got)
    gains = mix(jnp.add, gains, gains_got)
    gains = jnp.where(plan.core == 0, gains[:, : s.split], gains[:, s.split :])
    q_grad, k_grad, v_grad, out_grad = heads.finish()
    return mixed, input_grad, gains[0], gains[1], q_grad, k_grad, v_grad, out_grad, gate_grad, up_grad, down_grad


def pair_order(near, far):
    member = lax.axis_index("col") % 2
    return jnp.concatenate((jnp.where(member == 0, near, far), jnp.where(member == 0, far, near)), axis=0)


def from_pair(joined):
    member = lax.axis_index("col") % 2
    first, second = jnp.split(joined, 2, axis=0)
    return jnp.where(member == 0, first, second), jnp.where(member == 0, second, first)


def general(tokens, gain_attn, gain_ffn, w_query, w_key, w_value, w_out, w_gate, w_up, w_down, cotangent):
    blocks = lax.axis_size("col") // 2
    groups = [[i for i in range(2 * blocks) if i % 2 == m] for m in range(2)]
    plan = Plan(False, blocks)
    s = Sizes(tokens, w_query, w_gate)
    run, where = plan.run, plan.where
    cos, sin = rope_tables()
    shared = s.rows % SEQ_LEN != 0
    qkv_parts = [(p, 0, s.width, s.width) for p in range(3)]
    gu_parts = [(p, lo, s.tile, s.units) for p, lo in interleaved(s)]

    def gathered(own):
        every = lax.all_gather(own, "col", axis=0, axis_index_groups=groups)
        return [every[b] for b in range(blocks)]

    def pack_rows(weight, rows):
        return plan.place([weight], [of((rows, s.split))], [[(0, rows_at(OTHER, rows), 0, full)]], "pack", fixed=1)[0]

    got = other_core(pack_in(plan, s, [w_query, w_key, w_value], qkv_parts, "pack"))
    w_qkv = gathered(own_in(plan, s, [w_query, w_key, w_value], got, qkv_parts))
    got = other_core(pack_in(plan, s, [w_gate, w_up], gu_parts, "pack"))
    w_gu = gathered(own_in(plan, s, [w_gate, w_up], got, gu_parts))
    w_o = gathered(own_out(plan, s, w_out, other_core(pack_rows(w_out, s.width))))
    w_d = gathered(own_out(plan, s, w_down, other_core(pack_rows(w_down, s.units))))
    gains_mine = jnp.stack((gain_attn, gain_ffn))
    gains_attn, gains_ffn = both_gains(plan, gains_mine, other_core(gains_mine))

    def both_chips(values):
        far = other_chip(values)
        return join_features(plan, s, values, other_core(values)), join_features(plan, s, far, other_core(far))

    x_near, x_far = both_chips(tokens)
    cot_near, cot_far = both_chips(cotangent)

    def tables(offset):
        if shared:
            return [lax.dynamic_slice_in_dim(t, offset, s.rows) for t in (cos, sin)]
        return [jnp.tile(t, (s.rows // SEQ_LEN, 1)) for t in (cos, sin)]

    first = (lax.axis_index("col") % 2) * s.rows
    chips = []
    for x, offset in ((x_near, first), (x_far, s.rows - first)):
        turn = tables(offset)
        normed, *heads = run(lambda a: project_qkv(a, gains_attn, *turn, w_qkv[0], True), x)
        every = [heads]
        for w in w_qkv[1:]:
            every.append(run(lambda a: project_qkv(a, gains_attn, *turn, w, False), normed))
        chips.append((normed, every))
    (normed_near, heads_near), (normed_far, heads_far) = chips

    def together(near, far):
        return pair_order(near, far) if shared else jnp.concatenate((near, far), axis=0)

    def apart(joined):
        return from_pair(joined) if shared else jnp.split(joined, 2, axis=0)

    joined_heads = [[together(a, b) for a, b in zip(n, f)] for n, f in zip(heads_near, heads_far)]
    outs = [run(attend, *h) for h in joined_heads]
    att = [apart(o[0]) for o in outs]
    att_near, att_far = [a[0] for a in att], [a[1] for a in att]

    def four_core_sum(near, far, weights, turned, name):
        far = other_chip(add_pair(plan, core_sum(plan, far, weights, turned, name)))
        return core_sum(plan, near, weights, turned, name), far

    def gather_tokens(values):
        far = other_chip(values)
        return join_rows(plan, s, values, other_core(values)), join_rows(plan, s, far, other_core(far))

    residual, normed_ffn = norm_first(plan, s, *four_core_sum(att_near, att_far, w_o, False, "out"), x_near, gains_ffn)
    nf_near, nf_far = gather_tokens(normed_ffn)
    fed_near = [run(ffn, nf_near, cot_near, w_gu[b], w_d[b]) for b in range(blocks)]
    fed_far = [run(ffn, nf_far, cot_far, w_gu[b], w_d[b]) for b in range(blocks)]
    hid_near, ggu_near = [f[0] for f in fed_near], [f[1] for f in fed_near]
    hid_far, ggu_far = [f[0] for f in fed_far], [f[1] for f in fed_far]
    kinds = [0] * blocks
    ups = Group("gu_grad", plan, [(nf_near, nf_far)], kinds, ggu_near, ggu_far, gu_spans(s), [False, False])
    down = Group("down_grad", plan, [(cot_near, cot_far)], kinds, hid_near, hid_far, [[(0, s.units)]], [True])
    grad_residual, grad_low, gain_ffn_part = norm_ffn_back(
        plan, s, *four_core_sum(ggu_near, ggu_far, w_gu, True, "ffn_in"), residual, cot_near, gains_ffn
    )
    gr_near, gr_far = gather_tokens(grad_low)
    gr = together(gr_near, gr_far)
    backs = []
    for b in range(blocks):
        grads = run(attend_back, grad_attended(plan, gr, w_o[b]), *joined_heads[b], *outs[b], cos, sin)
        backs.append([apart(g) for g in grads])
    back_near = [[g[0] for g in b] for b in backs]
    back_far = [[g[1] for g in b] for b in backs]
    heads = Group(
        "head_grad", plan, [(normed_near, normed_far), (gr_near, gr_far)], [0, 0, 0, 1] * blocks,
        [a for b in range(blocks) for a in (*back_near[b], att_near[b])],
        [a for b in range(blocks) for a in (*back_far[b], att_far[b])],
        [[(p * s.width, (p + 1) * s.width)] for p in range(4)], [False, False, False, True],
    )
    dqkv_near = [jnp.concatenate(b, axis=1) for b in back_near]
    dqkv_far = [jnp.concatenate(b, axis=1) for b in back_far]
    input_mine, input_other, gain_attn_part = norm_input_back(
        plan, s, *four_core_sum(dqkv_near, dqkv_far, w_qkv, True, "qkv_in"), x_near, grad_residual, gains_attn
    )
    mixed_mine, mixed_other = add_mixed(plan, s, *four_core_sum(hid_near, hid_far, w_d, False, "down"), residual)
    gains = lax.psum(jnp.stack((jnp.sum(gain_attn_part, axis=0), jnp.sum(gain_ffn_part, axis=0))), ("dp", "col", "row"))
    gains = jnp.where(plan.core == 0, gains[:, : s.split], gains[:, s.split :])
    mixed = side_by_side(plan, s, mixed_mine, other_core(mixed_other))
    input_grad = side_by_side(plan, s, input_mine, other_core(input_other))
    q_grad, k_grad, v_grad, out_grad = heads.whole(groups)
    gate_grad, up_grad = ups.whole(groups)
    (down_grad,) = down.whole(groups)
    return mixed, input_grad, gains[0], gains[1], q_grad, k_grad, v_grad, out_grad, gate_grad, up_grad, down_grad


def solution(mesh):
    stream = P(("dp", "col"), "row")
    gain = P("row")
    inward, outward = P("row", "col"), P("col", "row")
    weights = (inward, inward, inward, outward, inward, inward, outward)
    fits = mesh.shape["dp"] == 4 and mesh.shape["col"] == 4
    return jax.shard_map(
        lambda *args: square(*args) if fits and args[0].shape[0] % SEQ_LEN == 0 else general(*args),
        mesh=mesh,
        in_specs=(stream, gain, gain, *weights, stream),
        out_specs=(stream, stream, gain, gain, *weights),
        check_vma=False,
    )
```

```python
import jax
import jax.numpy as jnp
from jax import lax
from jax.experimental import pallas as pl
from jax.experimental.pallas import tpu as pltpu
from jax.sharding import PartitionSpec as P

D = 2048
HEAD_DIM = 64
SEQ_LEN = 1024
LANES = 128
EPS = 1e-05
ROPE_BASE = 130000.0
VMEM = 48 * 1024 * 1024
UNIT_TILE = 256
QB = 256
COST = 10**12
F32 = jnp.float32
BF16 = jnp.bfloat16


def dot(a, b, ca, cb):
    return lax.dot_general(a, b, (((ca,), (cb,)), ((), ())), preferred_element_type=F32)


def of(shape, dtype=BF16):
    return jax.ShapeDtypeStruct(tuple(shape), dtype)


class Line:
    waiting = []
    mark = None

    def __init__(self):
        self.last = []

    def run(self, call, *values):
        Line.waiting = list(self.last)
        result = call(*values)
        self.last = [Line.mark]
        return result

    def tied(self, value):
        if not self.last:
            return value
        value, *self.last = lax.optimization_barrier((value, *self.last))
        return value

    def mix(self, call, first, *values):
        return self.tied(call(self.tied(first), *values))

    def send(self, move, value):
        return move(self.tied(value))

    def ship(self, move, value):
        return move(value)

    def post(self, move, value):
        sent = move(value)
        mark = other_core(self.tied(self.stamp))
        self.run(short_kernel, self.stamp)
        self.last = self.last + [mark]
        return sent

    def swap(self, value):
        return self.tied(lax.all_to_all(self.tied(value), "row", split_axis=0, concat_axis=0, tiled=True))


ONCE = pl.Buffered(1)


def launch(kernel, arrays, in_specs, name, prefetch=(), **rest):
    held, Line.waiting = Line.waiting, []
    skip, count = len(held), len(prefetch) + len(arrays)
    out_shape, out_specs = rest.pop("out_shape"), rest.pop("out_specs")
    single = not isinstance(out_shape, (list, tuple))
    out_shape, out_specs = ([out_shape], [out_specs]) if single else (list(out_shape), list(out_specs))
    outs = count + skip + len(out_shape)

    def body(*refs):
        kernel(*refs[:count], *refs[count + skip : outs], *refs[outs + 1 :])

    in_specs = list(in_specs) + [pl.BlockSpec(memory_space=pl.ANY)] * skip
    out_specs = out_specs + [pl.BlockSpec(memory_space=pl.ANY)]
    if prefetch:
        layout = dict(
            grid_spec=pltpu.PrefetchScalarGridSpec(
                num_scalar_prefetch=len(prefetch), in_specs=in_specs, out_specs=out_specs, **rest
            )
        )
    else:
        layout = dict(in_specs=in_specs, out_specs=out_specs, **rest)
    *results, Line.mark = pl.pallas_call(
        body,
        out_shape=out_shape + [of((8, LANES), F32)],
        compiler_params=pltpu.CompilerParams(vmem_limit_bytes=VMEM),
        cost_estimate=pl.CostEstimate(flops=COST, bytes_accessed=1, transcendentals=0),
        name=name,
        **layout,
    )(*prefetch, *arrays, *held)
    return results[0] if single else results


def short_kernel(values):
    def kernel(in_ref, out_ref):
        out_ref[0, 0] = 0.0

    return launch(
        kernel, [values], [pl.BlockSpec(memory_space=pl.ANY)], "short",
        out_specs=pl.BlockSpec(memory_space=pltpu.SMEM), out_shape=of((1, 1), F32),
    )


def extent(shape, index):
    sizes = []
    for size, at in zip(shape, index):
        if not isinstance(at, int):
            sizes.append(size if isinstance(at, slice) else at.size)
    return tuple(sizes)


def place(sources, outs, phases, where, name, kept=0, fixed=0):
    moves = [m for phase in phases for m in phase]
    shapes = [extent((sources[src] if src >= 0 else outs[-1 - src]).shape, src_at([0] * 8)) for src, src_at, _, _ in moves]
    count = len(sources)

    def kernel(where_ref, *refs):
        ins, out_refs, held = refs[:count], refs[count : count + len(outs)], refs[count + len(outs) : -2]
        in_sems, out_sems = refs[-2:]
        base = 0
        for phase in phases:
            loads, stores = [], []
            for n, (src, src_at, dst, dst_at) in enumerate(phase, base):
                src_ref = out_refs[-1 - src] if src < 0 else ins[src]
                loads.append(pltpu.make_async_copy(src_ref.at[src_at(where_ref)], held[n], in_sems.at[n]))
                stores.append(pltpu.make_async_copy(held[n], out_refs[dst].at[dst_at(where_ref)], out_sems.at[n]))
            for load in loads:
                load.start()
            for load, store in zip(loads, stores):
                load.wait()
                store.start()
            for store in stores:
                store.wait()
            base += len(phase)

    sources = [pltpu.with_memory_space_constraint(a, pltpu.HBM) for a in sources[:fixed]] + list(sources[fixed:])
    return launch(
        kernel,
        [where, *sources],
        [pl.BlockSpec(memory_space=pltpu.SMEM)]
        + [pl.BlockSpec(memory_space=pltpu.HBM)] * fixed
        + [pl.BlockSpec(memory_space=pl.ANY)] * (count - fixed),
        name,
        out_specs=[pl.BlockSpec(memory_space=pl.ANY)] * len(outs),
        out_shape=list(outs),
        scratch_shapes=[pltpu.VMEM(s, outs[m[2]].dtype) for s, m in zip(shapes, moves)] + [pltpu.SemaphoreType.DMA((len(moves),))] * 2,
        input_output_aliases={1 + count - kept + i: i for i in range(kept)},
    )


CORE, OTHER, QUARTER = 0, 1, 2


def full(_):
    return (slice(None), slice(None))


def rows_at(scalar, size, base=0):
    return lambda w: (pl.ds(pl.multiple_of(base + w[scalar] * size, size), size), slice(None))


def cols_at(scalar, size, lo=0, width=None):
    width = width or size
    return lambda w: (slice(None), pl.ds(pl.multiple_of(w[scalar] * size + lo, width), width))


def rows_span(scalar, size, lo, count):
    return lambda w: (pl.ds(pl.multiple_of(w[scalar] * size + lo, count), count), slice(None))


def rows_fixed(lo, count):
    return lambda w: (pl.ds(lo, count), slice(None))


def block_at(row_scalar, height, lo, width):
    return lambda w: (pl.ds(pl.multiple_of(w[row_scalar] * height, height), height), pl.ds(lo, width))


def rope_tables():
    half = HEAD_DIM // 2
    frequency = jnp.exp(-jnp.log(ROPE_BASE) * jnp.arange(half, dtype=F32) * (2.0 / HEAD_DIM))
    frequency = jnp.tile(frequency, 4)
    sign = jnp.where(jnp.arange(LANES) % HEAD_DIM < half, -1.0, 1.0)
    angles = jnp.arange(SEQ_LEN, dtype=F32)[:, None] * frequency[None, :]
    return jnp.cos(angles), jnp.sin(angles) * sign[None, :]


def swap_halves(values):
    half = HEAD_DIM // 2
    lane = lax.broadcasted_iota(jnp.int32, values.shape, 1)
    return jnp.where(lane % HEAD_DIM < half, pltpu.roll(values, LANES - half, 1), pltpu.roll(values, half, 1))


def qkv_kernel(first, x_ref, gain_ref, cos_ref, sin_ref, w_ref, *refs):
    q_ref, k_ref, v_ref = refs[-3:]
    if first:
        x = x_ref[...].astype(F32)
        scale = lax.rsqrt(jnp.sum(x * x, axis=1, keepdims=True) / D + EPS)
        refs[0][...] = (x * scale * gain_ref[...]).astype(BF16)
        normed = refs[0][...]
    else:
        normed = x_ref[...]
    cos, sin = cos_ref[...], sin_ref[...]
    width = q_ref.shape[1]
    projected = dot(normed, w_ref[...], 1, 0)
    for part, (out_ref, mult) in enumerate(((q_ref, HEAD_DIM**-0.5), (k_ref, 1.0))):
        for lo in range(0, width, LANES):
            piece = projected[:, part * width + lo : part * width + lo + LANES]
            out_ref[:, lo : lo + LANES] = ((piece * cos + swap_halves(piece) * sin).astype(BF16) * mult).astype(BF16)
    v_ref[...] = projected[:, 2 * width :].astype(BF16)


def project_qkv(x, gain, cos, sin, weight, first):
    rows, width = x.shape[0], weight.shape[1] // 3
    tile = min(512, rows)
    row_block = lambda n: pl.BlockSpec((tile, n), lambda i: (i, 0))
    whole = lambda a: pl.BlockSpec(a.shape, lambda i: (0, 0), pipeline_mode=ONCE)
    outs = [D] * first + [width] * 3
    return launch(
        lambda *refs: qkv_kernel(first, *refs),
        [x, gain, cos, sin, weight],
        [row_block(D), whole(gain), row_block(LANES), row_block(LANES), whole(weight)],
        "qkv",
        grid=(rows // tile,),
        out_specs=[row_block(n) for n in outs],
        out_shape=[of((rows, n)) for n in outs],
    )


def head_of(values, head):
    lane = lax.broadcasted_iota(jnp.int32, values.shape, 1)
    return jnp.where((lane >= HEAD_DIM) == (head == 1), values, jnp.zeros_like(values))


def causal_scores(keys, queries, start):
    scores = dot(keys, queries, 1, 1)
    last = scores[start:]
    key_at = lax.broadcasted_iota(jnp.int32, last.shape, 0)
    query_at = lax.broadcasted_iota(jnp.int32, last.shape, 1)
    last = jnp.where(key_at <= query_at, last, -1e30)
    return last if start == 0 else jnp.concatenate((scores[:start], last), axis=0)


def attend_kernel(q_ref, k_ref, v_ref, o_ref, lse_ref):
    values = [head_of(v_ref[...], head) for head in range(2)]
    for start in range(0, SEQ_LEN, QB):
        stop = start + QB
        queries = q_ref[start:stop, :]
        outs, scales = [], []
        for head in range(2):
            scores = causal_scores(k_ref[:stop, :], head_of(queries, head), start)
            top = jnp.max(scores, axis=0, keepdims=True)
            weights = jnp.exp(scores - top)
            total = jnp.sum(weights, axis=0, keepdims=True)
            lse_ref[0, 0, head : head + 1, start:stop] = top + jnp.log(total)
            outs.append(dot(weights.astype(BF16), values[head][:stop], 0, 0))
            scales.append(jnp.broadcast_to(1.0 / total, (HEAD_DIM, QB)))
        o_ref[start:stop, :] = ((outs[0] + outs[1]) * jnp.concatenate(scales, axis=0).T).astype(BF16)


def attend(q, k, v):
    rows, width = q.shape
    seqs, pairs = rows // SEQ_LEN, width // LANES
    block = pl.BlockSpec((SEQ_LEN, LANES), lambda s, h: (s, h))
    return launch(
        attend_kernel,
        [q, k, v],
        [block] * 3,
        "attend",
        grid=(seqs, pairs),
        out_specs=[block, pl.BlockSpec((1, 1, 8, SEQ_LEN), lambda s, h: (s, h, 0, 0))],
        out_shape=[of((rows, width)), of((seqs, pairs, 8, SEQ_LEN), F32)],
    )


def attend_back_kernel(do_ref, q_ref, k_ref, v_ref, o_ref, lse_ref, cos_ref, sin_ref, dq_ref, dk_ref, dv_ref, dk_acc, dv_acc):
    k_t = k_ref[...].T
    dk_acc[...] = jnp.zeros_like(dk_acc)
    dv_acc[...] = jnp.zeros_like(dv_acc)
    for start in range(0, SEQ_LEN, QB):
        stop = start + QB
        queries, grads = q_ref[start:stop, :], do_ref[start:stop, :]
        inner = (grads.astype(F32) * o_ref[start:stop, :].astype(F32)).T
        back = []
        for head in range(2):
            one_q, one_g = head_of(queries, head), head_of(grads, head)
            scores = causal_scores(k_ref[:stop, :], one_q, start)
            weights = jnp.exp(scores - lse_ref[0, 0, head : head + 1, start:stop])
            grad_weights = dot(v_ref[:stop, :], one_g, 1, 1)
            delta = jnp.sum(inner[head * HEAD_DIM : (head + 1) * HEAD_DIM], axis=0, keepdims=True)
            grad_scores = (weights * (grad_weights - delta)).astype(BF16)
            dv_acc[:stop, :] += dot(weights.astype(BF16), one_g, 1, 0)
            dk_acc[:stop, :] += dot(grad_scores, one_q, 1, 0)
            back.append(dot(k_t[head * HEAD_DIM : (head + 1) * HEAD_DIM, :stop], grad_scores, 1, 0))
        dq = jnp.concatenate(back, axis=0).T * HEAD_DIM**-0.5
        cos, sin = cos_ref[start:stop, :], sin_ref[start:stop, :]
        dq_ref[start:stop, :] = (dq * cos - swap_halves(dq) * sin).astype(BF16)
    dk = dk_acc[...]
    dk_ref[...] = (dk * cos_ref[...] - swap_halves(dk) * sin_ref[...]).astype(BF16)
    dv_ref[...] = dv_acc[...].astype(BF16)


def attend_back(do, q, k, v, o, lse, cos, sin):
    rows, width = q.shape
    seqs, pairs = rows // SEQ_LEN, width // LANES
    block = pl.BlockSpec((SEQ_LEN, LANES), lambda s, h: (s, h))
    table = pl.BlockSpec((SEQ_LEN, LANES), lambda s, h: (0, 0))
    return launch(
        attend_back_kernel,
        [do, q, k, v, o, lse, cos, sin],
        [block] * 5 + [pl.BlockSpec((1, 1, 8, SEQ_LEN), lambda s, h: (s, h, 0, 0)), table, table],
        "attend_back",
        grid=(seqs, pairs),
        out_specs=[block] * 3,
        out_shape=[of((rows, width))] * 3,
        scratch_shapes=[pltpu.VMEM((SEQ_LEN, LANES), F32)] * 2,
    )


def ffn_kernel(nf_ref, cot_ref, wgu_ref, wd_ref, hidden_ref, ggu_ref):
    tile = wd_ref.shape[0]
    chunk = 256
    for lo in range(0, nf_ref.shape[0], chunk):
        rows = slice(lo, lo + chunk)
        both = dot(nf_ref[rows, :], wgu_ref[...], 1, 0)
        grad_hidden = dot(cot_ref[rows, :], wd_ref[...], 1, 1)
        gate, up = both[:, :tile], both[:, tile:]
        sig = jax.nn.sigmoid(gate)
        act = gate * sig
        hidden_ref[rows, :] = (act * up).astype(BF16)
        ggu_ref[rows, :tile] = (grad_hidden * up * (sig * (1.0 + gate * (1.0 - sig)))).astype(BF16)
        ggu_ref[rows, tile:] = (grad_hidden * act).astype(BF16)


def ffn(nf, cot, w_gu, w_down):
    rows, units = nf.shape[0], w_down.shape[0]
    tile = min(UNIT_TILE, units)
    whole = pl.BlockSpec((rows, D), lambda j: (0, 0), pipeline_mode=ONCE)
    return launch(
        ffn_kernel,
        [nf, cot, w_gu, w_down],
        [
            whole,
            whole,
            pl.BlockSpec((D, 2 * tile), lambda j: (0, j)),
            pl.BlockSpec((tile, D), lambda j: (j, 0)),
        ],
        "ffn",
        grid=(units // tile,),
        out_specs=[pl.BlockSpec((rows, tile), lambda j: (0, j)), pl.BlockSpec((rows, 2 * tile), lambda j: (0, j))],
        out_shape=[of((rows, units)), of((rows, 2 * units))],
    )


def product(lhs, rhs, where=None, turned=False, name="product"):
    count = len(lhs)
    rows = lhs[0].shape[0]
    columns = rhs[0].shape[0 if turned else 1]
    wide = sum(a.shape[1] for a in lhs)
    tile = min(columns, 512 if wide > 1024 else 1024)
    parts = 1 if where is None else 2
    size = rows // parts

    def kernel(*refs):
        refs = refs[parts - 1 :]
        lhs_refs, rhs_refs, out_refs = refs[: parts * count], refs[parts * count : -parts], refs[-parts:]
        for i, out_ref in enumerate(out_refs):
            total = None
            for a, b in zip(lhs_refs[i * count : (i + 1) * count], rhs_refs):
                extra = dot(a[...], b[...], 1, 1 if turned else 0)
                total = extra if total is None else total + extra
            out_ref[...] = total.astype(BF16)

    if parts == 1:
        lhs_specs = [pl.BlockSpec((rows, a.shape[1]), lambda n, *w: (0, 0), pipeline_mode=ONCE) for a in lhs]
    else:
        lhs_specs = [
            pl.BlockSpec((size, a.shape[1]), (lambda s: lambda n, w: (w[s], 0))(s), pipeline_mode=ONCE)
            for s in (OTHER, CORE)
            for a in lhs
        ]
    if turned:
        rhs_specs = [pl.BlockSpec((tile, b.shape[1]), lambda n, *w: (n, 0)) for b in rhs]
    else:
        rhs_specs = [pl.BlockSpec((b.shape[0], tile), lambda n, *w: (0, n)) for b in rhs]
    result = launch(
        kernel,
        [*list(lhs) * parts, *rhs],
        lhs_specs + rhs_specs,
        name,
        [] if where is None else [where],
        grid=(columns // tile,),
        out_specs=[pl.BlockSpec((size, tile), lambda n, *w: (0, n))] * parts,
        out_shape=[of((size, columns))] * parts,
    )
    return result[0] if parts == 1 else result


def quarter_product(sets, kinds, near, far, where, scalars, name):
    rows = near[0].shape[0]
    part = D // 8
    width = near[0].shape[1]
    tile = min(width, 512)
    tiles = width // tile
    pieces = len(near)
    first, stride = scalars
    fixed_specs = [
        pl.BlockSpec((rows, part), (lambda k, h: lambda t, w: (0, 4 * h + w[first + stride * k]))(k, h), pipeline_mode=ONCE)
        for _ in sets
        for _ in range(2)
        for k in range(2)
        for h in range(2)
    ]
    piece_specs = [
        pl.BlockSpec((rows, tile), (lambda i: lambda t, w: (0, jnp.clip(t - i * tiles, 0, tiles - 1)))(i))
        for i in range(pieces)
    ]
    count = len(fixed_specs)

    def kernel(where_ref, *refs):
        fixed, near_refs, far_refs = refs[:count], refs[count : count + pieces], refs[count + pieces : -2]
        out_ref, flat = refs[-2:]
        step = pl.program_id(0)

        @pl.when(step == 0)
        def _():
            for n, ref in enumerate(fixed):
                kind, chip, at = n // 8, n // 4 % 2, n % 4
                flat[kind, at * part : (at + 1) * part, chip * rows : (chip + 1) * rows] = ref[...].T

        for i, kind in enumerate(kinds):

            @pl.when((step >= i * tiles) & (step < (i + 1) * tiles))
            def _():
                total = dot(flat[kind, :, :rows], near_refs[i][...], 1, 0)
                total += dot(flat[kind, :, rows:], far_refs[i][...], 1, 0)
                out_ref[0] = total[: 2 * part].astype(BF16)
                out_ref[1] = total[2 * part :].astype(BF16)

    return launch(
        kernel,
        [*[a for pair in sets for a in pair for _ in range(4)], *near, *far],
        fixed_specs + piece_specs * 2,
        name,
        [where],
        grid=(tiles * pieces,),
        out_specs=pl.BlockSpec((2, 2 * part, tile), lambda t, w: (0, 0, t)),
        out_shape=of((2, 2 * part, width * pieces)),
        scratch_shapes=[pltpu.VMEM((len(sets), 4 * part, 2 * rows), BF16)],
    )


def row_call(kernel, rows, where, ins, outs, sums, name):
    tile = min(256, rows)
    steps = rows // tile
    specs, arrays = [], []
    for item in ins:
        array, scalar = item if isinstance(item, tuple) else (item, None)
        if scalar is not None:
            specs.append(pl.BlockSpec((tile, D), (lambda s: lambda i, w: (w[s] * steps + i, 0))(scalar)))
        elif array.shape[0] == 1:
            specs.append(pl.BlockSpec((1, D), lambda i, w: (0, 0)))
        else:
            specs.append(pl.BlockSpec((tile, D), lambda i, w: (i, 0)))
        arrays.append(array)
    out_specs = [pl.BlockSpec((tile, width), lambda i, w: (i, 0)) for _, width in outs]
    out_shape = [of((rows, width), dtype) for dtype, width in outs]
    return launch(
        kernel,
        arrays,
        specs,
        name,
        [where],
        grid=(steps,),
        out_specs=out_specs + [pl.BlockSpec((8, D), lambda i, w: (0, 0))] * sums,
        out_shape=out_shape + [of((8, D), F32)] * sums,
    )


def add_refs(*refs):
    total = refs[0][...].astype(F32)
    for ref in refs[1:]:
        total += ref[...].astype(F32)
    return total


def split_features(where_ref, total, mine_ref, other_ref):
    first = where_ref[CORE] == 0
    low, high = total[:, : D // 2], total[:, D // 2 :]
    mine_ref[...] = jnp.where(first, low, high).astype(mine_ref.dtype)
    other_ref[...] = jnp.where(first, high, low).astype(other_ref.dtype)


def norm_kernel(where_ref, one_ref, two_ref, far_ref, x_ref, gain_ref, residual_ref, normed_ref):
    residual = add_refs(x_ref, one_ref, two_ref, far_ref)
    scale = lax.rsqrt(jnp.sum(residual * residual, axis=1, keepdims=True) / D + EPS)
    residual_ref[...] = residual
    normed_ref[...] = (residual * scale * gain_ref[...]).astype(BF16)


def norm_back(stream, gain, upstream, sum_ref):
    scale = lax.rsqrt(jnp.sum(stream * stream, axis=1, keepdims=True) / D + EPS)
    weighted = upstream * gain
    inner = jnp.sum(weighted * stream, axis=1, keepdims=True)
    part = jnp.sum((upstream * stream * scale).reshape(-1, 8, D), axis=0)

    @pl.when(pl.program_id(0) == 0)
    def _():
        sum_ref[...] = jnp.zeros_like(sum_ref)

    sum_ref[...] += part
    return scale * weighted - stream * (scale * scale * scale) * (inner / D)


def ffn_back_kernel(where_ref, one_ref, two_ref, far_ref, residual_ref, cot_ref, gain_ref, grad_ref, low_ref, sum_ref):
    back = norm_back(residual_ref[...], gain_ref[...], add_refs(one_ref, two_ref, far_ref), sum_ref)
    grad = cot_ref[...].astype(F32) + back
    grad_ref[...] = grad
    low_ref[...] = grad.astype(BF16)


def input_back_kernel(where_ref, one_ref, two_ref, far_ref, x_ref, grad_ref, gain_ref, mine_ref, other_ref, sum_ref):
    back = norm_back(x_ref[...].astype(F32), gain_ref[...], add_refs(one_ref, two_ref, far_ref), sum_ref)
    split_features(where_ref, grad_ref[...] + back, mine_ref, other_ref)


def mixed_kernel(where_ref, *refs):
    split_features(where_ref, add_refs(*refs[:-2]), *refs[-2:])


def finish(pieces, spans, turned, where, name):
    shape = pieces[0].shape
    part = shape[1]
    sizes = [2 * sum(hi - lo for lo, hi in mine) for mine in spans]

    def kernel(where_ref, *refs):
        ins, outs = refs[:4], refs[4:]
        for k in range(4):

            @pl.when(pl.program_id(0) == k)
            def _():
                for out_ref, mine, flip in zip(outs, spans, turned):
                    at = 0
                    for core in range(2):
                        for lo, hi in mine:
                            block = ins[k][core, :, lo:hi]
                            if flip:
                                out_ref[at : at + hi - lo, :] = block.T.astype(F32)
                            else:
                                out_ref[:, at : at + hi - lo] = block.astype(F32)
                            at += hi - lo

    return launch(
        kernel,
        pieces,
        [pl.BlockSpec(shape, lambda k, w: (0, 0, 0), pipeline_mode=ONCE)] * 4,
        name,
        [where],
        grid=(4,),
        out_specs=[
            pl.BlockSpec((n, part), lambda k, w: (0, w[QUARTER + k]))
            if flip
            else pl.BlockSpec((part, n), lambda k, w: (w[QUARTER + k], 0))
            for n, flip in zip(sizes, turned)
        ],
        out_shape=[of((n, 4 * part) if flip else (4 * part, n), F32) for n, flip in zip(sizes, turned)],
    )


def swap_axis(values, axis, distance):
    size = lax.axis_size(axis)
    return lax.ppermute(values, axis, [(i, i ^ distance) for i in range(size)])


def other_core(values):
    return swap_axis(values, "row", 1)


def other_chip(values):
    return swap_axis(values, "col", 1)


def far_plane(values):
    return swap_axis(values, "col", 2)


def hop(values, step):
    pairs = []
    for spot in range(4):
        for core in range(2):
            distance = 1 if (step == 1) == (core == 0) else 2
            pairs.append((spot * 2 + core, (spot ^ distance) * 2 + core))
    return lax.ppermute(values, ("dp", "row"), pairs)


def hop_one(values):
    return hop(values, 1)


def hop_two(values):
    return hop(values, 2)


def add32(*values):
    total = values[0].astype(F32)
    for value in values[1:]:
        total += value.astype(F32)
    return total


class Plan:
    def __init__(self, direct, blocks):
        self.blocks = blocks
        self.core = lax.axis_index("row")
        if direct:
            spot = lax.axis_index("dp")
            quarters = [spot ^ jnp.where(self.core == 0, k, (0, 2, 1, 3)[k]) for k in range(4)]
        else:
            quarters = [jnp.int32(k) for k in range(4)]
        self.where = jnp.stack([self.core, 1 - self.core] + quarters).astype(jnp.int32)
        self.line = Line()

    def run(self, call, *values):
        return self.line.run(call, *values)

    def mix(self, call, *values):
        return self.line.mix(call, *values)

    def send(self, move, value):
        return self.line.send(move, value)

    def ship(self, move, value):
        return self.line.ship(move, value)

    def post(self, move, value):
        return self.line.post(move, value)

    def pause(self):
        self.run(short_kernel, self.line.stamp)

    def swap(self, value):
        return self.line.swap(value)

    def place(self, sources, outs, phases, name, kept=0, fixed=0):
        return self.run(lambda first, *rest: place([first, *rest], outs, phases, self.where, name, kept, fixed), *sources)

    def by_core(self, low, high):
        return jnp.where(self.core == 0, low, high), jnp.where(self.core == 0, high, low)


class Group:
    def __init__(self, name, plan, sets, kinds, near, far, spans, turned):
        self.name, self.plan, self.sets, self.kinds = name, plan, sets, kinds
        self.near, self.far, self.spans, self.turned = near, far, spans, turned
        self.block = sum(a.shape[1] for a in near) // plan.blocks

    def produce(self, scalars):
        plan, count = self.plan, len(self.near)
        return plan.run(
            lambda first, *rest: quarter_product(
                self.sets, self.kinds, (first,) + rest[: count - 1], rest[count - 1 :], plan.where, scalars, self.name
            ),
            *self.near, *self.far,
        )

    def make(self):
        self.sent = self.produce((QUARTER + 1, 2))

    def leave(self):
        self.came = self.plan.post(hop_one, self.sent)

    def stay(self):
        self.kept = self.produce((QUARTER, 2))

    def second(self):
        def add(kept, came):
            return add32(kept[1], came[1]).astype(BF16)

        self.back = self.plan.post(hop_two, self.plan.mix(add, self.kept, self.came))

    def cross_plane(self):
        n = self.block

        def add(kept, came, back):
            return add32(kept[0, :, n:], came[0, :, n:], back[:, n:]).astype(BF16)

        self.arrived = self.plan.post(far_plane, self.plan.mix(add, self.kept, self.came, self.back))

    def total(self):
        n = self.block

        def add(arrived, kept, came, back):
            return add32(kept[0, :, :n], came[0, :, :n], back[:, :n], arrived).astype(BF16)

        whole = self.plan.swap(self.plan.mix(add, self.arrived, self.kept, self.came, self.back))
        self.both = whole.reshape(2, -1, n)

    def spread(self):
        self.one = self.plan.ship(hop_one, self.both)

    def spread_last(self):
        self.two = self.plan.send(hop_two, self.both)
        self.three = self.plan.send(hop_two, self.one)

    def finish(self):
        return self.plan.run(
            lambda first, *rest: finish((first,) + rest, self.spans, self.turned, self.plan.where, "finish"),
            self.both, self.one, self.two, self.three,
        )

    def whole(self, groups):
        plan = self.plan
        pieces = []
        for k in range(2):
            made = self.produce((QUARTER + 2 * k, 1))
            for one in made:
                total = jnp.stack(jnp.split(one.astype(F32), plan.blocks, axis=1))
                total = lax.psum_scatter(total, "col", scatter_dimension=0, axis_index_groups=groups)
                total = lax.psum(total, "dp").astype(BF16)
                pieces.append(plan.swap(total).reshape(2, -1, total.shape[1]))
        return finish(pieces, self.spans, self.turned, plan.where, "finish")


class Sizes:
    def __init__(self, tokens, w_query, w_gate):
        self.rows = tokens.shape[0]
        self.half = self.rows // 2
        self.width = w_query.shape[1] // 2
        self.units = w_gate.shape[1] // 2
        self.tile = min(UNIT_TILE, self.units)
        self.split = D // 2


def interleaved(s):
    return [(p, lo) for lo in range(0, s.units, s.tile) for p in range(2)]


def gu_spans(s):
    return [[(lo + p * s.tile, lo + (p + 1) * s.tile) for lo in range(0, 2 * s.units, 2 * s.tile)] for p in range(2)]


def columns(lo, size):
    return lambda w: (slice(None), pl.ds(lo, size))


def join_features(plan, s, mine, theirs):
    return plan.place(
        [mine, theirs], [of((s.rows, D))],
        [[(0, full, 0, cols_at(CORE, s.split)), (1, full, 0, cols_at(OTHER, s.split))]], "join",
    )[0]


def join_rows(plan, s, mine, theirs):
    return plan.place(
        [mine, theirs], [of((s.rows, D))], [[(0, full, 0, rows_at(CORE, s.half)), (1, full, 0, rows_at(OTHER, s.half))]], "join"
    )[0]


def pack_in(plan, s, weights, parts, name):
    total = sum(size for _, _, size, _ in parts)
    moves, at = [], 0
    for i, lo, size, step in parts:
        moves.append((i, cols_at(OTHER, step, lo, size), 0, columns(at, size)))
        at += size
    return plan.place(weights, [of((s.split, total))], [moves], name, fixed=len(weights))[0]


def own_in(plan, s, weights, got, parts):
    total = got.shape[1]
    moves, at = [], 0
    for i, lo, size, step in parts:
        moves.append((i, cols_at(CORE, step, lo, size), 0, block_at(CORE, s.split, at, size)))
        at += size
    moves.append((len(weights), full, 0, rows_at(OTHER, s.split)))
    return plan.place([*weights, got], [of((D, total))], [moves], "own", fixed=len(weights))[0]


def own_out(plan, s, weight, got):
    rows = got.shape[0]
    return plan.place(
        [weight, got], [of((rows, D))], [[(0, rows_at(CORE, rows), 0, cols_at(CORE, s.split)), (1, full, 0, cols_at(OTHER, s.split))]],
        "own", fixed=1,
    )[0]


def both_gains(plan, mine, other):
    joined = plan.mix(lambda a, b: jnp.concatenate(plan.by_core(a, b), axis=1), mine, other)
    return joined[:1], joined[1:]


def norm_first(plan, s, near, far, x_near, gains):
    return plan.run(
        lambda *a: row_call(
            norm_kernel, s.half, plan.where, [*a[:3], (a[3], CORE), a[4]], [(F32, D), (BF16, D)], 0, "norm"
        ),
        *near, far, x_near, gains,
    )


def norm_ffn_back(plan, s, near, far, residual, cot_near, gains):
    return plan.run(
        lambda *a: row_call(
            ffn_back_kernel, s.half, plan.where, [*a[:4], (a[4], CORE), a[5]], [(F32, D), (BF16, D)], 1, "ffn_back"
        ),
        *near, far, residual, cot_near, gains,
    )


def norm_input_back(plan, s, near, far, x_near, grad_residual, gains):
    return plan.run(
        lambda *a: row_call(
            input_back_kernel, s.half, plan.where, [*a[:3], (a[3], CORE), *a[4:]],
            [(F32, D // 2), (F32, D // 2)], 1, "input_back",
        ),
        *near, far, x_near, grad_residual, gains,
    )


def add_mixed(plan, s, near, *others):
    return plan.run(
        lambda *a: row_call(mixed_kernel, s.half, plan.where, list(a), [(BF16, D // 2), (BF16, D // 2)], 0, "mixed"),
        *near, *others,
    )


def core_sum(plan, lhs, weights, turned, name):
    count = len(lhs)
    other, mine = plan.run(lambda *a: product(a[:count], a[count:], plan.where, turned, name), *lhs, *weights)
    return mine, plan.ship(other_core, other)


def add_pair(plan, pair):
    return plan.mix(lambda a, b: add32(a, b).astype(BF16), pair[1], pair[0])


def side_by_side(plan, s, mine, got):
    width = mine.shape[1]
    return plan.place(
        [mine, got], [of((s.rows, width), mine.dtype)],
        [[(0, full, 0, rows_at(CORE, s.half)), (1, full, 0, rows_at(OTHER, s.half))]], "sides",
    )[0]


def grad_attended(plan, gr, weight):
    return plan.run(lambda a: product([a], [weight], turned=True, name="grad_att"), gr)


def square(tokens, gain_attn, gain_ffn, w_query, w_key, w_value, w_out, w_gate, w_up, w_down, cotangent):
    plan = Plan(True, 2)
    s = Sizes(tokens, w_query, w_gate)
    run, mix, send, ship, post, where = plan.run, plan.mix, plan.send, plan.ship, plan.post, plan.where
    cos, sin = rope_tables()
    cos_rows, sin_rows = jnp.tile(cos, (s.rows // SEQ_LEN, 1)), jnp.tile(sin, (s.rows // SEQ_LEN, 1))
    qkv_parts = [(p, 0, s.width, s.width) for p in range(3)]
    gu_parts = [(p, lo, s.tile, s.units) for p, lo in interleaved(s)]
    eighth = D // 4 // 8

    far_tokens = other_chip(tokens)
    near_tokens = other_core(tokens)
    gains_mine = jnp.stack((gain_attn, gain_ffn))
    gains_other = other_core(gains_mine)
    plan.line.stamp = gains_mine[:, :LANES]
    got_qkv = ship(other_core, pack_in(plan, s, [w_query, w_key, w_value], qkv_parts, "pack"))
    pack_out = plan.place([w_out], [of((s.width, s.split))], [[(0, rows_at(OTHER, s.width), 0, full)]], "pack", fixed=1)[0]
    got_out = ship(other_core, pack_out)
    own_qkv = own_in(plan, s, [w_query, w_key, w_value], got_qkv, qkv_parts)
    own_o = own_out(plan, s, w_out, got_out)
    quarter, out_rows = D // 4, s.width // 4
    slots = quarter // out_rows
    out_cols = D // slots
    qkvo = plan.place(
        [own_qkv, own_o], [of((quarter, 3 * s.width + out_cols))],
        [
            [(0, rows_at(QUARTER, quarter), 0, columns(0, 3 * s.width))]
            + [
                (
                    1, (lambda j: lambda w: (pl.ds(pl.multiple_of(w[QUARTER] * out_rows, out_rows), out_rows), pl.ds(j * out_cols, out_cols)))(j),
                    0, (lambda j: lambda w: (pl.ds(j * out_rows, out_rows), pl.ds(3 * s.width, out_cols)))(j),
                )
                for j in range(slots)
            ]
        ],
        "quarter",
    )[0]
    qkvo_zero = ship(far_plane, qkvo)
    gains_attn, gains_ffn = both_gains(plan, gains_mine, gains_other)
    got_gu = ship(other_core, pack_in(plan, s, [w_gate, w_up], gu_parts, "pack"))
    pack_down = plan.place([w_down], [of((s.units, s.split))], [[(0, rows_at(OTHER, s.units), 0, full)]], "pack", fixed=1)[0]
    got_down = ship(other_core, pack_down)
    x_near = join_features(plan, s, tokens, near_tokens)
    own_gu = own_in(plan, s, [w_gate, w_up], got_gu, gu_parts)
    own_d = own_out(plan, s, w_down, got_down)
    down_rows = s.units // 4
    mixed_rows = quarter // 2 + down_rows // 2
    gud = [
        plan.place(
            [own_gu, own_d], [of((mixed_rows, D))],
            [[
                (0, (lambda i: rows_span(QUARTER, quarter, i * (quarter // 2), quarter // 2))(i), 0, rows_fixed(0, quarter // 2)),
                (1, (lambda i: rows_span(QUARTER, down_rows, i * (down_rows // 2), down_rows // 2))(i), 0, rows_fixed(quarter // 2, down_rows // 2)),
            ]],
            "quarter",
        )[0]
        for i in range(2)
    ]
    gud_zero = [None, None]

    def project(x, weight, first):
        return run(lambda a: project_qkv(a, gains_attn, cos_rows, sin_rows, weight, first), x)

    normed_near, *near_own = project(x_near, own_qkv, True)
    far_half = send(other_core, far_tokens)
    o_near_own = run(attend, *near_own)
    qkvo_one, qkvo_two = send(hop_one, qkvo_zero), send(hop_two, qkvo_zero)
    gud_zero[0] = send(far_plane, gud[0])
    far_cot = send(other_chip, cotangent)
    x_far = join_features(plan, s, far_tokens, far_half)
    normed_far, *far_own = project(x_far, own_qkv, True)
    qkvo_three = send(hop_two, qkvo_one)
    o_far_own = run(attend, *far_own)
    pieces = [qkvo_zero, qkvo_one, qkvo_two, qkvo_three]
    for_qkv, for_o = plan.place(
        pieces, [of((D, 3 * s.width)), of((s.width, D))],
        [
            [(k, columns(0, 3 * s.width), 0, rows_at(QUARTER + k, quarter)) for k in range(4)]
            + [
                (
                    k, (lambda j: lambda w: (pl.ds(j * out_rows, out_rows), pl.ds(3 * s.width, out_cols)))(j),
                    1, (lambda k, j: lambda w: (pl.ds(pl.multiple_of(w[QUARTER + k] * out_rows, out_rows), out_rows), pl.ds(j * out_cols, out_cols)))(k, j),
                )
                for k in range(4)
                for j in range(slots)
            ]
        ],
        "other",
    )
    w_qkv, w_o = [own_qkv, for_qkv], [own_o, for_o]

    far_for = project(normed_far, for_qkv, False)
    gud_one, gud_two, gud_three = [None, None], [None, None], [None, None]
    o_far = [o_far_own, run(attend, *far_for)]
    far = core_sum(plan, [o[0] for o in o_far], w_o, False, "out")
    near_for = project(normed_near, for_qkv, False)
    far = post(other_chip, add_pair(plan, far))
    gud_one[0], gud_two[0] = send(hop_one, gud_zero[0]), send(hop_two, gud_zero[0])
    gud_zero[1] = send(far_plane, gud[1])
    near_cot = send(other_core, cotangent)
    o_near = [o_near_own, run(attend, *near_for)]
    near = core_sum(plan, [o[0] for o in o_near], w_o, False, "out")
    gud_three[0] = send(hop_two, gud_one[0])
    cot_near = join_features(plan, s, cotangent, near_cot)
    cot_far_row = send(other_core, far_cot)
    plan.pause()
    cot_far = join_features(plan, s, far_cot, cot_far_row)
    def spread_out(i, outs):
        count = quarter // 2, down_rows // 2
        return plan.place(
            [g[i] for g in (gud_zero, gud_one, gud_two, gud_three)] + outs, [of(own_gu.shape), of(own_d.shape)],
            [
                [(k, rows_fixed(0, count[0]), 0, rows_span(QUARTER + k, quarter, i * count[0], count[0])) for k in range(4)]
                + [(k, rows_fixed(count[0], count[1]), 1, rows_span(QUARTER + k, down_rows, i * count[1], count[1])) for k in range(4)]
            ],
            "other", len(outs),
        )

    halves = spread_out(0, [])
    residual, normed_ffn = norm_first(plan, s, near, far, x_near, gains_ffn)
    nf_row = ship(other_core, normed_ffn)
    nf_chip = post(other_chip, normed_ffn)
    gud_one[1], gud_two[1] = send(hop_one, gud_zero[1]), send(hop_two, gud_zero[1])
    nf_near = join_rows(plan, s, normed_ffn, nf_row)
    fed_near = [run(ffn, nf_near, cot_near, own_gu, own_d)]
    nf_far_row = send(other_core, nf_chip)
    gud_three[1] = send(hop_two, gud_one[1])
    plan.pause()
    nf_far = join_rows(plan, s, nf_chip, nf_far_row)
    fed_far = [run(ffn, nf_far, cot_far, own_gu, own_d)]
    for_gu, for_d = spread_out(1, list(halves))
    w_gu, w_d = [own_gu, for_gu], [own_d, for_d]
    fed_far.append(run(ffn, nf_far, cot_far, for_gu, for_d))
    fed_near.append(run(ffn, nf_near, cot_near, for_gu, for_d))
    hid_near, ggu_near = [f[0] for f in fed_near], [f[1] for f in fed_near]
    hid_far, ggu_far = [f[0] for f in fed_far], [f[1] for f in fed_far]

    ups = Group("gu_grad", plan, [(nf_near, nf_far)], [0, 0], ggu_near, ggu_far, gu_spans(s), [False, False])
    down = Group("down_grad", plan, [(cot_near, cot_far)], [0, 0], hid_near, hid_far, [[(0, s.units)]], [True])
    ups.make()
    ups.leave()
    far = core_sum(plan, ggu_far, w_gu, True, "ffn_in")
    plan.pause()
    far = post(other_chip, add_pair(plan, far))
    near = core_sum(plan, ggu_near, w_gu, True, "ffn_in")
    ups.stay()
    grad_residual, grad_low, gain_ffn_part = norm_ffn_back(plan, s, near, far, residual, cot_near, gains_ffn)
    gr_row = ship(other_core, grad_low)
    gr_chip = post(other_chip, grad_low)
    gr_near = join_rows(plan, s, grad_low, gr_row)
    ups.second()

    def back_one(gr, heads, outs, b):
        return run(attend_back, grad_attended(plan, gr, w_o[b]), *heads[b], *outs[b], cos, sin)

    near_heads, far_heads = [near_own, near_for], [far_own, far_for]
    back_near = [back_one(gr_near, near_heads, o_near, b) for b in range(2)]
    gr_far_row = send(other_core, gr_chip)
    down.make()
    ups.cross_plane()
    down.leave()
    down.stay()
    gr_far = join_rows(plan, s, gr_chip, gr_far_row)
    back_far = [back_one(gr_far, far_heads, o_far, b) for b in range(2)]
    down.second()
    dqkv_far = [jnp.concatenate(b, axis=1) for b in back_far]
    far = core_sum(plan, dqkv_far, w_qkv, True, "qkv_in")
    heads = Group(
        "head_grad", plan, [(normed_near, normed_far), (gr_near, gr_far)], [0, 0, 0, 1] * 2,
        [a for b in range(2) for a in (*back_near[b], o_near[b][0])],
        [a for b in range(2) for a in (*back_far[b], o_far[b][0])],
        [[(p * s.width, (p + 1) * s.width)] for p in range(4)], [False, False, False, True],
    )
    heads.make()
    heads.leave()
    far = post(other_chip, add_pair(plan, far))
    dqkv_near = [jnp.concatenate(b, axis=1) for b in back_near]
    near = core_sum(plan, dqkv_near, w_qkv, True, "qkv_in")
    down.cross_plane()
    heads.stay()
    heads.second()
    mixed_far = core_sum(plan, hid_far, w_d, False, "down")
    ups.total()
    input_mine, input_other, gain_attn_part = norm_input_back(plan, s, near, far, x_near, grad_residual, gains_attn)
    input_got = ship(other_core, input_other)
    gains = mix(lambda a, b: jnp.stack((jnp.sum(a, axis=0), jnp.sum(b, axis=0))), gain_attn_part, gain_ffn_part)
    gains_got = ship(other_core, gains)
    heads.cross_plane()
    mixed_far = post(other_chip, add_pair(plan, mixed_far))
    ups.spread()
    input_grad = side_by_side(plan, s, input_mine, input_got)
    gains = mix(jnp.add, gains, gains_got)
    gains_got = ship(hop_one, gains)
    ups.spread_last()
    mixed_near = core_sum(plan, hid_near, w_d, False, "down")
    gains = mix(jnp.add, gains, gains_got)
    down.total()
    down.spread()
    gains_got = ship(hop_two, gains)
    plan.pause()
    mixed_near = [add_pair(plan, mixed_near)]
    heads.total()
    heads.spread()
    down.spread_last()
    gains = mix(jnp.add, gains, gains_got)
    gains_got = ship(other_chip, gains)
    gate_grad, up_grad = ups.finish()
    gains = mix(jnp.add, gains, gains_got)
    gains_got = ship(far_plane, gains)
    mixed_mine, mixed_other = add_mixed(plan, s, mixed_near, mixed_far, residual)
    mixed_got = ship(other_core, mixed_other)
    heads.spread_last()
    (down_grad,) = down.finish()
    mixed = side_by_side(plan, s, mixed_mine, mixed_got)
    gains = mix(jnp.add, gains, gains_got)
    gains = jnp.where(plan.core == 0, gains[:, : s.split], gains[:, s.split :])
    q_grad, k_grad, v_grad, out_grad = heads.finish()
    return mixed, input_grad, gains[0], gains[1], q_grad, k_grad, v_grad, out_grad, gate_grad, up_grad, down_grad


def pair_order(near, far):
    member = lax.axis_index("col") % 2
    return jnp.concatenate((jnp.where(member == 0, near, far), jnp.where(member == 0, far, near)), axis=0)


def from_pair(joined):
    member = lax.axis_index("col") % 2
    first, second = jnp.split(joined, 2, axis=0)
    return jnp.where(member == 0, first, second), jnp.where(member == 0, second, first)


def general(tokens, gain_attn, gain_ffn, w_query, w_key, w_value, w_out, w_gate, w_up, w_down, cotangent):
    blocks = lax.axis_size("col") // 2
    groups = [[i for i in range(2 * blocks) if i % 2 == m] for m in range(2)]
    plan = Plan(False, blocks)
    s = Sizes(tokens, w_query, w_gate)
    run, where = plan.run, plan.where
    cos, sin = rope_tables()
    shared = s.rows % SEQ_LEN != 0
    qkv_parts = [(p, 0, s.width, s.width) for p in range(3)]
    gu_parts = [(p, lo, s.tile, s.units) for p, lo in interleaved(s)]

    def gathered(own):
        every = lax.all_gather(own, "col", axis=0, axis_index_groups=groups)
        return [every[b] for b in range(blocks)]

    def pack_rows(weight, rows):
        return plan.place([weight], [of((rows, s.split))], [[(0, rows_at(OTHER, rows), 0, full)]], "pack", fixed=1)[0]

    got = other_core(pack_in(plan, s, [w_query, w_key, w_value], qkv_parts, "pack"))
    w_qkv = gathered(own_in(plan, s, [w_query, w_key, w_value], got, qkv_parts))
    got = other_core(pack_in(plan, s, [w_gate, w_up], gu_parts, "pack"))
    w_gu = gathered(own_in(plan, s, [w_gate, w_up], got, gu_parts))
    w_o = gathered(own_out(plan, s, w_out, other_core(pack_rows(w_out, s.width))))
    w_d = gathered(own_out(plan, s, w_down, other_core(pack_rows(w_down, s.units))))
    gains_mine = jnp.stack((gain_attn, gain_ffn))
    gains_attn, gains_ffn = both_gains(plan, gains_mine, other_core(gains_mine))

    def both_chips(values):
        far = other_chip(values)
        return join_features(plan, s, values, other_core(values)), join_features(plan, s, far, other_core(far))

    x_near, x_far = both_chips(tokens)
    cot_near, cot_far = both_chips(cotangent)

    def tables(offset):
        if shared:
            return [lax.dynamic_slice_in_dim(t, offset, s.rows) for t in (cos, sin)]
        return [jnp.tile(t, (s.rows // SEQ_LEN, 1)) for t in (cos, sin)]

    first = (lax.axis_index("col") % 2) * s.rows
    chips = []
    for x, offset in ((x_near, first), (x_far, s.rows - first)):
        turn = tables(offset)
        normed, *heads = run(lambda a: project_qkv(a, gains_attn, *turn, w_qkv[0], True), x)
        every = [heads]
        for w in w_qkv[1:]:
            every.append(run(lambda a: project_qkv(a, gains_attn, *turn, w, False), normed))
        chips.append((normed, every))
    (normed_near, heads_near), (normed_far, heads_far) = chips

    def together(near, far):
        return pair_order(near, far) if shared else jnp.concatenate((near, far), axis=0)

    def apart(joined):
        return from_pair(joined) if shared else jnp.split(joined, 2, axis=0)

    joined_heads = [[together(a, b) for a, b in zip(n, f)] for n, f in zip(heads_near, heads_far)]
    outs = [run(attend, *h) for h in joined_heads]
    att = [apart(o[0]) for o in outs]
    att_near, att_far = [a[0] for a in att], [a[1] for a in att]

    def four_core_sum(near, far, weights, turned, name):
        far = other_chip(add_pair(plan, core_sum(plan, far, weights, turned, name)))
        return core_sum(plan, near, weights, turned, name), far

    def gather_tokens(values):
        far = other_chip(values)
        return join_rows(plan, s, values, other_core(values)), join_rows(plan, s, far, other_core(far))

    residual, normed_ffn = norm_first(plan, s, *four_core_sum(att_near, att_far, w_o, False, "out"), x_near, gains_ffn)
    nf_near, nf_far = gather_tokens(normed_ffn)
    fed_near = [run(ffn, nf_near, cot_near, w_gu[b], w_d[b]) for b in range(blocks)]
    fed_far = [run(ffn, nf_far, cot_far, w_gu[b], w_d[b]) for b in range(blocks)]
    hid_near, ggu_near = [f[0] for f in fed_near], [f[1] for f in fed_near]
    hid_far, ggu_far = [f[0] for f in fed_far], [f[1] for f in fed_far]
    kinds = [0] * blocks
    ups = Group("gu_grad", plan, [(nf_near, nf_far)], kinds, ggu_near, ggu_far, gu_spans(s), [False, False])
    down = Group("down_grad", plan, [(cot_near, cot_far)], kinds, hid_near, hid_far, [[(0, s.units)]], [True])
    grad_residual, grad_low, gain_ffn_part = norm_ffn_back(
        plan, s, *four_core_sum(ggu_near, ggu_far, w_gu, True, "ffn_in"), residual, cot_near, gains_ffn
    )
    gr_near, gr_far = gather_tokens(grad_low)
    gr = together(gr_near, gr_far)
    backs = []
    for b in range(blocks):
        grads = run(attend_back, grad_attended(plan, gr, w_o[b]), *joined_heads[b], *outs[b], cos, sin)
        backs.append([apart(g) for g in grads])
    back_near = [[g[0] for g in b] for b in backs]
    back_far = [[g[1] for g in b] for b in backs]
    heads = Group(
        "head_grad", plan, [(normed_near, normed_far), (gr_near, gr_far)], [0, 0, 0, 1] * blocks,
        [a for b in range(blocks) for a in (*back_near[b], att_near[b])],
        [a for b in range(blocks) for a in (*back_far[b], att_far[b])],
        [[(p * s.width, (p + 1) * s.width)] for p in range(4)], [False, False, False, True],
    )
    dqkv_near = [jnp.concatenate(b, axis=1) for b in back_near]
    dqkv_far = [jnp.concatenate(b, axis=1) for b in back_far]
    input_mine, input_other, gain_attn_part = norm_input_back(
        plan, s, *four_core_sum(dqkv_near, dqkv_far, w_qkv, True, "qkv_in"), x_near, grad_residual, gains_attn
    )
    mixed_mine, mixed_other = add_mixed(plan, s, *four_core_sum(hid_near, hid_far, w_d, False, "down"), residual)
    gains = lax.psum(jnp.stack((jnp.sum(gain_attn_part, axis=0), jnp.sum(gain_ffn_part, axis=0))), ("dp", "col", "row"))
    gains = jnp.where(plan.core == 0, gains[:, : s.split], gains[:, s.split :])
    mixed = side_by_side(plan, s, mixed_mine, other_core(mixed_other))
    input_grad = side_by_side(plan, s, input_mine, other_core(input_other))
    q_grad, k_grad, v_grad, out_grad = heads.whole(groups)
    gate_grad, up_grad = ups.whole(groups)
    (down_grad,) = down.whole(groups)
    return mixed, input_grad, gains[0], gains[1], q_grad, k_grad, v_grad, out_grad, gate_grad, up_grad, down_grad


def solution(mesh):
    stream = P(("dp", "col"), "row")
    gain = P("row")
    inward, outward = P("row", "col"), P("col", "row")
    weights = (inward, inward, inward, outward, inward, inward, outward)
    fits = mesh.shape["dp"] == 4 and mesh.shape["col"] == 4
    return jax.shard_map(
        lambda *args: square(*args) if fits and args[0].shape[0] % SEQ_LEN == 0 else general(*args),
        mesh=mesh,
        in_specs=(stream, gain, gain, *weights, stream),
        out_specs=(stream, stream, gain, gain, *weights),
        check_vma=False,
    )
```

```python
import jax
import jax.numpy as jnp
from jax import lax
from jax.experimental import pallas as pl
from jax.experimental.pallas import tpu as pltpu
from jax.sharding import PartitionSpec as P

D = 2048
HEAD_DIM = 64
SEQ_LEN = 1024
LANES = 128
EPS = 1e-05
ROPE_BASE = 130000.0
VMEM = 48 * 1024 * 1024
UNIT_TILE = 256
QB = 256
COST = 10**12
F32 = jnp.float32
BF16 = jnp.bfloat16


def dot(a, b, ca, cb):
    return lax.dot_general(a, b, (((ca,), (cb,)), ((), ())), preferred_element_type=F32)


def of(shape, dtype=BF16):
    return jax.ShapeDtypeStruct(tuple(shape), dtype)


class Line:
    waiting = []
    mark = None

    def __init__(self):
        self.last = []

    def run(self, call, *values):
        Line.waiting = list(self.last)
        result = call(*values)
        self.last = [Line.mark]
        return result

    def tied(self, value):
        if not self.last:
            return value
        value, *self.last = lax.optimization_barrier((value, *self.last))
        return value

    def mix(self, call, first, *values):
        return self.tied(call(self.tied(first), *values))

    def send(self, move, value):
        return move(self.tied(value))

    def ship(self, move, value):
        return move(value)

    def post(self, move, value):
        sent = move(value)
        mark = other_core(self.tied(self.stamp))
        self.run(short_kernel, self.stamp)
        self.last = self.last + [mark]
        return sent

    def swap(self, value):
        return self.tied(lax.all_to_all(self.tied(value), "row", split_axis=0, concat_axis=0, tiled=True))


ONCE = pl.Buffered(1)


def launch(kernel, arrays, in_specs, name, prefetch=(), **rest):
    held, Line.waiting = Line.waiting, []
    skip, count = len(held), len(prefetch) + len(arrays)
    out_shape, out_specs = rest.pop("out_shape"), rest.pop("out_specs")
    single = not isinstance(out_shape, (list, tuple))
    out_shape, out_specs = ([out_shape], [out_specs]) if single else (list(out_shape), list(out_specs))
    outs = count + skip + len(out_shape)

    def body(*refs):
        kernel(*refs[:count], *refs[count + skip : outs], *refs[outs + 1 :])

    in_specs = list(in_specs) + [pl.BlockSpec(memory_space=pl.ANY)] * skip
    out_specs = out_specs + [pl.BlockSpec(memory_space=pl.ANY)]
    if prefetch:
        layout = dict(
            grid_spec=pltpu.PrefetchScalarGridSpec(
                num_scalar_prefetch=len(prefetch), in_specs=in_specs, out_specs=out_specs, **rest
            )
        )
    else:
        layout = dict(in_specs=in_specs, out_specs=out_specs, **rest)
    *results, Line.mark = pl.pallas_call(
        body,
        out_shape=out_shape + [of((8, LANES), F32)],
        compiler_params=pltpu.CompilerParams(vmem_limit_bytes=VMEM),
        cost_estimate=pl.CostEstimate(flops=COST, bytes_accessed=1, transcendentals=0),
        name=name,
        **layout,
    )(*prefetch, *arrays, *held)
    return results[0] if single else results


def short_kernel(values):
    def kernel(in_ref, out_ref):
        out_ref[0, 0] = 0.0

    return launch(
        kernel, [values], [pl.BlockSpec(memory_space=pl.ANY)], "short",
        out_specs=pl.BlockSpec(memory_space=pltpu.SMEM), out_shape=of((1, 1), F32),
    )


def extent(shape, index):
    sizes = []
    for size, at in zip(shape, index):
        if not isinstance(at, int):
            sizes.append(size if isinstance(at, slice) else at.size)
    return tuple(sizes)


def place(sources, outs, phases, where, name, kept=0, fixed=0):
    moves = [m for phase in phases for m in phase]
    shapes = [extent((sources[src] if src >= 0 else outs[-1 - src]).shape, src_at([0] * 8)) for src, src_at, _, _ in moves]
    count = len(sources)

    def kernel(where_ref, *refs):
        ins, out_refs, held = refs[:count], refs[count : count + len(outs)], refs[count + len(outs) : -2]
        in_sems, out_sems = refs[-2:]
        base = 0
        for phase in phases:
            loads, stores = [], []
            for n, (src, src_at, dst, dst_at) in enumerate(phase, base):
                src_ref = out_refs[-1 - src] if src < 0 else ins[src]
                loads.append(pltpu.make_async_copy(src_ref.at[src_at(where_ref)], held[n], in_sems.at[n]))
                stores.append(pltpu.make_async_copy(held[n], out_refs[dst].at[dst_at(where_ref)], out_sems.at[n]))
            for load in loads:
                load.start()
            for load, store in zip(loads, stores):
                load.wait()
                store.start()
            for store in stores:
                store.wait()
            base += len(phase)

    sources = [pltpu.with_memory_space_constraint(a, pltpu.HBM) for a in sources[:fixed]] + list(sources[fixed:])
    return launch(
        kernel,
        [where, *sources],
        [pl.BlockSpec(memory_space=pltpu.SMEM)]
        + [pl.BlockSpec(memory_space=pltpu.HBM)] * fixed
        + [pl.BlockSpec(memory_space=pl.ANY)] * (count - fixed),
        name,
        out_specs=[pl.BlockSpec(memory_space=pl.ANY)] * len(outs),
        out_shape=list(outs),
        scratch_shapes=[pltpu.VMEM(s, outs[m[2]].dtype) for s, m in zip(shapes, moves)] + [pltpu.SemaphoreType.DMA((len(moves),))] * 2,
        input_output_aliases={1 + count - kept + i: i for i in range(kept)},
    )


CORE, OTHER, QUARTER = 0, 1, 2


def full(_):
    return (slice(None), slice(None))


def rows_at(scalar, size, base=0):
    return lambda w: (pl.ds(pl.multiple_of(base + w[scalar] * size, size), size), slice(None))


def cols_at(scalar, size, lo=0, width=None):
    width = width or size
    return lambda w: (slice(None), pl.ds(pl.multiple_of(w[scalar] * size + lo, width), width))


def rows_span(scalar, size, lo, count):
    return lambda w: (pl.ds(pl.multiple_of(w[scalar] * size + lo, count), count), slice(None))


def rows_fixed(lo, count):
    return lambda w: (pl.ds(lo, count), slice(None))


def block_at(row_scalar, height, lo, width):
    return lambda w: (pl.ds(pl.multiple_of(w[row_scalar] * height, height), height), pl.ds(lo, width))


def rope_tables():
    half = HEAD_DIM // 2
    frequency = jnp.exp(-jnp.log(ROPE_BASE) * jnp.arange(half, dtype=F32) * (2.0 / HEAD_DIM))
    frequency = jnp.tile(frequency, 4)
    sign = jnp.where(jnp.arange(LANES) % HEAD_DIM < half, -1.0, 1.0)
    angles = jnp.arange(SEQ_LEN, dtype=F32)[:, None] * frequency[None, :]
    return jnp.cos(angles), jnp.sin(angles) * sign[None, :]


def swap_halves(values):
    half = HEAD_DIM // 2
    lane = lax.broadcasted_iota(jnp.int32, values.shape, 1)
    return jnp.where(lane % HEAD_DIM < half, pltpu.roll(values, LANES - half, 1), pltpu.roll(values, half, 1))


def qkv_kernel(first, x_ref, gain_ref, cos_ref, sin_ref, w_ref, *refs):
    q_ref, k_ref, v_ref = refs[-3:]
    if first:
        x = x_ref[...].astype(F32)
        scale = lax.rsqrt(jnp.sum(x * x, axis=1, keepdims=True) / D + EPS)
        refs[0][...] = (x * scale * gain_ref[...]).astype(BF16)
        normed = refs[0][...]
    else:
        normed = x_ref[...]
    cos, sin = cos_ref[...], sin_ref[...]
    width = q_ref.shape[1]
    projected = dot(normed, w_ref[...], 1, 0)
    for part, (out_ref, mult) in enumerate(((q_ref, HEAD_DIM**-0.5), (k_ref, 1.0))):
        for lo in range(0, width, LANES):
            piece = projected[:, part * width + lo : part * width + lo + LANES]
            out_ref[:, lo : lo + LANES] = ((piece * cos + swap_halves(piece) * sin).astype(BF16) * mult).astype(BF16)
    v_ref[...] = projected[:, 2 * width :].astype(BF16)


def project_qkv(x, gain, cos, sin, weight, first):
    rows, width = x.shape[0], weight.shape[1] // 3
    tile = min(512, rows)
    row_block = lambda n: pl.BlockSpec((tile, n), lambda i: (i, 0))
    whole = lambda a: pl.BlockSpec(a.shape, lambda i: (0, 0), pipeline_mode=ONCE)
    outs = [D] * first + [width] * 3
    return launch(
        lambda *refs: qkv_kernel(first, *refs),
        [x, gain, cos, sin, weight],
        [row_block(D), whole(gain), row_block(LANES), row_block(LANES), whole(weight)],
        "qkv",
        grid=(rows // tile,),
        out_specs=[row_block(n) for n in outs],
        out_shape=[of((rows, n)) for n in outs],
    )


def head_of(values, head):
    lane = lax.broadcasted_iota(jnp.int32, values.shape, 1)
    return jnp.where((lane >= HEAD_DIM) == (head == 1), values, jnp.zeros_like(values))


def causal_scores(keys, queries, start):
    scores = dot(keys, queries, 1, 1)
    last = scores[start:]
    key_at = lax.broadcasted_iota(jnp.int32, last.shape, 0)
    query_at = lax.broadcasted_iota(jnp.int32, last.shape, 1)
    last = jnp.where(key_at <= query_at, last, -1e30)
    return last if start == 0 else jnp.concatenate((scores[:start], last), axis=0)


def attend_kernel(q_ref, k_ref, v_ref, o_ref, lse_ref):
    values = [head_of(v_ref[...], head) for head in range(2)]
    for start in range(0, SEQ_LEN, QB):
        stop = start + QB
        queries = q_ref[start:stop, :]
        outs, scales = [], []
        for head in range(2):
            scores = causal_scores(k_ref[:stop, :], head_of(queries, head), start)
            top = jnp.max(scores, axis=0, keepdims=True)
            weights = jnp.exp(scores - top)
            total = jnp.sum(weights, axis=0, keepdims=True)
            lse_ref[0, 0, head : head + 1, start:stop] = top + jnp.log(total)
            outs.append(dot(weights.astype(BF16), values[head][:stop], 0, 0))
            scales.append(jnp.broadcast_to(1.0 / total, (HEAD_DIM, QB)))
        o_ref[start:stop, :] = ((outs[0] + outs[1]) * jnp.concatenate(scales, axis=0).T).astype(BF16)


def attend(q, k, v):
    rows, width = q.shape
    seqs, pairs = rows // SEQ_LEN, width // LANES
    block = pl.BlockSpec((SEQ_LEN, LANES), lambda s, h: (s, h))
    return launch(
        attend_kernel,
        [q, k, v],
        [block] * 3,
        "attend",
        grid=(seqs, pairs),
        out_specs=[block, pl.BlockSpec((1, 1, 8, SEQ_LEN), lambda s, h: (s, h, 0, 0))],
        out_shape=[of((rows, width)), of((seqs, pairs, 8, SEQ_LEN), F32)],
    )


def attend_back_kernel(do_ref, q_ref, k_ref, v_ref, o_ref, lse_ref, cos_ref, sin_ref, dq_ref, dk_ref, dv_ref, dk_acc, dv_acc):
    k_t = k_ref[...].T
    dk_acc[...] = jnp.zeros_like(dk_acc)
    dv_acc[...] = jnp.zeros_like(dv_acc)
    for start in range(0, SEQ_LEN, QB):
        stop = start + QB
        queries, grads = q_ref[start:stop, :], do_ref[start:stop, :]
        inner = (grads.astype(F32) * o_ref[start:stop, :].astype(F32)).T
        back = []
        for head in range(2):
            one_q, one_g = head_of(queries, head), head_of(grads, head)
            scores = causal_scores(k_ref[:stop, :], one_q, start)
            weights = jnp.exp(scores - lse_ref[0, 0, head : head + 1, start:stop])
            grad_weights = dot(v_ref[:stop, :], one_g, 1, 1)
            delta = jnp.sum(inner[head * HEAD_DIM : (head + 1) * HEAD_DIM], axis=0, keepdims=True)
            grad_scores = (weights * (grad_weights - delta)).astype(BF16)
            dv_acc[:stop, :] += dot(weights.astype(BF16), one_g, 1, 0)
            dk_acc[:stop, :] += dot(grad_scores, one_q, 1, 0)
            back.append(dot(k_t[head * HEAD_DIM : (head + 1) * HEAD_DIM, :stop], grad_scores, 1, 0))
        dq = jnp.concatenate(back, axis=0).T * HEAD_DIM**-0.5
        cos, sin = cos_ref[start:stop, :], sin_ref[start:stop, :]
        dq_ref[start:stop, :] = (dq * cos - swap_halves(dq) * sin).astype(BF16)
    dk = dk_acc[...]
    dk_ref[...] = (dk * cos_ref[...] - swap_halves(dk) * sin_ref[...]).astype(BF16)
    dv_ref[...] = dv_acc[...].astype(BF16)


def attend_back(do, q, k, v, o, lse, cos, sin):
    rows, width = q.shape
    seqs, pairs = rows // SEQ_LEN, width // LANES
    block = pl.BlockSpec((SEQ_LEN, LANES), lambda s, h: (s, h))
    table = pl.BlockSpec((SEQ_LEN, LANES), lambda s, h: (0, 0))
    return launch(
        attend_back_kernel,
        [do, q, k, v, o, lse, cos, sin],
        [block] * 5 + [pl.BlockSpec((1, 1, 8, SEQ_LEN), lambda s, h: (s, h, 0, 0)), table, table],
        "attend_back",
        grid=(seqs, pairs),
        out_specs=[block] * 3,
        out_shape=[of((rows, width))] * 3,
        scratch_shapes=[pltpu.VMEM((SEQ_LEN, LANES), F32)] * 2,
    )


def ffn_kernel(nf_ref, cot_ref, wgu_ref, wd_ref, hidden_ref, ggu_ref):
    tile = wd_ref.shape[0]
    chunk = 256
    for lo in range(0, nf_ref.shape[0], chunk):
        rows = slice(lo, lo + chunk)
        both = dot(nf_ref[rows, :], wgu_ref[...], 1, 0)
        grad_hidden = dot(cot_ref[rows, :], wd_ref[...], 1, 1)
        gate, up = both[:, :tile], both[:, tile:]
        sig = jax.nn.sigmoid(gate)
        act = gate * sig
        hidden_ref[rows, :] = (act * up).astype(BF16)
        ggu_ref[rows, :tile] = (grad_hidden * up * (sig * (1.0 + gate * (1.0 - sig)))).astype(BF16)
        ggu_ref[rows, tile:] = (grad_hidden * act).astype(BF16)


def ffn(nf, cot, w_gu, w_down):
    rows, units = nf.shape[0], w_down.shape[0]
    tile = min(UNIT_TILE, units)
    whole = pl.BlockSpec((rows, D), lambda j: (0, 0), pipeline_mode=ONCE)
    return launch(
        ffn_kernel,
        [nf, cot, w_gu, w_down],
        [
            whole,
            whole,
            pl.BlockSpec((D, 2 * tile), lambda j: (0, j)),
            pl.BlockSpec((tile, D), lambda j: (j, 0)),
        ],
        "ffn",
        grid=(units // tile,),
        out_specs=[pl.BlockSpec((rows, tile), lambda j: (0, j)), pl.BlockSpec((rows, 2 * tile), lambda j: (0, j))],
        out_shape=[of((rows, units)), of((rows, 2 * units))],
    )


def product(lhs, rhs, where=None, turned=False, name="product"):
    count = len(lhs)
    rows = lhs[0].shape[0]
    columns = rhs[0].shape[0 if turned else 1]
    wide = sum(a.shape[1] for a in lhs)
    tile = min(columns, 512 if wide > 1024 else 1024)
    parts = 1 if where is None else 2
    size = rows // parts

    def kernel(*refs):
        refs = refs[parts - 1 :]
        lhs_refs, rhs_refs, out_refs = refs[: parts * count], refs[parts * count : -parts], refs[-parts:]
        for i, out_ref in enumerate(out_refs):
            total = None
            for a, b in zip(lhs_refs[i * count : (i + 1) * count], rhs_refs):
                extra = dot(a[...], b[...], 1, 1 if turned else 0)
                total = extra if total is None else total + extra
            out_ref[...] = total.astype(BF16)

    if parts == 1:
        lhs_specs = [pl.BlockSpec((rows, a.shape[1]), lambda n, *w: (0, 0), pipeline_mode=ONCE) for a in lhs]
    else:
        lhs_specs = [
            pl.BlockSpec((size, a.shape[1]), (lambda s: lambda n, w: (w[s], 0))(s), pipeline_mode=ONCE)
            for s in (OTHER, CORE)
            for a in lhs
        ]
    if turned:
        rhs_specs = [pl.BlockSpec((tile, b.shape[1]), lambda n, *w: (n, 0)) for b in rhs]
    else:
        rhs_specs = [pl.BlockSpec((b.shape[0], tile), lambda n, *w: (0, n)) for b in rhs]
    result = launch(
        kernel,
        [*list(lhs) * parts, *rhs],
        lhs_specs + rhs_specs,
        name,
        [] if where is None else [where],
        grid=(columns // tile,),
        out_specs=[pl.BlockSpec((size, tile), lambda n, *w: (0, n))] * parts,
        out_shape=[of((size, columns))] * parts,
    )
    return result[0] if parts == 1 else result


def quarter_product(sets, kinds, near, far, where, scalars, name):
    rows = near[0].shape[0]
    part = D // 8
    width = near[0].shape[1]
    tile = min(width, 512)
    tiles = width // tile
    pieces = len(near)
    first, stride = scalars
    fixed_specs = [
        pl.BlockSpec((rows, part), (lambda k, h: lambda t, w: (0, 4 * h + w[first + stride * k]))(k, h), pipeline_mode=ONCE)
        for _ in sets
        for _ in range(2)
        for k in range(2)
        for h in range(2)
    ]
    piece_specs = [
        pl.BlockSpec((rows, tile), (lambda i: lambda t, w: (0, jnp.clip(t - i * tiles, 0, tiles - 1)))(i))
        for i in range(pieces)
    ]
    count = len(fixed_specs)

    def kernel(where_ref, *refs):
        fixed, near_refs, far_refs = refs[:count], refs[count : count + pieces], refs[count + pieces : -2]
        out_ref, flat = refs[-2:]
        step = pl.program_id(0)

        @pl.when(step == 0)
        def _():
            for n, ref in enumerate(fixed):
                kind, chip, at = n // 8, n // 4 % 2, n % 4
                flat[kind, at * part : (at + 1) * part, chip * rows : (chip + 1) * rows] = ref[...].T

        for i, kind in enumerate(kinds):

            @pl.when((step >= i * tiles) & (step < (i + 1) * tiles))
            def _():
                total = dot(flat[kind, :, :rows], near_refs[i][...], 1, 0)
                total += dot(flat[kind, :, rows:], far_refs[i][...], 1, 0)
                out_ref[0] = total[: 2 * part].astype(BF16)
                out_ref[1] = total[2 * part :].astype(BF16)

    return launch(
        kernel,
        [*[a for pair in sets for a in pair for _ in range(4)], *near, *far],
        fixed_specs + piece_specs * 2,
        name,
        [where],
        grid=(tiles * pieces,),
        out_specs=pl.BlockSpec((2, 2 * part, tile), lambda t, w: (0, 0, t)),
        out_shape=of((2, 2 * part, width * pieces)),
        scratch_shapes=[pltpu.VMEM((len(sets), 4 * part, 2 * rows), BF16)],
    )


def row_call(kernel, rows, where, ins, outs, sums, name):
    tile = min(256, rows)
    steps = rows // tile
    specs, arrays = [], []
    for item in ins:
        array, scalar = item if isinstance(item, tuple) else (item, None)
        if scalar is not None:
            specs.append(pl.BlockSpec((tile, D), (lambda s: lambda i, w: (w[s] * steps + i, 0))(scalar)))
        elif array.shape[0] == 1:
            specs.append(pl.BlockSpec((1, D), lambda i, w: (0, 0)))
        else:
            specs.append(pl.BlockSpec((tile, D), lambda i, w: (i, 0)))
        arrays.append(array)
    out_specs = [pl.BlockSpec((tile, width), lambda i, w: (i, 0)) for _, width in outs]
    out_shape = [of((rows, width), dtype) for dtype, width in outs]
    return launch(
        kernel,
        arrays,
        specs,
        name,
        [where],
        grid=(steps,),
        out_specs=out_specs + [pl.BlockSpec((8, D), lambda i, w: (0, 0))] * sums,
        out_shape=out_shape + [of((8, D), F32)] * sums,
    )


def add_refs(*refs):
    total = refs[0][...].astype(F32)
    for ref in refs[1:]:
        total += ref[...].astype(F32)
    return total


def split_features(where_ref, total, mine_ref, other_ref):
    first = where_ref[CORE] == 0
    low, high = total[:, : D // 2], total[:, D // 2 :]
    mine_ref[...] = jnp.where(first, low, high).astype(mine_ref.dtype)
    other_ref[...] = jnp.where(first, high, low).astype(other_ref.dtype)


def norm_kernel(where_ref, one_ref, two_ref, far_ref, x_ref, gain_ref, residual_ref, normed_ref):
    residual = add_refs(x_ref, one_ref, two_ref, far_ref)
    scale = lax.rsqrt(jnp.sum(residual * residual, axis=1, keepdims=True) / D + EPS)
    residual_ref[...] = residual
    normed_ref[...] = (residual * scale * gain_ref[...]).astype(BF16)


def norm_back(stream, gain, upstream, sum_ref):
    scale = lax.rsqrt(jnp.sum(stream * stream, axis=1, keepdims=True) / D + EPS)
    weighted = upstream * gain
    inner = jnp.sum(weighted * stream, axis=1, keepdims=True)
    part = jnp.sum((upstream * stream * scale).reshape(-1, 8, D), axis=0)

    @pl.when(pl.program_id(0) == 0)
    def _():
        sum_ref[...] = jnp.zeros_like(sum_ref)

    sum_ref[...] += part
    return scale * weighted - stream * (scale * scale * scale) * (inner / D)


def ffn_back_kernel(where_ref, one_ref, two_ref, far_ref, residual_ref, cot_ref, gain_ref, grad_ref, low_ref, sum_ref):
    back = norm_back(residual_ref[...], gain_ref[...], add_refs(one_ref, two_ref, far_ref), sum_ref)
    grad = cot_ref[...].astype(F32) + back
    grad_ref[...] = grad
    low_ref[...] = grad.astype(BF16)


def input_back_kernel(where_ref, one_ref, two_ref, far_ref, x_ref, grad_ref, gain_ref, mine_ref, other_ref, sum_ref):
    back = norm_back(x_ref[...].astype(F32), gain_ref[...], add_refs(one_ref, two_ref, far_ref), sum_ref)
    split_features(where_ref, grad_ref[...] + back, mine_ref, other_ref)


def mixed_kernel(where_ref, *refs):
    split_features(where_ref, add_refs(*refs[:-2]), *refs[-2:])


def finish(pieces, spans, turned, where, name):
    shape = pieces[0].shape
    part = shape[1]
    sizes = [2 * sum(hi - lo for lo, hi in mine) for mine in spans]

    def kernel(where_ref, *refs):
        ins, outs = refs[:4], refs[4:]
        for k in range(4):

            @pl.when(pl.program_id(0) == k)
            def _():
                for out_ref, mine, flip in zip(outs, spans, turned):
                    at = 0
                    for core in range(2):
                        for lo, hi in mine:
                            block = ins[k][core, :, lo:hi]
                            if flip:
                                out_ref[at : at + hi - lo, :] = block.T.astype(F32)
                            else:
                                out_ref[:, at : at + hi - lo] = block.astype(F32)
                            at += hi - lo

    return launch(
        kernel,
        pieces,
        [pl.BlockSpec(shape, lambda k, w: (0, 0, 0), pipeline_mode=ONCE)] * 4,
        name,
        [where],
        grid=(4,),
        out_specs=[
            pl.BlockSpec((n, part), lambda k, w: (0, w[QUARTER + k]))
            if flip
            else pl.BlockSpec((part, n), lambda k, w: (w[QUARTER + k], 0))
            for n, flip in zip(sizes, turned)
        ],
        out_shape=[of((n, 4 * part) if flip else (4 * part, n), F32) for n, flip in zip(sizes, turned)],
    )


def swap_axis(values, axis, distance):
    size = lax.axis_size(axis)
    return lax.ppermute(values, axis, [(i, i ^ distance) for i in range(size)])


def other_core(values):
    return swap_axis(values, "row", 1)


def other_chip(values):
    return swap_axis(values, "col", 1)


def far_plane(values):
    return swap_axis(values, "col", 2)


def hop(values, step):
    pairs = []
    for spot in range(4):
        for core in range(2):
            distance = 1 if (step == 1) == (core == 0) else 2
            pairs.append((spot * 2 + core, (spot ^ distance) * 2 + core))
    return lax.ppermute(values, ("dp", "row"), pairs)


def hop_one(values):
    return hop(values, 1)


def hop_two(values):
    return hop(values, 2)


def add32(*values):
    total = values[0].astype(F32)
    for value in values[1:]:
        total += value.astype(F32)
    return total


class Plan:
    def __init__(self, direct, blocks):
        self.blocks = blocks
        self.core = lax.axis_index("row")
        if direct:
            spot = lax.axis_index("dp")
            quarters = [spot ^ jnp.where(self.core == 0, k, (0, 2, 1, 3)[k]) for k in range(4)]
        else:
            quarters = [jnp.int32(k) for k in range(4)]
        self.where = jnp.stack([self.core, 1 - self.core] + quarters).astype(jnp.int32)
        self.line = Line()

    def run(self, call, *values):
        return self.line.run(call, *values)

    def mix(self, call, *values):
        return self.line.mix(call, *values)

    def send(self, move, value):
        return self.line.send(move, value)

    def ship(self, move, value):
        return self.line.ship(move, value)

    def post(self, move, value):
        return self.line.post(move, value)

    def pause(self):
        self.run(short_kernel, self.line.stamp)

    def swap(self, value):
        return self.line.swap(value)

    def place(self, sources, outs, phases, name, kept=0, fixed=0):
        return self.run(lambda first, *rest: place([first, *rest], outs, phases, self.where, name, kept, fixed), *sources)

    def by_core(self, low, high):
        return jnp.where(self.core == 0, low, high), jnp.where(self.core == 0, high, low)


class Group:
    def __init__(self, name, plan, sets, kinds, near, far, spans, turned):
        self.name, self.plan, self.sets, self.kinds = name, plan, sets, kinds
        self.near, self.far, self.spans, self.turned = near, far, spans, turned
        self.block = sum(a.shape[1] for a in near) // plan.blocks

    def produce(self, scalars):
        plan, count = self.plan, len(self.near)
        return plan.run(
            lambda first, *rest: quarter_product(
                self.sets, self.kinds, (first,) + rest[: count - 1], rest[count - 1 :], plan.where, scalars, self.name
            ),
            *self.near, *self.far,
        )

    def make(self):
        self.sent = self.produce((QUARTER + 1, 2))

    def leave(self):
        self.came = self.plan.post(hop_one, self.sent)

    def stay(self):
        self.kept = self.produce((QUARTER, 2))

    def second(self):
        def add(kept, came):
            return add32(kept[1], came[1]).astype(BF16)

        self.back = self.plan.post(hop_two, self.plan.mix(add, self.kept, self.came))

    def cross_plane(self):
        n = self.block

        def add(kept, came, back):
            return add32(kept[0, :, n:], came[0, :, n:], back[:, n:]).astype(BF16)

        self.arrived = self.plan.post(far_plane, self.plan.mix(add, self.kept, self.came, self.back))

    def total(self):
        n = self.block

        def add(arrived, kept, came, back):
            return add32(kept[0, :, :n], came[0, :, :n], back[:, :n], arrived).astype(BF16)

        whole = self.plan.swap(self.plan.mix(add, self.arrived, self.kept, self.came, self.back))
        self.both = whole.reshape(2, -1, n)

    def spread(self):
        self.one = self.plan.ship(hop_one, self.both)

    def spread_last(self):
        self.two = self.plan.send(hop_two, self.both)
        self.three = self.plan.send(hop_two, self.one)

    def finish(self):
        return self.plan.run(
            lambda first, *rest: finish((first,) + rest, self.spans, self.turned, self.plan.where, "finish"),
            self.both, self.one, self.two, self.three,
        )

    def whole(self, groups):
        plan = self.plan
        pieces = []
        for k in range(2):
            made = self.produce((QUARTER + 2 * k, 1))
            for one in made:
                total = jnp.stack(jnp.split(one.astype(F32), plan.blocks, axis=1))
                total = lax.psum_scatter(total, "col", scatter_dimension=0, axis_index_groups=groups)
                total = lax.psum(total, "dp").astype(BF16)
                pieces.append(plan.swap(total).reshape(2, -1, total.shape[1]))
        return finish(pieces, self.spans, self.turned, plan.where, "finish")


class Sizes:
    def __init__(self, tokens, w_query, w_gate):
        self.rows = tokens.shape[0]
        self.half = self.rows // 2
        self.width = w_query.shape[1] // 2
        self.units = w_gate.shape[1] // 2
        self.tile = min(UNIT_TILE, self.units)
        self.split = D // 2


def interleaved(s):
    return [(p, lo) for lo in range(0, s.units, s.tile) for p in range(2)]


def gu_spans(s):
    return [[(lo + p * s.tile, lo + (p + 1) * s.tile) for lo in range(0, 2 * s.units, 2 * s.tile)] for p in range(2)]


def columns(lo, size):
    return lambda w: (slice(None), pl.ds(lo, size))


def join_features(plan, s, mine, theirs):
    return plan.place(
        [mine, theirs], [of((s.rows, D))],
        [[(0, full, 0, cols_at(CORE, s.split)), (1, full, 0, cols_at(OTHER, s.split))]], "join",
    )[0]


def join_rows(plan, s, mine, theirs):
    return plan.place(
        [mine, theirs], [of((s.rows, D))], [[(0, full, 0, rows_at(CORE, s.half)), (1, full, 0, rows_at(OTHER, s.half))]], "join"
    )[0]


def pack_in(plan, s, weights, parts, name):
    total = sum(size for _, _, size, _ in parts)
    moves, at = [], 0
    for i, lo, size, step in parts:
        moves.append((i, cols_at(OTHER, step, lo, size), 0, columns(at, size)))
        at += size
    return plan.place(weights, [of((s.split, total))], [moves], name, fixed=len(weights))[0]


def own_in(plan, s, weights, got, parts):
    total = got.shape[1]
    moves, at = [], 0
    for i, lo, size, step in parts:
        moves.append((i, cols_at(CORE, step, lo, size), 0, block_at(CORE, s.split, at, size)))
        at += size
    moves.append((len(weights), full, 0, rows_at(OTHER, s.split)))
    return plan.place([*weights, got], [of((D, total))], [moves], "own", fixed=len(weights))[0]


def own_out(plan, s, weight, got):
    rows = got.shape[0]
    return plan.place(
        [weight, got], [of((rows, D))], [[(0, rows_at(CORE, rows), 0, cols_at(CORE, s.split)), (1, full, 0, cols_at(OTHER, s.split))]],
        "own", fixed=1,
    )[0]


def both_gains(plan, mine, other):
    joined = plan.mix(lambda a, b: jnp.concatenate(plan.by_core(a, b), axis=1), mine, other)
    return joined[:1], joined[1:]


def norm_first(plan, s, near, far, x_near, gains):
    return plan.run(
        lambda *a: row_call(
            norm_kernel, s.half, plan.where, [*a[:3], (a[3], CORE), a[4]], [(F32, D), (BF16, D)], 0, "norm"
        ),
        *near, far, x_near, gains,
    )


def norm_ffn_back(plan, s, near, far, residual, cot_near, gains):
    return plan.run(
        lambda *a: row_call(
            ffn_back_kernel, s.half, plan.where, [*a[:4], (a[4], CORE), a[5]], [(F32, D), (BF16, D)], 1, "ffn_back"
        ),
        *near, far, residual, cot_near, gains,
    )


def norm_input_back(plan, s, near, far, x_near, grad_residual, gains):
    return plan.run(
        lambda *a: row_call(
            input_back_kernel, s.half, plan.where, [*a[:3], (a[3], CORE), *a[4:]],
            [(F32, D // 2), (F32, D // 2)], 1, "input_back",
        ),
        *near, far, x_near, grad_residual, gains,
    )


def add_mixed(plan, s, near, *others):
    return plan.run(
        lambda *a: row_call(mixed_kernel, s.half, plan.where, list(a), [(BF16, D // 2), (BF16, D // 2)], 0, "mixed"),
        *near, *others,
    )


def core_sum(plan, lhs, weights, turned, name):
    count = len(lhs)
    other, mine = plan.run(lambda *a: product(a[:count], a[count:], plan.where, turned, name), *lhs, *weights)
    return mine, plan.ship(other_core, other)


def add_pair(plan, pair):
    return plan.mix(lambda a, b: add32(a, b).astype(BF16), pair[1], pair[0])


def side_by_side(plan, s, mine, got):
    width = mine.shape[1]
    return plan.place(
        [mine, got], [of((s.rows, width), mine.dtype)],
        [[(0, full, 0, rows_at(CORE, s.half)), (1, full, 0, rows_at(OTHER, s.half))]], "sides",
    )[0]


def grad_attended(plan, gr, weight):
    return plan.run(lambda a: product([a], [weight], turned=True, name="grad_att"), gr)


def square(tokens, gain_attn, gain_ffn, w_query, w_key, w_value, w_out, w_gate, w_up, w_down, cotangent):
    plan = Plan(True, 2)
    s = Sizes(tokens, w_query, w_gate)
    run, mix, send, ship, post, where = plan.run, plan.mix, plan.send, plan.ship, plan.post, plan.where
    cos, sin = rope_tables()
    cos_rows, sin_rows = jnp.tile(cos, (s.rows // SEQ_LEN, 1)), jnp.tile(sin, (s.rows // SEQ_LEN, 1))
    qkv_parts = [(p, 0, s.width, s.width) for p in range(3)]
    gu_parts = [(p, lo, s.tile, s.units) for p, lo in interleaved(s)]
    eighth = D // 4 // 8

    far_tokens = other_chip(tokens)
    near_tokens = other_core(tokens)
    gains_mine = jnp.stack((gain_attn, gain_ffn))
    gains_other = other_core(gains_mine)
    plan.line.stamp = gains_mine[:, :LANES]
    got_qkv = ship(other_core, pack_in(plan, s, [w_query, w_key, w_value], qkv_parts, "pack"))
    pack_out = plan.place([w_out], [of((s.width, s.split))], [[(0, rows_at(OTHER, s.width), 0, full)]], "pack", fixed=1)[0]
    got_out = ship(other_core, pack_out)
    own_qkv = own_in(plan, s, [w_query, w_key, w_value], got_qkv, qkv_parts)
    own_o = own_out(plan, s, w_out, got_out)
    quarter, out_rows = D // 4, s.width // 4
    slots = quarter // out_rows
    out_cols = D // slots
    qkvo = plan.place(
        [own_qkv, own_o], [of((quarter, 3 * s.width + out_cols))],
        [
            [(0, rows_at(QUARTER, quarter), 0, columns(0, 3 * s.width))]
            + [
                (
                    1, (lambda j: lambda w: (pl.ds(pl.multiple_of(w[QUARTER] * out_rows, out_rows), out_rows), pl.ds(j * out_cols, out_cols)))(j),
                    0, (lambda j: lambda w: (pl.ds(j * out_rows, out_rows), pl.ds(3 * s.width, out_cols)))(j),
                )
                for j in range(slots)
            ]
        ],
        "quarter",
    )[0]
    qkvo_zero = ship(far_plane, qkvo)
    gains_attn, gains_ffn = both_gains(plan, gains_mine, gains_other)
    got_gu = ship(other_core, pack_in(plan, s, [w_gate, w_up], gu_parts, "pack"))
    pack_down = plan.place([w_down], [of((s.units, s.split))], [[(0, rows_at(OTHER, s.units), 0, full)]], "pack", fixed=1)[0]
    got_down = ship(other_core, pack_down)
    x_near = join_features(plan, s, tokens, near_tokens)
    own_gu = own_in(plan, s, [w_gate, w_up], got_gu, gu_parts)
    own_d = own_out(plan, s, w_down, got_down)
    down_rows = s.units // 4
    mixed_rows = quarter // 2 + down_rows // 2
    gud = [
        plan.place(
            [own_gu, own_d], [of((mixed_rows, D))],
            [[
                (0, (lambda i: rows_span(QUARTER, quarter, i * (quarter // 2), quarter // 2))(i), 0, rows_fixed(0, quarter // 2)),
                (1, (lambda i: rows_span(QUARTER, down_rows, i * (down_rows // 2), down_rows // 2))(i), 0, rows_fixed(quarter // 2, down_rows // 2)),
            ]],
            "quarter",
        )[0]
        for i in range(2)
    ]
    gud_zero = [None, None]

    def project(x, weight, first):
        return run(lambda a: project_qkv(a, gains_attn, cos_rows, sin_rows, weight, first), x)

    normed_near, *near_own = project(x_near, own_qkv, True)
    far_half = send(other_core, far_tokens)
    o_near_own = run(attend, *near_own)
    qkvo_one, qkvo_two = send(hop_one, qkvo_zero), send(hop_two, qkvo_zero)
    gud_zero[0] = send(far_plane, gud[0])
    far_cot = send(other_chip, cotangent)
    x_far = join_features(plan, s, far_tokens, far_half)
    normed_far, *far_own = project(x_far, own_qkv, True)
    qkvo_three = send(hop_two, qkvo_one)
    o_far_own = run(attend, *far_own)
    pieces = [qkvo_zero, qkvo_one, qkvo_two, qkvo_three]
    for_qkv, for_o = plan.place(
        pieces, [of((D, 3 * s.width)), of((s.width, D))],
        [
            [(k, columns(0, 3 * s.width), 0, rows_at(QUARTER + k, quarter)) for k in range(4)]
            + [
                (
                    k, (lambda j: lambda w: (pl.ds(j * out_rows, out_rows), pl.ds(3 * s.width, out_cols)))(j),
                    1, (lambda k, j: lambda w: (pl.ds(pl.multiple_of(w[QUARTER + k] * out_rows, out_rows), out_rows), pl.ds(j * out_cols, out_cols)))(k, j),
                )
                for k in range(4)
                for j in range(slots)
            ]
        ],
        "other",
    )
    w_qkv, w_o = [own_qkv, for_qkv], [own_o, for_o]

    far_for = project(normed_far, for_qkv, False)
    gud_one, gud_two, gud_three = [None, None], [None, None], [None, None]
    o_far = [o_far_own, run(attend, *far_for)]
    far = core_sum(plan, [o[0] for o in o_far], w_o, False, "out")
    near_for = project(normed_near, for_qkv, False)
    far = post(other_chip, add_pair(plan, far))
    gud_one[0], gud_two[0] = send(hop_one, gud_zero[0]), send(hop_two, gud_zero[0])
    gud_zero[1] = send(far_plane, gud[1])
    near_cot = send(other_core, cotangent)
    o_near = [o_near_own, run(attend, *near_for)]
    near = core_sum(plan, [o[0] for o in o_near], w_o, False, "out")
    gud_three[0] = send(hop_two, gud_one[0])
    cot_near = join_features(plan, s, cotangent, near_cot)
    cot_far_row = send(other_core, far_cot)
    plan.pause()
    cot_far = join_features(plan, s, far_cot, cot_far_row)
    def spread_out(i, outs):
        count = quarter // 2, down_rows // 2
        return plan.place(
            [g[i] for g in (gud_zero, gud_one, gud_two, gud_three)] + outs, [of(own_gu.shape), of(own_d.shape)],
            [
                [(k, rows_fixed(0, count[0]), 0, rows_span(QUARTER + k, quarter, i * count[0], count[0])) for k in range(4)]
                + [(k, rows_fixed(count[0], count[1]), 1, rows_span(QUARTER + k, down_rows, i * count[1], count[1])) for k in range(4)]
            ],
            "other", len(outs),
        )

    halves = spread_out(0, [])
    residual, normed_ffn = norm_first(plan, s, near, far, x_near, gains_ffn)
    nf_row = ship(other_core, normed_ffn)
    nf_chip = post(other_chip, normed_ffn)
    gud_one[1], gud_two[1] = send(hop_one, gud_zero[1]), send(hop_two, gud_zero[1])
    nf_near = join_rows(plan, s, normed_ffn, nf_row)
    fed_near = [run(ffn, nf_near, cot_near, own_gu, own_d)]
    nf_far_row = send(other_core, nf_chip)
    gud_three[1] = send(hop_two, gud_one[1])
    plan.pause()
    nf_far = join_rows(plan, s, nf_chip, nf_far_row)
    fed_far = [run(ffn, nf_far, cot_far, own_gu, own_d)]
    for_gu, for_d = spread_out(1, list(halves))
    w_gu, w_d = [own_gu, for_gu], [own_d, for_d]
    fed_far.append(run(ffn, nf_far, cot_far, for_gu, for_d))
    fed_near.append(run(ffn, nf_near, cot_near, for_gu, for_d))
    hid_near, ggu_near = [f[0] for f in fed_near], [f[1] for f in fed_near]
    hid_far, ggu_far = [f[0] for f in fed_far], [f[1] for f in fed_far]

    ups = Group("gu_grad", plan, [(nf_near, nf_far)], [0, 0], ggu_near, ggu_far, gu_spans(s), [False, False])
    down = Group("down_grad", plan, [(cot_near, cot_far)], [0, 0], hid_near, hid_far, [[(0, s.units)]], [True])
    ups.make()
    ups.leave()
    far = core_sum(plan, ggu_far, w_gu, True, "ffn_in")
    plan.pause()
    far = post(other_chip, add_pair(plan, far))
    near = core_sum(plan, ggu_near, w_gu, True, "ffn_in")
    ups.stay()
    grad_residual, grad_low, gain_ffn_part = norm_ffn_back(plan, s, near, far, residual, cot_near, gains_ffn)
    gr_row = ship(other_core, grad_low)
    gr_chip = post(other_chip, grad_low)
    gr_near = join_rows(plan, s, grad_low, gr_row)
    ups.second()

    def back_one(gr, heads, outs, b):
        return run(attend_back, grad_attended(plan, gr, w_o[b]), *heads[b], *outs[b], cos, sin)

    near_heads, far_heads = [near_own, near_for], [far_own, far_for]
    back_near = [back_one(gr_near, near_heads, o_near, b) for b in range(2)]
    gr_far_row = send(other_core, gr_chip)
    down.make()
    ups.cross_plane()
    down.leave()
    down.stay()
    gr_far = join_rows(plan, s, gr_chip, gr_far_row)
    back_far = [back_one(gr_far, far_heads, o_far, b) for b in range(2)]
    down.second()
    dqkv_far = [jnp.concatenate(b, axis=1) for b in back_far]
    far = core_sum(plan, dqkv_far, w_qkv, True, "qkv_in")
    heads = Group(
        "head_grad", plan, [(normed_near, normed_far), (gr_near, gr_far)], [0, 0, 0, 1] * 2,
        [a for b in range(2) for a in (*back_near[b], o_near[b][0])],
        [a for b in range(2) for a in (*back_far[b], o_far[b][0])],
        [[(p * s.width, (p + 1) * s.width)] for p in range(4)], [False, False, False, True],
    )
    heads.make()
    heads.leave()
    far = post(other_chip, add_pair(plan, far))
    dqkv_near = [jnp.concatenate(b, axis=1) for b in back_near]
    near = core_sum(plan, dqkv_near, w_qkv, True, "qkv_in")
    down.cross_plane()
    heads.stay()
    heads.second()
    mixed_far = core_sum(plan, hid_far, w_d, False, "down")
    ups.total()
    input_mine, input_other, gain_attn_part = norm_input_back(plan, s, near, far, x_near, grad_residual, gains_attn)
    input_got = ship(other_core, input_other)
    gains = mix(lambda a, b: jnp.stack((jnp.sum(a, axis=0), jnp.sum(b, axis=0))), gain_attn_part, gain_ffn_part)
    gains_got = ship(other_core, gains)
    heads.cross_plane()
    mixed_far = post(other_chip, add_pair(plan, mixed_far))
    ups.spread()
    input_grad = side_by_side(plan, s, input_mine, input_got)
    gains = mix(jnp.add, gains, gains_got)
    gains_got = ship(hop_one, gains)
    ups.spread_last()
    mixed_near = core_sum(plan, hid_near, w_d, False, "down")
    gains = mix(jnp.add, gains, gains_got)
    down.total()
    down.spread()
    gains_got = ship(hop_two, gains)
    plan.pause()
    mixed_near = [add_pair(plan, mixed_near)]
    heads.total()
    heads.one = post(hop_one, heads.both)
    down.spread_last()
    gate_grad, up_grad = ups.finish()
    gains = mix(jnp.add, gains, gains_got)
    gains_got = ship(other_chip, gains)
    mixed_mine, mixed_other = add_mixed(plan, s, mixed_near, mixed_far, residual)
    mixed_got = ship(other_core, mixed_other)
    gains = mix(jnp.add, gains, gains_got)
    gains_got = ship(far_plane, gains)
    heads.spread_last()
    (down_grad,) = down.finish()
    mixed = side_by_side(plan, s, mixed_mine, mixed_got)
    gains = mix(jnp.add, gains, gains_got)
    gains = jnp.where(plan.core == 0, gains[:, : s.split], gains[:, s.split :])
    q_grad, k_grad, v_grad, out_grad = heads.finish()
    return mixed, input_grad, gains[0], gains[1], q_grad, k_grad, v_grad, out_grad, gate_grad, up_grad, down_grad


def pair_order(near, far):
    member = lax.axis_index("col") % 2
    return jnp.concatenate((jnp.where(member == 0, near, far), jnp.where(member == 0, far, near)), axis=0)


def from_pair(joined):
    member = lax.axis_index("col") % 2
    first, second = jnp.split(joined, 2, axis=0)
    return jnp.where(member == 0, first, second), jnp.where(member == 0, second, first)


def general(tokens, gain_attn, gain_ffn, w_query, w_key, w_value, w_out, w_gate, w_up, w_down, cotangent):
    blocks = lax.axis_size("col") // 2
    groups = [[i for i in range(2 * blocks) if i % 2 == m] for m in range(2)]
    plan = Plan(False, blocks)
    s = Sizes(tokens, w_query, w_gate)
    run, where = plan.run, plan.where
    cos, sin = rope_tables()
    shared = s.rows % SEQ_LEN != 0
    qkv_parts = [(p, 0, s.width, s.width) for p in range(3)]
    gu_parts = [(p, lo, s.tile, s.units) for p, lo in interleaved(s)]

    def gathered(own):
        every = lax.all_gather(own, "col", axis=0, axis_index_groups=groups)
        return [every[b] for b in range(blocks)]

    def pack_rows(weight, rows):
        return plan.place([weight], [of((rows, s.split))], [[(0, rows_at(OTHER, rows), 0, full)]], "pack", fixed=1)[0]

    got = other_core(pack_in(plan, s, [w_query, w_key, w_value], qkv_parts, "pack"))
    w_qkv = gathered(own_in(plan, s, [w_query, w_key, w_value], got, qkv_parts))
    got = other_core(pack_in(plan, s, [w_gate, w_up], gu_parts, "pack"))
    w_gu = gathered(own_in(plan, s, [w_gate, w_up], got, gu_parts))
    w_o = gathered(own_out(plan, s, w_out, other_core(pack_rows(w_out, s.width))))
    w_d = gathered(own_out(plan, s, w_down, other_core(pack_rows(w_down, s.units))))
    gains_mine = jnp.stack((gain_attn, gain_ffn))
    gains_attn, gains_ffn = both_gains(plan, gains_mine, other_core(gains_mine))

    def both_chips(values):
        far = other_chip(values)
        return join_features(plan, s, values, other_core(values)), join_features(plan, s, far, other_core(far))

    x_near, x_far = both_chips(tokens)
    cot_near, cot_far = both_chips(cotangent)

    def tables(offset):
        if shared:
            return [lax.dynamic_slice_in_dim(t, offset, s.rows) for t in (cos, sin)]
        return [jnp.tile(t, (s.rows // SEQ_LEN, 1)) for t in (cos, sin)]

    first = (lax.axis_index("col") % 2) * s.rows
    chips = []
    for x, offset in ((x_near, first), (x_far, s.rows - first)):
        turn = tables(offset)
        normed, *heads = run(lambda a: project_qkv(a, gains_attn, *turn, w_qkv[0], True), x)
        every = [heads]
        for w in w_qkv[1:]:
            every.append(run(lambda a: project_qkv(a, gains_attn, *turn, w, False), normed))
        chips.append((normed, every))
    (normed_near, heads_near), (normed_far, heads_far) = chips

    def together(near, far):
        return pair_order(near, far) if shared else jnp.concatenate((near, far), axis=0)

    def apart(joined):
        return from_pair(joined) if shared else jnp.split(joined, 2, axis=0)

    joined_heads = [[together(a, b) for a, b in zip(n, f)] for n, f in zip(heads_near, heads_far)]
    outs = [run(attend, *h) for h in joined_heads]
    att = [apart(o[0]) for o in outs]
    att_near, att_far = [a[0] for a in att], [a[1] for a in att]

    def four_core_sum(near, far, weights, turned, name):
        far = other_chip(add_pair(plan, core_sum(plan, far, weights, turned, name)))
        return core_sum(plan, near, weights, turned, name), far

    def gather_tokens(values):
        far = other_chip(values)
        return join_rows(plan, s, values, other_core(values)), join_rows(plan, s, far, other_core(far))

    residual, normed_ffn = norm_first(plan, s, *four_core_sum(att_near, att_far, w_o, False, "out"), x_near, gains_ffn)
    nf_near, nf_far = gather_tokens(normed_ffn)
    fed_near = [run(ffn, nf_near, cot_near, w_gu[b], w_d[b]) for b in range(blocks)]
    fed_far = [run(ffn, nf_far, cot_far, w_gu[b], w_d[b]) for b in range(blocks)]
    hid_near, ggu_near = [f[0] for f in fed_near], [f[1] for f in fed_near]
    hid_far, ggu_far = [f[0] for f in fed_far], [f[1] for f in fed_far]
    kinds = [0] * blocks
    ups = Group("gu_grad", plan, [(nf_near, nf_far)], kinds, ggu_near, ggu_far, gu_spans(s), [False, False])
    down = Group("down_grad", plan, [(cot_near, cot_far)], kinds, hid_near, hid_far, [[(0, s.units)]], [True])
    grad_residual, grad_low, gain_ffn_part = norm_ffn_back(
        plan, s, *four_core_sum(ggu_near, ggu_far, w_gu, True, "ffn_in"), residual, cot_near, gains_ffn
    )
    gr_near, gr_far = gather_tokens(grad_low)
    gr = together(gr_near, gr_far)
    backs = []
    for b in range(blocks):
        grads = run(attend_back, grad_attended(plan, gr, w_o[b]), *joined_heads[b], *outs[b], cos, sin)
        backs.append([apart(g) for g in grads])
    back_near = [[g[0] for g in b] for b in backs]
    back_far = [[g[1] for g in b] for b in backs]
    heads = Group(
        "head_grad", plan, [(normed_near, normed_far), (gr_near, gr_far)], [0, 0, 0, 1] * blocks,
        [a for b in range(blocks) for a in (*back_near[b], att_near[b])],
        [a for b in range(blocks) for a in (*back_far[b], att_far[b])],
        [[(p * s.width, (p + 1) * s.width)] for p in range(4)], [False, False, False, True],
    )
    dqkv_near = [jnp.concatenate(b, axis=1) for b in back_near]
    dqkv_far = [jnp.concatenate(b, axis=1) for b in back_far]
    input_mine, input_other, gain_attn_part = norm_input_back(
        plan, s, *four_core_sum(dqkv_near, dqkv_far, w_qkv, True, "qkv_in"), x_near, grad_residual, gains_attn
    )
    mixed_mine, mixed_other = add_mixed(plan, s, *four_core_sum(hid_near, hid_far, w_d, False, "down"), residual)
    gains = lax.psum(jnp.stack((jnp.sum(gain_attn_part, axis=0), jnp.sum(gain_ffn_part, axis=0))), ("dp", "col", "row"))
    gains = jnp.where(plan.core == 0, gains[:, : s.split], gains[:, s.split :])
    mixed = side_by_side(plan, s, mixed_mine, other_core(mixed_other))
    input_grad = side_by_side(plan, s, input_mine, other_core(input_other))
    q_grad, k_grad, v_grad, out_grad = heads.whole(groups)
    gate_grad, up_grad = ups.whole(groups)
    (down_grad,) = down.whole(groups)
    return mixed, input_grad, gains[0], gains[1], q_grad, k_grad, v_grad, out_grad, gate_grad, up_grad, down_grad


def solution(mesh):
    stream = P(("dp", "col"), "row")
    gain = P("row")
    inward, outward = P("row", "col"), P("col", "row")
    weights = (inward, inward, inward, outward, inward, inward, outward)
    fits = mesh.shape["dp"] == 4 and mesh.shape["col"] == 4
    return jax.shard_map(
        lambda *args: square(*args) if fits and args[0].shape[0] % SEQ_LEN == 0 else general(*args),
        mesh=mesh,
        in_specs=(stream, gain, gain, *weights, stream),
        out_specs=(stream, stream, gain, gain, *weights),
        check_vma=False,
    )
```
